128 devices in a mesh: dp: 16 (over x_hi, z, core), tensor: 8 (over x_lo, y).
Axes of the slice: x: 4 (x_hi: 2, x_lo: 2; x = x_hi * 2 + x_lo), y: 4, z: 4, core: 2. Of those that a mesh axis runs over, the one named last changes fastest.
Arguments:
- query_states: bfloat16 [4608, 3584], P('dp', 'tensor'), may hold values from -256 to 256, as said below
- doc_states: bfloat16 [4608, 3584], P('dp', 'tensor'), may hold values from -256 to 256, as said below
- gain: float32 [3584], P('tensor'), may hold values from 0.5 to 1.5
- positives: int32 [4608], P('dp'), may hold values from 0 to 4607, each once
Outputs:
- grad_query: bfloat16 [4608, 3584], P('dp', 'tensor')
- grad_doc: bfloat16 [4608, 3584], P('dp', 'tensor')
- grad_gain: float32 [3584], P('tensor')
- loss: float32 [], replicated
The draws below stay inside these ranges and needn't reach their ends.
Inputs may be any that keep to these rules, and one draw needn't show every extreme that they name: `query_states`: finite hidden states. `doc_states`: finite hidden states.
All inputs are finite; a program needn't handle non-finite values.
Results may differ from the reference program's by a relative error of at most 0.0066.
Values may be sent and summed in bfloat16 or wider, within the bound.
A program may use at most 128 MiB of HBM per device.

```python
import math
import jax
import jax.numpy as jnp
from jax import lax

WIDTH = 3584
PAIRS = 4608


def pair_states(key):
    keys = jax.random.split(key, 5)
    position = jnp.arange(WIDTH, dtype=jnp.float32)[None, :] / WIDTH
    rising = jnp.exp(math.log(4.0) * position)
    base_d = jax.random.normal(keys[1], (PAIRS, WIDTH)) * rising
    base_q = jax.random.normal(keys[2], (PAIRS, WIDTH)) * rising
    scale_d = jnp.exp(jax.random.uniform(keys[3], (PAIRS, 1), minval=0.0, maxval=math.log(10.0)))
    scale_q = jnp.exp(jax.random.uniform(keys[4], (PAIRS, 1), minval=0.0, maxval=math.log(10.0)))
    docs = base_d * scale_d
    queries = base_q * scale_q
    return (jnp.clip(queries, -256.0, 256.0), jnp.clip(docs, -256.0, 256.0))


def draw_query_states(key, part):
    return pair_states(key)[0].astype(jnp.bfloat16)


def draw_doc_states(key, part):
    return pair_states(key)[1].astype(jnp.bfloat16)


def setup_inputs(seed: int = 0) -> dict:
    streams_of = jax.random.split(jax.random.key(seed), 5)
    return {
        "query_states": draw_query_states(jax.random.fold_in(streams_of[4], 71), 0),
        "doc_states": draw_doc_states(jax.random.fold_in(streams_of[4], 71), 0),
        "gain": jnp.clip(1.0 + 0.1 * jax.random.normal(streams_of[2], (WIDTH,), jnp.float32), 0.5, 1.5),
        "positives": jax.random.permutation(streams_of[3], PAIRS).astype(jnp.int32),
    }


eps_len = 1e-06
inv_temp = 100.0
masked = -1e+30

def forward_side(states, gain):
    hstate = states.astype(jnp.float32)
    normed = hstate * gain[None, :]
    inverse = lax.rsqrt(lax.optimization_barrier(jnp.sum(normed * normed, axis=1)) + eps_len)
    embedded = (normed * inverse[:, None]).astype(jnp.bfloat16)
    return (hstate, normed, inverse, embedded)

def backward_side(grad_emb, hstate, normed, inverse, gain):
    first = lax.optimization_barrier(jnp.sum(grad_emb * normed, axis=1))
    grad_x = inverse[:, None] * grad_emb - normed * (inverse ** 3 * first)[:, None]
    grad_h = grad_x * gain[None, :]
    gain_part = lax.optimization_barrier(jnp.sum(grad_x * hstate, axis=0))
    return (grad_h, gain_part)

def reference(query_states, doc_states, gain, positives):
    hq, nq, iq, query_emb = forward_side(query_states, gain)
    hd, nd, idd, doc_emb = forward_side(doc_states, gain)
    qf = query_emb.astype(jnp.float32)
    df = doc_emb.astype(jnp.float32)
    high = lax.Precision.HIGHEST
    pairs = qf.shape[0]
    logit_d = jnp.dot(qf, df.T, precision=high) * inv_temp
    logit_q = jnp.dot(qf, qf.T, precision=high) * inv_temp
    index = jnp.arange(pairs, dtype=jnp.int32)
    logit_q = jnp.where(index[:, None] == index[None, :], masked, logit_q)
    top = jnp.maximum(lax.optimization_barrier(jnp.max(logit_d, axis=1)), lax.optimization_barrier(jnp.max(logit_q, axis=1)))
    total = lax.optimization_barrier(jnp.sum(jnp.exp(logit_d - top[:, None]), axis=1)) + lax.optimization_barrier(jnp.sum(jnp.exp(logit_q - top[:, None]), axis=1))
    lse = top + jnp.log(total)
    hit = positives[:, None] == index[None, :]
    posit = lax.optimization_barrier(jnp.sum(jnp.where(hit, logit_d, 0.0), axis=1))
    loss = jnp.sum(lse - posit) / pairs
    weight_d = ((jnp.exp(logit_d - lse[:, None]) - hit.astype(jnp.float32)) / pairs).astype(jnp.bfloat16).astype(jnp.float32)
    weight_q = (jnp.exp(logit_q - lse[:, None]) / pairs).astype(jnp.bfloat16).astype(jnp.float32)
    grad_emb_q = (jnp.dot(weight_d, df, precision=high) + jnp.dot(weight_q, qf, precision=high)) * inv_temp + jnp.dot(weight_q.T, qf, precision=high) * inv_temp
    grad_emb_d = jnp.dot(weight_d.T, qf, precision=high) * inv_temp
    grad_hq, gain_q = backward_side(grad_emb_q, hq, nq, iq, gain)
    grad_hd, gain_d = backward_side(grad_emb_d, hd, nd, idd, gain)
    return (grad_hq.astype(jnp.bfloat16), grad_hd.astype(jnp.bfloat16), gain_q + gain_d, loss)
```

```python
import jax
import jax.numpy as jnp
from jax import lax
from jax.sharding import PartitionSpec as P

eps_len = 1e-06
inv_temp = 100.0
masked = -1e30


def contract_cols(left, right):
    return lax.dot_general(
        left, right, (((1,), (1,)), ((), ())), preferred_element_type=jnp.float32
    )


def contract_rows(left, right):
    return lax.dot_general(
        left, right, (((0,), (0,)), ((), ())), preferred_element_type=jnp.float32
    )


def shards(query_states, doc_states, gain, positives):
    rows, feats = query_states.shape
    groups = lax.axis_size("dp")
    parts = lax.axis_size("tensor")
    own = lax.axis_index("dp")
    part = lax.axis_index("tensor")
    take = rows // parts
    pairs = rows * groups
    hq = query_states.astype(jnp.float32)
    hd = doc_states.astype(jnp.float32)
    normed_q = hq * gain[None, :]
    normed_d = hd * gain[None, :]
    length_q, length_d = lax.psum(
        (jnp.sum(normed_q * normed_q, axis=1), jnp.sum(normed_d * normed_d, axis=1)), "tensor"
    )
    inverse_q = lax.rsqrt(length_q + eps_len)
    inverse_d = lax.rsqrt(length_d + eps_len)
    query_emb = (normed_q * inverse_q[:, None]).astype(jnp.bfloat16)
    doc_emb = (normed_d * inverse_d[:, None]).astype(jnp.bfloat16)
    query_full = lax.all_gather(query_emb, "tensor", axis=1, tiled=True)
    doc_full = lax.all_gather(doc_emb, "tensor", axis=1, tiled=True)
    subset = lax.dynamic_slice_in_dim(query_full, part * take, take, axis=0)
    query_rows = lax.all_gather(subset, "dp", axis=0, tiled=True)
    row_ids = (
        (lax.iota(jnp.int32, groups) * rows)[:, None]
        + part * take
        + lax.iota(jnp.int32, take)[None, :]
    ).reshape(-1)
    col_ids = own * rows + lax.iota(jnp.int32, rows)
    positive_rows = lax.all_gather(
        lax.dynamic_slice_in_dim(positives, part * take, take, axis=0), "dp", axis=0, tiled=True
    )
    logit_d = contract_cols(query_rows, doc_full) * inv_temp
    logit_q = contract_cols(query_rows, query_full) * inv_temp
    logit_q = jnp.where(row_ids[:, None] == col_ids[None, :], masked, logit_q)
    hit = positive_rows[:, None] == col_ids[None, :]
    top = jnp.maximum(jnp.max(logit_d, axis=1), jnp.max(logit_q, axis=1))
    total = jnp.sum(jnp.exp(logit_d - top[:, None]), axis=1) + jnp.sum(
        jnp.exp(logit_q - top[:, None]), axis=1
    )
    posit = jnp.sum(jnp.where(hit, logit_d, 0.0), axis=1)
    stats = lax.all_gather(jnp.stack([top, total, posit]), "dp", axis=0)
    all_top = jnp.max(stats[:, 0], axis=0)
    lse = all_top + jnp.log(jnp.sum(stats[:, 1] * jnp.exp(stats[:, 0] - all_top[None, :]), axis=0))
    loss_rows = jnp.sum(lse - jnp.sum(stats[:, 2], axis=0))
    lse_cols = lax.all_gather(
        lax.dynamic_slice_in_dim(lse, own * take, take, axis=0), "tensor", axis=0, tiled=True
    )
    weight_d = ((jnp.exp(logit_d - lse[:, None]) - hit.astype(jnp.float32)) / pairs).astype(
        jnp.bfloat16
    )
    weight_q = (jnp.exp(logit_q - lse[:, None]) / pairs).astype(jnp.bfloat16)
    weight_t = (jnp.exp(logit_q - lse_cols[None, :]) / pairs).astype(jnp.bfloat16)
    weight_s = (weight_q.astype(jnp.float32) + weight_t.astype(jnp.float32)).astype(jnp.bfloat16)
    part_q = (
        jnp.dot(weight_d, doc_full, preferred_element_type=jnp.float32)
        + jnp.dot(weight_s, query_full, preferred_element_type=jnp.float32)
    ) * inv_temp
    part_d = contract_rows(weight_d, query_rows) * inv_temp
    back_q = lax.psum_scatter(part_q, "dp", scatter_dimension=0, tiled=True)
    grad_emb_d = lax.psum_scatter(part_d, "tensor", scatter_dimension=1, tiled=True)
    grad_emb_q = lax.all_to_all(back_q, "tensor", split_axis=1, concat_axis=0, tiled=True)
    first_q, first_d = lax.psum(
        (jnp.sum(grad_emb_q * normed_q, axis=1), jnp.sum(grad_emb_d * normed_d, axis=1)), "tensor"
    )
    grad_x_q = inverse_q[:, None] * grad_emb_q - normed_q * (inverse_q**3 * first_q)[:, None]
    grad_x_d = inverse_d[:, None] * grad_emb_d - normed_d * (inverse_d**3 * first_d)[:, None]
    grad_hq = grad_x_q * gain[None, :]
    grad_hd = grad_x_d * gain[None, :]
    gain_local = jnp.sum(grad_x_q * hq, axis=0) + jnp.sum(grad_x_d * hd, axis=0)
    grad_gain = lax.psum(gain_local, "dp")
    loss_sum = lax.psum(loss_rows, "tensor")
    return (grad_hq.astype(jnp.bfloat16), grad_hd.astype(jnp.bfloat16), grad_gain, loss_sum / pairs)


def solution(mesh):
    return jax.shard_map(
        shards,
        mesh=mesh,
        in_specs=(P("dp", "tensor"), P("dp", "tensor"), P("tensor"), P("dp")),
        out_specs=(P("dp", "tensor"), P("dp", "tensor"), P("tensor"), P()),
        check_vma=False,
    )
```

```python
import functools

import jax
import jax.numpy as jnp
from jax import lax
from jax.experimental import pallas as pl
from jax.experimental.pallas import tpu as pltpu
from jax.sharding import PartitionSpec as P

eps_len = 1e-06
inv_temp = 100.0
masked = -1e30

MESH = pl.DeviceIdType.MESH
HIGH = lax.Precision.HIGHEST
f32 = jnp.float32
bf16 = jnp.bfloat16

DP = 16
TP = 8
ROWS = 288
FEATS = 448
WIDE = 2 * FEATS
FULL = TP * FEATS
PAIRS = DP * ROWS
TAKE = DP * ROWS // TP
TILE = 16
CHUNK = 96
NCH = ROWS // CHUNK
HALF = CHUNK // 2


def step(
    hq, hd, gain, pos,
    oq, od, ogain, oloss,
    xq, xd, pq, pd, gpart, emb, qi, invq, invd, logits, wts, wtt,
    e0s, e0r, cs1, cr1, e1s, e1r, e2s, e2r, e3s, e3r, cs4, cr4, e4s, e4r, epr,
    partq, sibr, sendq, recvq, pd2, pd1, pdm, halfs, r1, r2, gd, xsend, xrecv,
    asend, arecv, gqs, outq, outd,
    x_s, x_r, e0_s, e0_r, e1_s, e1_r, e2_s, e2_r, e3_s, e3_r, e4_s, e4_r, ep_s, ep_r,
    y_s, y_r, a_s, a_r, loc, b_s, b_r, u_s, u_r, g_s, g_r, t_s, t_r, c_s, c_r, io,
):
    d = lax.axis_index("dp")
    t = lax.axis_index("tensor")
    hz = d // 2
    core = d % 2
    zc = hz % 4
    d4 = (hz // 4) * 2 + core
    low = t // 4
    y = t % 4
    xh = hz // 4
    sources = [pltpu.make_async_copy(hq, xq, io.at[0]), pltpu.make_async_copy(hd, xd, io.at[1])]
    for c in sources:
        c.start()
    third = t // 2
    sibling = (hz * 2 + (1 - core), t)
    partner = (d, (t + 4) % TP)
    up = (d, low * 4 + (y + 1) % 4)
    down = (d, low * 4 + (y + 3) % 4)
    zup = ((xh * 4 + (zc + 1) % 4) * 2 + core, t)
    zdown = ((xh * 4 + (zc + 3) % 4) * 2 + core, t)
    across = ((hz + 4) % 8 * 2 + core, t)

    sent = []

    def copy(src, dst, ss, rs, dev):
        return pltpu.make_async_remote_copy(
            src_ref=src, dst_ref=dst, send_sem=ss, recv_sem=rs, device_id=dev, device_id_type=MESH
        )

    def lanes(block):
        return pl.ds(pl.multiple_of(block * WIDE, 128), WIDE)

    def rows_at(tile, n):
        return pl.ds(pl.multiple_of(tile * TILE, TILE), n)

    def place(hz_s, core_s, tens):
        q = (hz_s // 4) * 2 + core_s
        e = tens // 2
        return (hz_s % 4) * 9 + 2 * q + jnp.where(q > e, 1, 0)

    def begin(q, tens):
        return 2 * tens + jnp.clip(tens - 2 * q, 0, 2)

    def sized(extra, fn):
        @pl.when(extra)
        def _():
            fn(3 * TILE)

        @pl.when(jnp.logical_not(extra))
        def _():
            fn(2 * TILE)

    barrier = pltpu.get_barrier_semaphore()

    @pl.loop(1, TP)
    def _(k):
        pl.semaphore_signal(barrier, inc=1, device_id=(d, (t + k) % TP), device_id_type=MESH)

    @pl.loop(1, 8)
    def _(k):
        pl.semaphore_signal(
            barrier, inc=1, device_id=((hz + k) % 8 * 2 + core, t), device_id_type=MESH
        )

    pl.semaphore_signal(barrier, inc=1, device_id=sibling, device_id_type=MESH)
    def to_lanes(col):
        return jnp.transpose(jnp.broadcast_to(col, (ROWS, 128)))[:8]

    def to_rows(vec):
        return jnp.transpose(jnp.broadcast_to(vec, (128, ROWS)))

    sub8 = lambda n: lax.broadcasted_iota(jnp.int32, (8, n), 0)

    for c in sources:
        c.wait()
    nq = xq[...].astype(f32) * gain[...]
    nd = xd[...].astype(f32) * gain[...]
    lq = to_lanes(jnp.sum(nq * nq, axis=1, keepdims=True))
    ld = to_lanes(jnp.sum(nd * nd, axis=1, keepdims=True))
    e0s[...] = jnp.where(sub8(ROWS) == 0, lq, ld)
    pl.semaphore_wait(barrier, TP + 7)

    def xcopy(i):
        if i == 0:
            return copy(gain, gpart, x_s.at[0], x_r.at[0], partner)
        src, dst = (xq, pq) if i <= NCH else (xd, pd)
        part = pl.ds(((i - 1) % NCH) * CHUNK, CHUNK)
        return copy(src.at[part], dst.at[part], x_s.at[i], x_r.at[i], partner)

    def begun(c):
        c.start()
        sent.append(c.wait_send)

    def exchange(src, recv, ss, rs, size, me, dev):
        @pl.loop(1, size)
        def _(k):
            copy(src, recv.at[me], ss.at[k], rs.at[me], dev((me + k) % size)).start()

        @sent.append
        def _():
            @pl.loop(1, size)
            def _(k):
                copy(src, recv.at[me], ss.at[k], rs.at[me], dev((me + k) % size)).wait_send()

    def finish(src, recv, ss, rs, size, me, dev):
        recv[me] = src[...]

        @pl.loop(1, size)
        def _(k):
            s = (me + k) % size
            copy(src, recv.at[s], ss.at[k], rs.at[s], dev(s)).wait_recv()

    by_tensor = lambda s: (d, s)
    by_hz = lambda s: (s * 2 + core, t)

    def total(recv, size):
        acc = recv[0]
        for s in range(1, size):
            acc = acc + recv[s]
        return acc

    e0 = (e0s, e0r, e0_s, e0_r, TP, t, by_tensor)
    begun(xcopy(0))
    begun(xcopy(1))
    exchange(*e0)
    for i in range(2, 1 + 2 * NCH):
        begun(xcopy(i))

    mine = begin(d4, t)
    here = place(hz, core, t)
    extra = d4 == third

    finish(*e0)
    inv = lax.rsqrt(total(e0r, TP) + eps_len)
    invq[0:ROWS] = to_rows(inv[0:1])
    invd[...] = to_rows(inv[1:2])

    def pack(a, k):
        own, part, inverse, base = (xq, pq, invq, ROWS) if a == 0 else (xd, pd, invd, 0)
        xcopy(1 + a * NCH + k).wait_recv()
        rs = pl.ds(k * CHUNK, CHUNK)
        scale = inverse[rs, 0:1]
        eo = own[rs].astype(f32) * gain[...] * scale
        ep = part[rs].astype(f32) * gpart[...] * scale
        left = jnp.where(low == 0, eo, ep)
        right = jnp.where(low == 0, ep, eo)
        emb[pl.ds(base + k * CHUNK, CHUNK), lanes(y)] = jnp.concatenate(
            [left, right], axis=1
        ).astype(bf16)

    def ycopy(a, k, kind):
        base = (ROWS if a == 0 else 0) + k * CHUNK
        i = (a * NCH + k) * 4 + kind
        if kind < 2:
            at, dev, block = pl.ds(base, CHUNK), (up, down)[kind], y
        elif kind == 2:
            at, dev, block = pl.ds(base, HALF), up, (y + 3) % 4
        else:
            at, dev, block = pl.ds(base + HALF, HALF), down, (y + 1) % 4
        ref = emb.at[at, lanes(block)]
        return copy(ref, ref, y_s.at[i], y_r.at[i], dev)

    def yrecv(a, k, kind):
        base = (ROWS if a == 0 else 0) + k * CHUNK
        i = (a * NCH + k) * 4 + kind
        at = pl.ds(base, CHUNK) if kind < 2 else pl.ds(base + (kind - 2) * HALF, HALF)
        block = ((y + 3) % 4, (y + 1) % 4, (y + 2) % 4, (y + 2) % 4)[kind]
        ref = emb.at[at, lanes(block)]
        copy(ref, ref, y_s.at[i], y_r.at[i], up).wait_recv()

    def arow(i, hz_s, core_s, n):
        block = (y + (0, 3, 1, 2)[i]) % 4
        return qi.at[rows_at(place(hz_s, core_s, t), n), lanes(block)]

    def own_rows(i, n):
        block = (y + (0, 3, 1, 2)[i]) % 4
        return emb.at[pl.ds(pl.multiple_of(ROWS + mine * TILE, TILE), n), lanes(block)]

    def acopy(i, k, n):
        to = (hz + k) % 8 * 2 + jnp.where(k == 0, 1 - core, core)
        return copy(
            own_rows(i, n), arow(i, hz, core, n), a_s.at[i * 16 + k], a_r.at[i * 16 + k], (to, t)
        )

    def alocal(i, n):
        return pltpu.make_async_copy(own_rows(i, n), arow(i, hz, core, n), loc.at[i])

    def arrived(i, k, core_s, slot, n):
        ref = arow(i, (hz + 8 - k) % 8, core_s, n)
        return copy(ref, ref, a_s.at[i * 16 + slot], a_r.at[i * 16 + slot], sibling)

    def gives(k, core_s):
        return (((hz + 8 - k) % 8) // 4) * 2 + core_s == third

    def astart(i):
        @pl.loop(0, 8)
        def _(k):
            sized(extra, lambda n: acopy(i, k, n).start())

        sized(extra, lambda n: alocal(i, n).start())

        @sent.append
        def _():
            @pl.loop(0, 8)
            def _(k):
                sized(extra, lambda n: acopy(i, k, n).wait_send())

    def aforward(i):
        @pl.loop(1, 8)
        def _(k):
            def pass_on(n):
                arrived(i, k, core, k, n).wait_recv()
                arrived(i, k, core, 8 + k, n).start()

            sized(gives(k, core), pass_on)

        @sent.append
        def _():
            @pl.loop(1, 8)
            def _(k):
                sized(gives(k, core), lambda n: arrived(i, k, core, 8 + k, n).wait_send())

    def afinish(i):
        sized(extra, lambda n: alocal(i, n).wait())
        sized(gives(0, 1 - core), lambda n: arrived(i, 0, 1 - core, 0, n).wait_recv())

        @pl.loop(1, 8)
        def _(k):
            sized(gives(k, 1 - core), lambda n: arrived(i, k, 1 - core, 8 + k, n).wait_recv())

    xcopy(0).wait_recv()
    for k in range(NCH):
        pack(0, k)
        begun(ycopy(0, k, 0))
        begun(ycopy(0, k, 1))
    astart(0)
    ep = (pos, epr, ep_s, ep_r, 8, hz, by_hz)
    exchange(*ep)
    for k in range(NCH):
        yrecv(0, k, 0)
        begun(ycopy(0, k, 2))
        yrecv(0, k, 1)
        begun(ycopy(0, k, 3))
        pack(1, k)
        begun(ycopy(1, k, 0))
        begun(ycopy(1, k, 1))
    astart(1)
    astart(2)
    aforward(0)
    for k in range(NCH):
        yrecv(0, k, 2)
        yrecv(0, k, 3)
    astart(3)
    aforward(1)
    aforward(2)
    for k in range(NCH):
        yrecv(1, k, 0)
        begun(ycopy(1, k, 2))
        yrecv(1, k, 1)
        begun(ycopy(1, k, 3))
    aforward(3)
    for i in range(4):
        afinish(i)

    lane_p = lax.broadcasted_iota(jnp.int32, (1, TAKE), 1)
    tile_p = lane_p // TILE
    w_p = tile_p % 9
    q_p = jnp.where(
        w_p < 2 * third, w_p // 2, jnp.where(w_p <= 2 * third + 2, third, (w_p - 1) // 2)
    )
    off_p = w_p - 2 * q_p - jnp.where(q_p > third, 1, 0)
    dev_p = (q_p // 2) * 8 + (tile_p // 9) * 2 + q_p % 2
    row_p = dev_p * ROWS + (begin(q_p, t) + off_p) * TILE + lane_p % TILE
    finish(*ep)
    epc = copy(epr.at[pl.ds(0, 8)], epr.at[pl.ds(8, 8)], c_s.at[0], c_r.at[0], sibling)
    begun(epc)

    MC = 144

    def logit_rows(r, query):
        at = pl.ds(pl.multiple_of(r, TILE), MC)
        s = lax.dot_general(
            emb[at], qi[...], (((1,), (1,)), ((), ())), preferred_element_type=f32
        ) * inv_temp
        if query:
            j = d * ROWS + r - ROWS + lax.broadcasted_iota(jnp.int32, (MC, TAKE), 0)
            s = jnp.where(j == row_p, masked, s)
        logits[at] = s

    @pl.loop(0, ROWS // MC)
    def _(m):
        logit_rows(ROWS + m * MC, True)

    epc.wait_recv()
    local_p = (begin(q_p, t) + off_p) * TILE + lane_p % TILE
    lane_of = lax.broadcasted_iota(jnp.int32, (128, TAKE), 0)
    spread = jnp.where(lane_of == local_p % 128, 1.0, 0.0).astype(bf16)
    found = jnp.dot(
        epr[...].reshape(DP * 8, 128).astype(bf16), spread, preferred_element_type=f32
    )
    slot_p = jnp.where(dev_p % 2 == core, dev_p // 2, 8 + dev_p // 2) * 8 + local_p // 128
    high = jnp.sum(jnp.where(lane_of == slot_p, found, 0.0), axis=0, keepdims=True)
    rest = jnp.sum(jnp.where(lane_of == slot_p + 3, found, 0.0), axis=0, keepdims=True)
    pos_p = (high * 128.0 + rest).astype(jnp.int32)

    for k in range(NCH):
        yrecv(1, k, 2)
        yrecv(1, k, 3)

    @pl.loop(0, ROWS // MC)
    def _(m):
        logit_rows(m * MC, False)

    own_j = d * ROWS + lax.broadcasted_iota(jnp.int32, (ROWS, TAKE), 0)
    top = jnp.max(logits[...], axis=0, keepdims=True)
    tot = jnp.sum(jnp.exp(logits[...] - top), axis=0, keepdims=True)
    posit = jnp.sum(
        jnp.where(own_j == pos_p, logits[0:ROWS], 0.0), axis=0, keepdims=True
    )
    sub_t = sub8(TAKE)
    cs1[...] = jnp.where(sub_t == 0, top, jnp.where(sub_t == 1, tot, posit))
    c1 = copy(cs1, cr1, c_s.at[1], c_r.at[1], sibling)
    begun(c1)
    c1.wait_recv()
    top_o = cr1[0:1]
    top_c = jnp.maximum(top, top_o)
    tot = tot * jnp.exp(top - top_c) + cr1[1:2] * jnp.exp(top_o - top_c)
    e1s[...] = jnp.where(sub_t == 0, top_c, jnp.where(sub_t == 1, tot, posit + cr1[2:3]))
    e1 = (e1s, e1r, e1_s, e1_r, 8, hz, by_hz)
    exchange(*e1)
    finish(*e1)
    all_top = e1r[0, 0:1]
    for s in range(1, 8):
        all_top = jnp.maximum(all_top, e1r[s, 0:1])
    all_tot = jnp.zeros_like(all_top)
    all_pos = jnp.zeros_like(all_top)
    for s in range(8):
        all_tot = all_tot + e1r[s, 1:2] * jnp.exp(e1r[s, 0:1] - all_top)
        all_pos = all_pos + e1r[s, 2:3]
    lse = all_top + jnp.log(all_tot)
    loss_part = jnp.sum(lse - all_pos, axis=1, keepdims=True)

    pick = (own_j == row_p).astype(f32)
    lse_own = lax.dot_general(
        jnp.broadcast_to(lse, (8, TAKE)), pick, (((1,), (1,)), ((), ())),
        precision=HIGH, preferred_element_type=f32,
    )
    e2s[...] = jnp.where(sub8(ROWS) == 0, lse_own, loss_part)
    e2 = (e2s, e2r, e2_s, e2_r, TP, t, by_tensor)
    exchange(*e2)
    wd = (jnp.exp(logits[0:ROWS] - lse) - (own_j == pos_p).astype(f32)) * (1.0 / PAIRS)
    wts[0:ROWS] = wd.astype(bf16)

    def part_d(block):
        return lax.dot_general(
            wts[0:ROWS], qi[:, lanes(block)], (((1,), (0,)), ((), ())),
            preferred_element_type=f32,
        ) * inv_temp

    MID = ROWS // 2
    pd2[...] = part_d((y + 2) % 4).astype(bf16)
    gc = [
        copy(pd2.at[pl.ds(0, MID)], halfs.at[0], g_s.at[0], g_r.at[0], up),
        copy(pd2.at[pl.ds(MID, MID)], halfs.at[1], g_s.at[1], g_r.at[1], down),
        copy(pd1, r1, g_s.at[2], g_r.at[2], up),
        copy(pdm, r2, g_s.at[3], g_r.at[3], down),
        copy(xsend, xrecv, g_s.at[4], g_r.at[4], partner),
    ]
    begun(gc[0])
    begun(gc[1])

    finish(*e2)
    sums = total(e2r, TP)
    oloss[...] = sums[1:2, 0:1] * (1.0 / PAIRS)
    lse_j = to_rows(sums[0:1])[:, 0:1]
    wq = (jnp.exp(logits[ROWS:] - lse) * (1.0 / PAIRS)).astype(bf16).astype(f32)
    wt = (jnp.exp(logits[ROWS:] - lse_j) * (1.0 / PAIRS)).astype(bf16).astype(f32)
    wts[ROWS:] = (wq + wt).astype(bf16)
    wtt[...] = jnp.transpose(wts[...])

    def target(s):
        return (xh + s // 4) % 2 * 4 + (zc + s % 4) % 4

    def bcopy(f, k, n):
        at = rows_at(place(k, 1 - core, t), n)
        return copy(
            partq.at[at, pl.ds(f * WIDE, WIDE)], sibr.at[k, pl.ds(0, n), pl.ds(f * WIDE, WIDE)],
            b_s.at[f * 8 + k], b_r.at[f * 8 + k], sibling,
        )

    def three(k, core_s):
        return (k // 4) * 2 + core_s == third

    def part_q(f):
        partq[0:TAKE, f * WIDE : (f + 1) * WIDE] = (
            jnp.dot(
                wtt[...], emb[0 : 2 * ROWS, f * WIDE : (f + 1) * WIDE],
                preferred_element_type=f32,
            ) * inv_temp
        ).astype(bf16)

        @pl.loop(0, 8)
        def _(k):
            sized(three(k, 1 - core), lambda n: bcopy(f, k, n).start())

        @sent.append
        def _():
            @pl.loop(0, 8)
            def _(k):
                sized(three(k, 1 - core), lambda n: bcopy(f, k, n).wait_send())

    N3 = 3 * TILE

    def both(f, s):
        k = target(s)
        sized(three(k, core), lambda n: bcopy(f, k, n).wait_recv())
        cs = slice(f * WIDE, (f + 1) * WIDE)
        return partq[rows_at(place(k, core, t), N3), cs].astype(f32) + sibr[k, :, cs].astype(f32)

    FLOW = ((2, zup), (6, zdown), (5, zup), (3, zdown), (1, zup), (7, zdown), (4, across))

    def ucopy(f, i, n):
        cs = pl.ds(f * WIDE, WIDE)
        return copy(
            sendq.at[i, pl.ds(0, n), cs], recvq.at[i, pl.ds(0, n), cs],
            u_s.at[f * 8 + i], u_r.at[f * 8 + i], FLOW[i][1],
        )

    def usend(f, i, value):
        sendq[i, :, f * WIDE : (f + 1) * WIDE] = value.astype(bf16)
        far = three(target(FLOW[i][0]), core)
        sized(far, lambda n: ucopy(f, i, n).start())
        sent.append(lambda: sized(far, lambda n: ucopy(f, i, n).wait_send()))

    def uwait(f, i, s):
        sized(three(target(s), core), lambda n: ucopy(f, i, n).wait_recv())
        return recvq[i, :, f * WIDE : (f + 1) * WIDE].astype(f32)

    def q_far(f):
        usend(f, 0, both(f, 2))
        usend(f, 1, both(f, 6))
        usend(f, 2, both(f, 5))
        usend(f, 3, both(f, 3))

    def q_near(f):
        usend(f, 4, both(f, 1) + uwait(f, 0, 1))
        usend(f, 5, both(f, 7) + uwait(f, 1, 7))

    def q_across(f):
        usend(f, 6, both(f, 4) + uwait(f, 2, 4) + uwait(f, 5, 4))

    def q_own(f):
        gqs[:, f * WIDE : (f + 1) * WIDE] = (
            both(f, 0) + uwait(f, 3, 0) + uwait(f, 4, 0) + uwait(f, 6, 0)
        )

    part_q(0)
    part_q(1)
    gd[...] = part_d((y + 1) % 4)
    gc[0].wait_recv()
    gd[0:MID] = gd[0:MID] + halfs[0].astype(f32)
    pd1[...] = gd[...].astype(bf16)
    begun(gc[2])
    q_far(0)
    gd[...] = part_d((y + 3) % 4)
    gc[1].wait_recv()
    gd[MID:] = gd[MID:] + halfs[1].astype(f32)
    pdm[...] = gd[...].astype(bf16)
    begun(gc[3])
    q_far(1)
    part_q(2)
    part_q(3)
    q_near(0)
    q_far(2)
    q_near(1)
    q_far(3)
    gd[...] = part_d(y)
    q_near(2)
    q_across(0)
    q_near(3)
    q_across(1)
    q_own(0)
    gc[2].wait_recv()
    gc[3].wait_recv()
    gd[...] = gd[...] + r1[...].astype(f32) + r2[...].astype(f32)
    xsend[...] = jnp.where(low == 0, gd[:, FEATS:], gd[:, :FEATS]).astype(bf16)
    begun(gc[4])
    q_across(2)
    q_own(1)
    q_across(3)
    q_own(2)

    gc[4].wait_recv()
    gd[:, 0:FEATS] = jnp.where(low == 0, gd[:, :FEATS], gd[:, FEATS:]) + xrecv[...].astype(f32)
    fd = jnp.sum(gd[:, 0:FEATS] * (xd[...].astype(f32) * gain[...]), axis=1, keepdims=True)
    e3s[...] = to_lanes(fd)
    e3 = (e3s, e3r, e3_s, e3_r, TP, t, by_tensor)
    exchange(*e3)

    q_own(3)
    eq = emb[pl.ds(pl.multiple_of(ROWS + mine * TILE, TILE), N3)].astype(f32)
    dots = jnp.sum(gqs[...] * eq, axis=1, keepdims=True)
    scale = invq[pl.ds(pl.multiple_of(mine * TILE, TILE), N3), 0:1]
    gqs[...] = (gqs[...] - eq * dots) * scale
    for f in range(4):
        asend[f] = gqs[:, f * WIDE : f * WIDE + FEATS].astype(bf16)
        asend[4 + f] = gqs[:, f * WIDE + FEATS : (f + 1) * WIDE].astype(bf16)

    def tcopy(k, n):
        to = (t + k) % TP
        return copy(
            asend.at[to, pl.ds(0, n)], arecv.at[rows_at(mine, n)], t_s.at[k], t_r.at[k], (d, to)
        )

    def trecv(k, n):
        s = (t + TP - k) % TP
        at = arecv.at[rows_at(begin(d4, s), n)]
        return copy(at, at, t_s.at[k], t_r.at[k], (d, s))

    @pl.loop(1, TP)
    def _(k):
        sized(extra, lambda n: tcopy(k, n).start())

    @sent.append
    def _():
        @pl.loop(1, TP)
        def _(k):
            sized(extra, lambda n: tcopy(k, n).wait_send())

    def tlocal(n):
        arecv[rows_at(mine, n)] = asend[t, pl.ds(0, n)]

    sized(extra, tlocal)

    finish(*e3)
    col = to_rows(total(e3r, TP)[0:1])[:, 0:1]
    iv = invd[:, 0:1]
    h = xd[...].astype(f32)
    gx = iv * gd[:, 0:FEATS] - h * gain[...] * (iv * iv * iv * col)
    outd[...] = (gx * gain[...]).astype(bf16)
    outs = [pltpu.make_async_copy(outd, od, io.at[0]), pltpu.make_async_copy(outq, oq, io.at[1])]
    outs[0].start()
    gg = jnp.sum(gx * h, axis=0, keepdims=True)

    @pl.loop(1, TP)
    def _(k):
        sized(d4 == ((t + TP - k) % TP) // 2, lambda n: trecv(k, n).wait_recv())

    gx = arecv[...].astype(f32)
    gg = gg + jnp.sum(gx * xq[...].astype(f32), axis=0, keepdims=True)
    cs4[...] = jnp.broadcast_to(gg, (8, FEATS))
    c4 = copy(cs4, cr4, c_s.at[2], c_r.at[2], sibling)
    begun(c4)
    outq[...] = (gx * gain[...]).astype(bf16)
    outs[1].start()
    c4.wait_recv()
    e4s[...] = cs4[...] + cr4[...]
    e4 = (e4s, e4r, e4_s, e4_r, 8, hz, by_hz)
    exchange(*e4)
    finish(*e4)
    ogain[...] = total(e4r, 8)[0:1]
    for c in outs:
        c.wait()

    for wait in sent:
        wait()


def shards(query_states, doc_states, gain, positives):
    vm = pl.BlockSpec(memory_space=pltpu.VMEM)
    hbm = pl.BlockSpec(memory_space=pl.ANY)
    S = pltpu.VMEM
    dma = lambda n: pltpu.SemaphoreType.DMA((n,))
    pair = lambda n: [dma(n), dma(n)]
    scratch = [
        S((ROWS, FEATS), bf16), S((ROWS, FEATS), bf16),
        S((ROWS, FEATS), bf16), S((ROWS, FEATS), bf16), S((1, FEATS), f32),
        S((2 * ROWS + TILE, FULL), bf16), S((TAKE, FULL), bf16),
        S((ROWS + TILE, 128), f32), S((ROWS, 128), f32),
        S((2 * ROWS, TAKE), f32), S((2 * ROWS, TAKE), bf16), S((TAKE, 2 * ROWS), bf16),
        S((8, ROWS), f32), S((TP, 8, ROWS), f32),
        S((8, TAKE), f32), S((8, TAKE), f32), S((8, TAKE), f32), S((8, 8, TAKE), f32),
        S((8, ROWS), f32), S((TP, 8, ROWS), f32),
        S((8, ROWS), f32), S((TP, 8, ROWS), f32),
        S((8, FEATS), f32), S((8, FEATS), f32), S((8, FEATS), f32), S((8, 8, FEATS), f32),
        S((DP, 8, 128), f32),
        S((TAKE + TILE, FULL), bf16), S((8, 3 * TILE, FULL), bf16),
        S((7, 3 * TILE, FULL), bf16), S((7, 3 * TILE, FULL), bf16),
        S((ROWS, WIDE), bf16), S((ROWS, WIDE), bf16), S((ROWS, WIDE), bf16),
        S((2, ROWS // 2, WIDE), bf16), S((ROWS, WIDE), bf16), S((ROWS, WIDE), bf16),
        S((ROWS, WIDE), f32), S((ROWS, FEATS), bf16), S((ROWS, FEATS), bf16),
        S((TP, 3 * TILE, FEATS), bf16), S((ROWS, FEATS), bf16), S((3 * TILE, FULL), f32),
        S((ROWS, FEATS), bf16), S((ROWS, FEATS), bf16),
    ]
    sems = (
        pair(1 + 2 * NCH) + pair(TP) + pair(8) + pair(TP) + pair(TP) + pair(8) + pair(8)
        + pair(8 * NCH) + pair(64) + [dma(4)] + pair(32) + pair(32) + pair(5) + pair(TP)
        + pair(3) + [dma(2)]
    )
    padded = jnp.pad(positives, (0, 3 * 128 - ROWS)).reshape(3, 128)
    parts = jnp.concatenate([padded // 128, padded % 128, jnp.zeros((2, 128), jnp.int32)])
    gq, gdoc, ggain, loss = pl.pallas_call(
        step,
        name="infonce_step",
        out_shape=(
            jax.ShapeDtypeStruct((ROWS, FEATS), bf16),
            jax.ShapeDtypeStruct((ROWS, FEATS), bf16),
            jax.ShapeDtypeStruct((1, FEATS), f32),
            jax.ShapeDtypeStruct((1, 1), f32),
        ),
        in_specs=[hbm, hbm, vm, vm],
        out_specs=(hbm, hbm, vm, vm),
        scratch_shapes=scratch + sems,
        compiler_params=pltpu.CompilerParams(
            collective_id=0, has_side_effects=True, vmem_limit_bytes=56 * 2**20
        ),
        cost_estimate=pl.CostEstimate(
            flops=7_000_000_000, bytes_accessed=3_000_000, transcendentals=1_000_000
        ),
    )(query_states, doc_states, gain[None, :], parts.astype(f32))
    return gq, gdoc, ggain[0], loss[0, 0]


def solution(mesh):
    return jax.shard_map(
        shards,
        mesh=mesh,
        in_specs=(P("dp", "tensor"), P("dp", "tensor"), P("tensor"), P("dp")),
        out_specs=(P("dp", "tensor"), P("dp", "tensor"), P("tensor"), P()),
        check_vma=False,
    )
```

```python
import functools

import jax
import jax.numpy as jnp
from jax import lax
from jax.experimental import pallas as pl
from jax.experimental.pallas import tpu as pltpu
from jax.sharding import PartitionSpec as P

eps_len = 1e-06
inv_temp = 100.0
masked = -1e30

MESH = pl.DeviceIdType.MESH
HIGH = lax.Precision.HIGHEST
f32 = jnp.float32
bf16 = jnp.bfloat16

DP = 16
TP = 8
ROWS = 288
FEATS = 448
WIDE = 2 * FEATS
FULL = TP * FEATS
PAIRS = DP * ROWS
TAKE = DP * ROWS // TP
TILE = 16
CHUNK = 96
NCH = ROWS // CHUNK
HALF = CHUNK // 2


def step(
    hq, hd, gain, pos,
    oq, od, ogain, oloss,
    xq, xd, pq, pd, gfull, raw, emb, qi, invq, invd, logits, stat, wts, wtt,
    e0s, e0r, cr1, e1s, e1r, e2s, e2r, e3s, e3r, cs4, cr4, e4s, e4r, epr,
    partq, sibr, sendq, recvq, pd2, pd1, pdm, halfs, r1, r2, gd, xsend, xrecv,
    asend, arecv, dsend, drecv, outq, outd,
    x_s, x_r, e0_s, e0_r, e1_s, e1_r, e2_s, e2_r, e3_s, e3_r, e4_s, e4_r, ep_s, ep_r,
    y_s, y_r, a_s, a_r, loc, b_s, b_r, u_s, u_r, g_s, g_r, t_s, t_r, v_s, v_r, c_s, c_r, io,
):
    d = lax.axis_index("dp")
    t = lax.axis_index("tensor")
    hz = d // 2
    core = d % 2
    zc = hz % 4
    d4 = (hz // 4) * 2 + core
    low = t // 4
    y = t % 4
    xh = hz // 4
    sources = [pltpu.make_async_copy(hq, xq, io.at[0]), pltpu.make_async_copy(hd, xd, io.at[1])]
    for c in sources:
        c.start()
    third = t // 2
    sibling = (hz * 2 + (1 - core), t)
    partner = (d, (t + 4) % TP)
    up = (d, low * 4 + (y + 1) % 4)
    down = (d, low * 4 + (y + 3) % 4)
    zup = ((xh * 4 + (zc + 1) % 4) * 2 + core, t)
    zdown = ((xh * 4 + (zc + 3) % 4) * 2 + core, t)
    across = ((hz + 4) % 8 * 2 + core, t)

    sent = []

    def copy(src, dst, ss, rs, dev):
        return pltpu.make_async_remote_copy(
            src_ref=src, dst_ref=dst, send_sem=ss, recv_sem=rs, device_id=dev, device_id_type=MESH
        )

    def lanes(block):
        return pl.ds(pl.multiple_of(block * WIDE, 128), WIDE)

    def rows_at(tile, n):
        return pl.ds(pl.multiple_of(tile * TILE, TILE), n)

    def place(hz_s, core_s, tens):
        q = (hz_s // 4) * 2 + core_s
        e = tens // 2
        return (hz_s % 4) * 9 + 2 * q + jnp.where(q > e, 1, 0)

    def begin(q, tens):
        return 2 * tens + jnp.clip(tens - 2 * q, 0, 2)

    def sized(extra, fn):
        @pl.when(extra)
        def _():
            fn(3 * TILE)

        @pl.when(jnp.logical_not(extra))
        def _():
            fn(2 * TILE)

    barrier = pltpu.get_barrier_semaphore()

    @pl.loop(1, TP)
    def _(k):
        pl.semaphore_signal(barrier, inc=1, device_id=(d, (t + k) % TP), device_id_type=MESH)

    @pl.loop(1, 8)
    def _(k):
        pl.semaphore_signal(
            barrier, inc=1, device_id=((hz + k) % 8 * 2 + core, t), device_id_type=MESH
        )

    pl.semaphore_signal(barrier, inc=1, device_id=sibling, device_id_type=MESH)
    def to_lanes(col):
        return jnp.transpose(jnp.broadcast_to(col, (ROWS, 128)))[:8]

    def to_rows(vec):
        return jnp.transpose(jnp.broadcast_to(vec, (128, ROWS)))

    sub8 = lambda n: lax.broadcasted_iota(jnp.int32, (8, n), 0)

    for c in sources:
        c.wait()
    nq = xq[...].astype(f32) * gain[...]
    nd = xd[...].astype(f32) * gain[...]
    lq = to_lanes(jnp.sum(nq * nq, axis=1, keepdims=True))
    ld = to_lanes(jnp.sum(nd * nd, axis=1, keepdims=True))
    e0s[...] = jnp.broadcast_to(gain[...], (8, FEATS))
    e0s[0:1, 0:ROWS] = lq[0:1]
    e0s[1:2, 0:ROWS] = ld[0:1]
    pl.semaphore_wait(barrier, TP + 7)

    def xcopy(i):
        src, dst = (xq, pq) if i < NCH else (xd, pd)
        part = pl.ds((i % NCH) * CHUNK, CHUNK)
        return copy(src.at[part], dst.at[part], x_s.at[i], x_r.at[i], partner)

    def begun(c):
        c.start()
        sent.append(c.wait_send)

    def exchange(src, recv, ss, rs, size, me, dev):
        @pl.loop(1, size)
        def _(k):
            copy(src, recv.at[me], ss.at[k], rs.at[me], dev((me + k) % size)).start()

        @sent.append
        def _():
            @pl.loop(1, size)
            def _(k):
                copy(src, recv.at[me], ss.at[k], rs.at[me], dev((me + k) % size)).wait_send()

    def finish(src, recv, ss, rs, size, me, dev):
        recv[me] = src[...]

        @pl.loop(1, size)
        def _(k):
            s = (me + k) % size
            copy(src, recv.at[s], ss.at[k], rs.at[s], dev(s)).wait_recv()

    by_tensor = lambda s: (d, s)
    by_hz = lambda s: (s * 2 + core, t)

    def total(recv, size):
        acc = recv[0]
        for s in range(1, size):
            acc = acc + recv[s]
        return acc

    e0 = (e0s, e0r, e0_s, e0_r, TP, t, by_tensor)
    begun(xcopy(0))
    exchange(*e0)
    for i in range(1, 2 * NCH):
        begun(xcopy(i))

    mine = begin(d4, t)
    here = place(hz, core, t)
    extra = d4 == third

    def pack(a, k):
        own, part, base = (xq, pq, ROWS) if a == 0 else (xd, pd, 0)
        xcopy(a * NCH + k).wait_recv()
        rs = pl.ds(k * CHUNK, CHUNK)
        eo = own[rs].astype(f32)
        ep = part[rs].astype(f32)
        left = jnp.where(low == 0, eo, ep)
        right = jnp.where(low == 0, ep, eo)
        raw[pl.ds(base + k * CHUNK, CHUNK), lanes(y)] = jnp.concatenate(
            [left, right], axis=1
        ).astype(bf16)

    def normalise(a, k, block):
        inverse, base = (invq, ROWS) if a == 0 else (invd, 0)
        for part in range(2):
            rs = k * CHUNK + part * HALF
            scale = inverse[pl.ds(rs, HALF), 0:1]
            at = pl.ds(base + rs, HALF)
            cs = lanes(block)
            emb[at, cs] = (raw[at, cs].astype(f32) * gfull[:, cs] * scale).astype(bf16)

    def ycopy(a, k, kind):
        base = (ROWS if a == 0 else 0) + k * CHUNK
        i = (a * NCH + k) * 4 + kind
        if kind < 2:
            at, dev, block = pl.ds(base, CHUNK), (up, down)[kind], y
        elif kind == 2:
            at, dev, block = pl.ds(base, HALF), up, (y + 3) % 4
        else:
            at, dev, block = pl.ds(base + HALF, HALF), down, (y + 1) % 4
        ref = raw.at[at, lanes(block)]
        return copy(ref, ref, y_s.at[i], y_r.at[i], dev)

    def yrecv(a, k, kind):
        base = (ROWS if a == 0 else 0) + k * CHUNK
        i = (a * NCH + k) * 4 + kind
        at = pl.ds(base, CHUNK) if kind < 2 else pl.ds(base + (kind - 2) * HALF, HALF)
        block = ((y + 3) % 4, (y + 1) % 4, (y + 2) % 4, (y + 2) % 4)[kind]
        ref = raw.at[at, lanes(block)]
        copy(ref, ref, y_s.at[i], y_r.at[i], up).wait_recv()

    def arow(i, hz_s, core_s, n):
        block = (y + (0, 3, 1, 2)[i]) % 4
        return qi.at[rows_at(place(hz_s, core_s, t), n), lanes(block)]

    def own_rows(i, n):
        block = (y + (0, 3, 1, 2)[i]) % 4
        return emb.at[pl.ds(pl.multiple_of(ROWS + mine * TILE, TILE), n), lanes(block)]

    def acopy(i, k, n):
        to = (hz + k) % 8 * 2 + jnp.where(k == 0, 1 - core, core)
        return copy(
            own_rows(i, n), arow(i, hz, core, n), a_s.at[i * 16 + k], a_r.at[i * 16 + k], (to, t)
        )

    def alocal(i, n):
        return pltpu.make_async_copy(own_rows(i, n), arow(i, hz, core, n), loc.at[i])

    def arrived(i, k, core_s, slot, n):
        ref = arow(i, (hz + 8 - k) % 8, core_s, n)
        return copy(ref, ref, a_s.at[i * 16 + slot], a_r.at[i * 16 + slot], sibling)

    def gives(k, core_s):
        return (((hz + 8 - k) % 8) // 4) * 2 + core_s == third

    def astart(i):
        @pl.loop(0, 8)
        def _(k):
            sized(extra, lambda n: acopy(i, k, n).start())

        sized(extra, lambda n: alocal(i, n).start())

        @sent.append
        def _():
            @pl.loop(0, 8)
            def _(k):
                sized(extra, lambda n: acopy(i, k, n).wait_send())

    def aforward(i):
        @pl.loop(1, 8)
        def _(k):
            def pass_on(n):
                arrived(i, k, core, k, n).wait_recv()
                arrived(i, k, core, 8 + k, n).start()

            sized(gives(k, core), pass_on)

        @sent.append
        def _():
            @pl.loop(1, 8)
            def _(k):
                sized(gives(k, core), lambda n: arrived(i, k, core, 8 + k, n).wait_send())

    def afinish(i):
        sized(extra, lambda n: alocal(i, n).wait())
        sized(gives(0, 1 - core), lambda n: arrived(i, 0, 1 - core, 0, n).wait_recv())

        @pl.loop(1, 8)
        def _(k):
            sized(gives(k, 1 - core), lambda n: arrived(i, k, 1 - core, 8 + k, n).wait_recv())

    for k in range(NCH):
        pack(0, k)
        begun(ycopy(0, k, 0))
        begun(ycopy(0, k, 1))
    finish(*e0)
    inv = lax.rsqrt(total(e0r, TP)[:, 0:ROWS] + eps_len)
    invq[0:ROWS] = to_rows(inv[0:1])
    invd[...] = to_rows(inv[1:2])
    for b in range(4):
        gfull[:, b * WIDE : (b + 1) * WIDE] = jnp.concatenate(
            [e0r[b, 2:3], e0r[4 + b, 2:3]], axis=1
        )
    for k in range(NCH):
        normalise(0, k, y)
    astart(0)
    ep = (pos, epr, ep_s, ep_r, 8, hz, by_hz)
    exchange(*ep)
    for k in range(NCH):
        yrecv(0, k, 0)
        begun(ycopy(0, k, 2))
        yrecv(0, k, 1)
        begun(ycopy(0, k, 3))
        pack(1, k)
        begun(ycopy(1, k, 0))
        begun(ycopy(1, k, 1))
        normalise(0, k, (y + 3) % 4)
        normalise(0, k, (y + 1) % 4)
    astart(1)
    astart(2)
    aforward(0)
    for k in range(NCH):
        normalise(1, k, y)
        yrecv(0, k, 2)
        yrecv(0, k, 3)
        normalise(0, k, (y + 2) % 4)
    astart(3)
    aforward(1)
    aforward(2)
    for k in range(NCH):
        yrecv(1, k, 0)
        begun(ycopy(1, k, 2))
        yrecv(1, k, 1)
        begun(ycopy(1, k, 3))
    for k in range(NCH):
        normalise(1, k, (y + 3) % 4)
        normalise(1, k, (y + 1) % 4)
    aforward(3)
    for i in range(4):
        afinish(i)

    lane_p = lax.broadcasted_iota(jnp.int32, (1, TAKE), 1)
    tile_p = lane_p // TILE
    w_p = tile_p % 9
    q_p = jnp.where(
        w_p < 2 * third, w_p // 2, jnp.where(w_p <= 2 * third + 2, third, (w_p - 1) // 2)
    )
    off_p = w_p - 2 * q_p - jnp.where(q_p > third, 1, 0)
    dev_p = (q_p // 2) * 8 + (tile_p // 9) * 2 + q_p % 2
    row_p = dev_p * ROWS + (begin(q_p, t) + off_p) * TILE + lane_p % TILE
    finish(*ep)
    epc = copy(epr.at[pl.ds(0, 8)], epr.at[pl.ds(8, 8)], c_s.at[0], c_r.at[0], sibling)
    begun(epc)

    stat[0:1] = jnp.full((1, TAKE), masked, f32)
    stat[1:8] = jnp.zeros((7, TAKE), f32)

    def logit_rows(r, query):
        at = pl.ds(pl.multiple_of(r, TILE), CHUNK)
        s = lax.dot_general(
            emb[at], qi[...], (((1,), (1,)), ((), ())), preferred_element_type=f32
        ) * inv_temp
        row = lax.broadcasted_iota(jnp.int32, (CHUNK, TAKE), 0)
        if query:
            s = jnp.where(d * ROWS + r - ROWS + row == row_p, masked, s)
        else:
            hit = jnp.where(d * ROWS + r + row == pos_p, s, 0.0)
            stat[2:3] = stat[2:3] + jnp.sum(hit, axis=0, keepdims=True)
        logits[at] = s
        old = stat[0:1]
        new = jnp.maximum(old, jnp.max(s, axis=0, keepdims=True))
        stat[0:1] = new
        stat[1:2] = stat[1:2] * jnp.exp(old - new) + jnp.sum(
            jnp.exp(s - new), axis=0, keepdims=True
        )

    @pl.loop(0, NCH)
    def _(m):
        logit_rows(ROWS + m * CHUNK, True)

    epc.wait_recv()
    local_p = (begin(q_p, t) + off_p) * TILE + lane_p % TILE
    lane_of = lax.broadcasted_iota(jnp.int32, (128, TAKE), 0)
    spread = jnp.where(lane_of == local_p % 128, 1.0, 0.0).astype(bf16)
    found = jnp.dot(
        epr[...].reshape(DP * 8, 128).astype(bf16), spread, preferred_element_type=f32
    )
    slot_p = jnp.where(dev_p % 2 == core, dev_p // 2, 8 + dev_p // 2) * 8 + local_p // 128
    high = jnp.sum(jnp.where(lane_of == slot_p, found, 0.0), axis=0, keepdims=True)
    rest = jnp.sum(jnp.where(lane_of == slot_p + 3, found, 0.0), axis=0, keepdims=True)
    pos_p = (high * 128.0 + rest).astype(jnp.int32)

    for k in range(NCH):
        yrecv(1, k, 2)
        yrecv(1, k, 3)
        normalise(1, k, (y + 2) % 4)
        logit_rows(k * CHUNK, False)

    own_j = d * ROWS + lax.broadcasted_iota(jnp.int32, (ROWS, TAKE), 0)
    sub_t = sub8(TAKE)
    c1 = copy(stat, cr1, c_s.at[1], c_r.at[1], sibling)
    begun(c1)
    c1.wait_recv()
    top, tot, posit = stat[0:1], stat[1:2], stat[2:3]
    top_o = cr1[0:1]
    top_c = jnp.maximum(top, top_o)
    tot = tot * jnp.exp(top - top_c) + cr1[1:2] * jnp.exp(top_o - top_c)
    e1s[...] = jnp.where(sub_t == 0, top_c, jnp.where(sub_t == 1, tot, posit + cr1[2:3]))
    e1 = (e1s, e1r, e1_s, e1_r, 8, hz, by_hz)
    exchange(*e1)
    pick = jnp.where(own_j == row_p, 1.0, 0.0).astype(bf16)
    finish(*e1)
    all_top = e1r[0, 0:1]
    for s in range(1, 8):
        all_top = jnp.maximum(all_top, e1r[s, 0:1])
    all_tot = jnp.zeros_like(all_top)
    all_pos = jnp.zeros_like(all_top)
    for s in range(8):
        all_tot = all_tot + e1r[s, 1:2] * jnp.exp(e1r[s, 0:1] - all_top)
        all_pos = all_pos + e1r[s, 2:3]
    lse = all_top + jnp.log(all_tot)
    loss_part = jnp.sum(lse - all_pos, axis=1, keepdims=True)

    lse1 = lse.astype(bf16).astype(f32)
    lse2 = (lse - lse1).astype(bf16).astype(f32)
    split = jnp.where(
        sub_t == 0, lse1, jnp.where(sub_t == 1, lse2, jnp.where(sub_t == 2, lse - lse1 - lse2, 0.0))
    )
    lse_own = jnp.sum(
        lax.dot_general(
            split.astype(bf16), pick, (((1,), (1,)), ((), ())), preferred_element_type=f32
        ),
        axis=0, keepdims=True,
    )
    e2s[...] = jnp.where(sub8(ROWS) == 0, lse_own, loss_part)
    e2 = (e2s, e2r, e2_s, e2_r, TP, t, by_tensor)
    exchange(*e2)
    wd = (jnp.exp(logits[0:ROWS] - lse) - (own_j == pos_p).astype(f32)) * (1.0 / PAIRS)
    wts[0:ROWS] = wd.astype(bf16)

    def part_d(block):
        return lax.dot_general(
            wts[0:ROWS], qi[:, lanes(block)], (((1,), (0,)), ((), ())),
            preferred_element_type=f32,
        ) * inv_temp

    MID = ROWS // 2
    pd2[...] = part_d((y + 2) % 4).astype(bf16)
    gc = [
        copy(pd2.at[pl.ds(0, MID)], halfs.at[0], g_s.at[0], g_r.at[0], up),
        copy(pd2.at[pl.ds(MID, MID)], halfs.at[1], g_s.at[1], g_r.at[1], down),
        copy(pd1, r1, g_s.at[2], g_r.at[2], up),
        copy(pdm, r2, g_s.at[3], g_r.at[3], down),
        copy(xsend, xrecv, g_s.at[4], g_r.at[4], partner),
    ]
    begun(gc[0])
    begun(gc[1])

    finish(*e2)
    sums = total(e2r, TP)
    oloss[...] = sums[1:2, 0:1] * (1.0 / PAIRS)
    lse_j = to_rows(sums[0:1])[:, 0:1]
    wq = (jnp.exp(logits[ROWS:] - lse) * (1.0 / PAIRS)).astype(bf16).astype(f32)
    wt = (jnp.exp(logits[ROWS:] - lse_j) * (1.0 / PAIRS)).astype(bf16).astype(f32)
    wts[ROWS:] = (wq + wt).astype(bf16)
    wtt[...] = jnp.transpose(wts[...])

    def target(s):
        return (xh + s // 4) % 2 * 4 + (zc + s % 4) % 4

    def cols(f):
        return lanes((y + 1 + f) % 4)

    def bcopy(f, k, n):
        at = rows_at(place(k, 1 - core, t), n)
        return copy(
            partq.at[at, cols(f)], sibr.at[k, pl.ds(0, n), cols(f)],
            b_s.at[f * 8 + k], b_r.at[f * 8 + k], sibling,
        )

    def three(k, core_s):
        return (k // 4) * 2 + core_s == third

    def part_q(f):
        partq[0:TAKE, cols(f)] = (
            jnp.dot(
                wtt[...], emb[0 : 2 * ROWS, cols(f)],
                preferred_element_type=f32,
            ) * inv_temp
        ).astype(bf16)

        @pl.loop(0, 8)
        def _(k):
            sized(three(k, 1 - core), lambda n: bcopy(f, k, n).start())

        @sent.append
        def _():
            @pl.loop(0, 8)
            def _(k):
                sized(three(k, 1 - core), lambda n: bcopy(f, k, n).wait_send())

    N3 = 3 * TILE

    def both(f, s):
        k = target(s)
        sized(three(k, core), lambda n: bcopy(f, k, n).wait_recv())
        cs = cols(f)
        return partq[rows_at(place(k, core, t), N3), cs].astype(f32) + sibr[k, :, cs].astype(f32)

    FLOW = ((2, zup), (6, zdown), (5, zup), (3, zdown), (1, zup), (7, zdown), (4, across))

    def ucopy(f, i, n):
        cs = cols(f)
        return copy(
            sendq.at[i, pl.ds(0, n), cs], recvq.at[i, pl.ds(0, n), cs],
            u_s.at[f * 8 + i], u_r.at[f * 8 + i], FLOW[i][1],
        )

    def usend(f, i, value):
        sendq[i, :, cols(f)] = value.astype(bf16)
        far = three(target(FLOW[i][0]), core)
        sized(far, lambda n: ucopy(f, i, n).start())
        sent.append(lambda: sized(far, lambda n: ucopy(f, i, n).wait_send()))

    def uwait(f, i, s):
        sized(three(target(s), core), lambda n: ucopy(f, i, n).wait_recv())
        return recvq[i, :, cols(f)].astype(f32)

    def q_far(f):
        usend(f, 0, both(f, 2))
        usend(f, 1, both(f, 6))
        usend(f, 2, both(f, 5))
        usend(f, 3, both(f, 3))

    def q_near(f):
        usend(f, 4, both(f, 1) + uwait(f, 0, 1))
        usend(f, 5, both(f, 7) + uwait(f, 1, 7))

    def q_across(f):
        usend(f, 6, both(f, 4) + uwait(f, 2, 4) + uwait(f, 5, 4))

    def tcopy(f, far, n):
        to = (y + 1 + f) % 4 + 4 * ((low + far) % 2)
        return copy(
            asend.at[to, pl.ds(0, n)], arecv.at[rows_at(mine, n)],
            t_s.at[f * 2 + far], t_r.at[f * 2 + far], (d, to),
        )

    def trecv(f, far):
        s = (y + 3 - f) % 4 + 4 * ((low + far) % 2)
        at = lambda n: arecv.at[rows_at(begin(d4, s), n)]
        sized(
            d4 == s // 2,
            lambda n: copy(at(n), at(n), t_s.at[0], t_r.at[f * 2 + far], (d, s)).wait_recv(),
        )

    def q_own(f):
        g = both(f, 0) + uwait(f, 3, 0) + uwait(f, 4, 0) + uwait(f, 6, 0)
        fb = (y + 1 + f) % 4
        asend[fb] = g[:, :FEATS].astype(bf16)
        asend[4 + fb] = g[:, FEATS:].astype(bf16)
        for far in range(2):
            if f < 3 or far == 1:
                sized(extra, lambda n: tcopy(f, far, n).start())
                sent.append(
                    lambda far=far: sized(extra, lambda n: tcopy(f, far, n).wait_send())
                )
        eq = emb[pl.ds(pl.multiple_of(ROWS + mine * TILE, TILE), N3), lanes(fb)].astype(f32)
        return jnp.sum(g * eq, axis=1, keepdims=True)

    part_q(0)
    part_q(1)
    gd[...] = part_d((y + 1) % 4)
    gc[0].wait_recv()
    gd[0:MID] = gd[0:MID] + halfs[0].astype(f32)
    pd1[...] = gd[...].astype(bf16)
    begun(gc[2])
    q_far(0)
    gd[...] = part_d((y + 3) % 4)
    gc[1].wait_recv()
    gd[MID:] = gd[MID:] + halfs[1].astype(f32)
    pdm[...] = gd[...].astype(bf16)
    begun(gc[3])
    q_far(1)
    part_q(2)
    part_q(3)
    q_near(0)
    q_far(2)
    q_near(1)
    q_far(3)
    gd[...] = part_d(y)
    q_near(2)
    q_across(0)
    q_near(3)
    q_across(1)
    dots = q_own(0)
    gc[2].wait_recv()
    gc[3].wait_recv()
    gd[...] = gd[...] + r1[...].astype(f32) + r2[...].astype(f32)
    xsend[...] = jnp.where(low == 0, gd[:, FEATS:], gd[:, :FEATS]).astype(bf16)
    begun(gc[4])
    q_across(2)
    dots = dots + q_own(1)
    q_across(3)
    dots = dots + q_own(2)

    gc[4].wait_recv()
    gd[:, 0:FEATS] = jnp.where(low == 0, gd[:, :FEATS], gd[:, FEATS:]) + xrecv[...].astype(f32)
    fd = jnp.sum(gd[:, 0:FEATS] * (xd[...].astype(f32) * gain[...]), axis=1, keepdims=True)
    e3s[...] = to_lanes(fd)
    e3 = (e3s, e3r, e3_s, e3_r, TP, t, by_tensor)
    exchange(*e3)

    dots = dots + q_own(3)
    dsend[...] = jnp.broadcast_to(dots, (N3, 128))

    def vcopy(k, n):
        to = (t + k) % TP
        return copy(
            dsend.at[pl.ds(0, n)], drecv.at[rows_at(mine, n)], v_s.at[k], v_r.at[k], (d, to)
        )

    def vrecv(k, n):
        s = (t + TP - k) % TP
        at = drecv.at[rows_at(begin(d4, s), n)]
        return copy(at, at, v_s.at[k], v_r.at[k], (d, s))

    @pl.loop(1, TP)
    def _(k):
        sized(extra, lambda n: vcopy(k, n).start())

    @sent.append
    def _():
        @pl.loop(1, TP)
        def _(k):
            sized(extra, lambda n: vcopy(k, n).wait_send())

    def tlocal(n):
        arecv[rows_at(mine, n)] = asend[t, pl.ds(0, n)]
        drecv[rows_at(mine, n)] = dsend[pl.ds(0, n)]

    sized(extra, tlocal)

    finish(*e3)
    col = to_rows(total(e3r, TP)[0:1])[:, 0:1]
    iv = invd[:, 0:1]
    h = xd[...].astype(f32)
    gx = iv * gd[:, 0:FEATS] - h * gain[...] * (iv * iv * iv * col)
    outd[...] = (gx * gain[...]).astype(bf16)
    outs = [pltpu.make_async_copy(outd, od, io.at[0]), pltpu.make_async_copy(outq, oq, io.at[1])]
    outs[0].start()
    gg = jnp.sum(gx * h, axis=0, keepdims=True)

    for f in range(4):
        for far in range(2):
            if f < 3 or far == 1:
                trecv(f, far)

    @pl.loop(1, TP)
    def _(k):
        sized(d4 == ((t + TP - k) % TP) // 2, lambda n: vrecv(k, n).wait_recv())

    h = xq[...].astype(f32)
    iv = invq[0:ROWS, 0:1]
    gx = iv * arecv[...].astype(f32) - h * gain[...] * (iv * iv * drecv[:, 0:1])
    gg = gg + jnp.sum(gx * h, axis=0, keepdims=True)
    cs4[...] = jnp.broadcast_to(gg, (8, FEATS))
    c4 = copy(cs4, cr4, c_s.at[2], c_r.at[2], sibling)
    begun(c4)
    outq[...] = (gx * gain[...]).astype(bf16)
    outs[1].start()
    c4.wait_recv()
    e4s[...] = cs4[...] + cr4[...]
    e4 = (e4s, e4r, e4_s, e4_r, 8, hz, by_hz)
    exchange(*e4)
    finish(*e4)
    ogain[...] = total(e4r, 8)[0:1]
    for c in outs:
        c.wait()

    for wait in sent:
        wait()


def shards(query_states, doc_states, gain, positives):
    vm = pl.BlockSpec(memory_space=pltpu.VMEM)
    hbm = pl.BlockSpec(memory_space=pl.ANY)
    S = pltpu.VMEM
    dma = lambda n: pltpu.SemaphoreType.DMA((n,))
    pair = lambda n: [dma(n), dma(n)]
    scratch = [
        S((ROWS, FEATS), bf16), S((ROWS, FEATS), bf16),
        S((ROWS, FEATS), bf16), S((ROWS, FEATS), bf16), S((1, FULL), f32),
        S((2 * ROWS, FULL), bf16), S((2 * ROWS + TILE, FULL), bf16), S((TAKE, FULL), bf16),
        S((ROWS + TILE, 128), f32), S((ROWS, 128), f32),
        S((2 * ROWS, TAKE), f32), S((8, TAKE), f32), S((2 * ROWS, TAKE), bf16), S((TAKE, 2 * ROWS), bf16),
        S((8, FEATS), f32), S((TP, 8, FEATS), f32),
        S((8, TAKE), f32), S((8, TAKE), f32), S((8, 8, TAKE), f32),
        S((8, ROWS), f32), S((TP, 8, ROWS), f32),
        S((8, ROWS), f32), S((TP, 8, ROWS), f32),
        S((8, FEATS), f32), S((8, FEATS), f32), S((8, FEATS), f32), S((8, 8, FEATS), f32),
        S((DP, 8, 128), f32),
        S((TAKE + TILE, FULL), bf16), S((8, 3 * TILE, FULL), bf16),
        S((7, 3 * TILE, FULL), bf16), S((7, 3 * TILE, FULL), bf16),
        S((ROWS, WIDE), bf16), S((ROWS, WIDE), bf16), S((ROWS, WIDE), bf16),
        S((2, ROWS // 2, WIDE), bf16), S((ROWS, WIDE), bf16), S((ROWS, WIDE), bf16),
        S((ROWS, WIDE), f32), S((ROWS, FEATS), bf16), S((ROWS, FEATS), bf16),
        S((TP, 3 * TILE, FEATS), bf16), S((ROWS, FEATS), bf16), S((3 * TILE, 128), f32), S((ROWS, 128), f32),
        S((ROWS, FEATS), bf16), S((ROWS, FEATS), bf16),
    ]
    sems = (
        pair(2 * NCH) + pair(TP) + pair(8) + pair(TP) + pair(TP) + pair(8) + pair(8)
        + pair(8 * NCH) + pair(64) + [dma(4)] + pair(32) + pair(32) + pair(5) + pair(TP) + pair(TP)
        + pair(3) + [dma(2)]
    )
    padded = jnp.pad(positives, (0, 3 * 128 - ROWS)).reshape(3, 128)
    parts = jnp.concatenate([padded // 128, padded % 128, jnp.zeros((2, 128), jnp.int32)])
    gq, gdoc, ggain, loss = pl.pallas_call(
        step,
        name="infonce_step",
        out_shape=(
            jax.ShapeDtypeStruct((ROWS, FEATS), bf16),
            jax.ShapeDtypeStruct((ROWS, FEATS), bf16),
            jax.ShapeDtypeStruct((1, FEATS), f32),
            jax.ShapeDtypeStruct((1, 1), f32),
        ),
        in_specs=[hbm, hbm, vm, vm],
        out_specs=(hbm, hbm, vm, vm),
        scratch_shapes=scratch + sems,
        compiler_params=pltpu.CompilerParams(
            collective_id=0, has_side_effects=True, vmem_limit_bytes=56 * 2**20
        ),
        cost_estimate=pl.CostEstimate(
            flops=7_000_000_000, bytes_accessed=3_000_000, transcendentals=1_000_000
        ),
    )(query_states, doc_states, gain[None, :], parts.astype(f32))
    return gq, gdoc, ggain[0], loss[0, 0]


def solution(mesh):
    return jax.shard_map(
        shards,
        mesh=mesh,
        in_specs=(P("dp", "tensor"), P("dp", "tensor"), P("tensor"), P("dp")),
        out_specs=(P("dp", "tensor"), P("dp", "tensor"), P("tensor"), P()),
        check_vma=False,
    )
```

```python
import functools

import jax
import jax.numpy as jnp
from jax import lax
from jax.experimental import pallas as pl
from jax.experimental.pallas import tpu as pltpu
from jax.sharding import PartitionSpec as P

eps_len = 1e-06
inv_temp = 100.0
masked = -1e30

MESH = pl.DeviceIdType.MESH
HIGH = lax.Precision.HIGHEST
f32 = jnp.float32
bf16 = jnp.bfloat16

DP = 16
TP = 8
ROWS = 288
FEATS = 448
WIDE = 2 * FEATS
FULL = TP * FEATS
PAIRS = DP * ROWS
TAKE = DP * ROWS // TP
TILE = 16
CHUNK = 96
NCH = ROWS // CHUNK
HALF = CHUNK // 2


def step(
    hq, hd, gain, pos,
    oq, od, ogain, oloss,
    xq, xd, pq, pd, gfull, raw, emb, qi, invq, invd, logits, stat, wts, wtt,
    e0s, e0r, cr1, e1s, e1r, e2s, e2r, e3s, e3r, cs4, cr4, e4s, e4r, epr,
    partq, sibr, sendq, recvq, acc1, acc2, pd2, pd1, pdm, halfs, r1, r2, gd, xsend, xrecv,
    asend, arecv, dsend, drecv, outq, outd,
    x_s, x_r, e0_s, e0_r, e1_s, e1_r, e2_s, e2_r, e3_s, e3_r, e4_s, e4_r, ep_s, ep_r,
    y_s, y_r, a_s, a_r, loc, b_s, b_r, u_s, u_r, g_s, g_r, t_s, t_r, v_s, v_r, c_s, c_r, io,
):
    d = lax.axis_index("dp")
    t = lax.axis_index("tensor")
    hz = d // 2
    core = d % 2
    zc = hz % 4
    d4 = (hz // 4) * 2 + core
    low = t // 4
    y = t % 4
    xh = hz // 4
    sources = [pltpu.make_async_copy(hq, xq, io.at[0]), pltpu.make_async_copy(hd, xd, io.at[1])]
    for c in sources:
        c.start()
    third = t // 2
    sibling = (hz * 2 + (1 - core), t)
    partner = (d, (t + 4) % TP)
    up = (d, low * 4 + (y + 1) % 4)
    down = (d, low * 4 + (y + 3) % 4)
    zup = ((xh * 4 + (zc + 1) % 4) * 2 + core, t)
    zdown = ((xh * 4 + (zc + 3) % 4) * 2 + core, t)
    across = ((hz + 4) % 8 * 2 + core, t)

    sent = []

    def copy(src, dst, ss, rs, dev):
        return pltpu.make_async_remote_copy(
            src_ref=src, dst_ref=dst, send_sem=ss, recv_sem=rs, device_id=dev, device_id_type=MESH
        )

    def lanes(block):
        return pl.ds(pl.multiple_of(block * WIDE, 128), WIDE)

    def rows_at(tile, n):
        return pl.ds(pl.multiple_of(tile * TILE, TILE), n)

    def place(hz_s, core_s, tens):
        q = (hz_s // 4) * 2 + core_s
        e = tens // 2
        return (hz_s % 4) * 9 + 2 * q + jnp.where(q > e, 1, 0)

    def begin(q, tens):
        return 2 * tens + jnp.clip(tens - 2 * q, 0, 2)

    def sized(extra, fn):
        @pl.when(extra)
        def _():
            fn(3 * TILE)

        @pl.when(jnp.logical_not(extra))
        def _():
            fn(2 * TILE)

    barrier = pltpu.get_barrier_semaphore()

    @pl.loop(1, TP)
    def _(k):
        pl.semaphore_signal(barrier, inc=1, device_id=(d, (t + k) % TP), device_id_type=MESH)

    @pl.loop(1, 8)
    def _(k):
        pl.semaphore_signal(
            barrier, inc=1, device_id=((hz + k) % 8 * 2 + core, t), device_id_type=MESH
        )

    pl.semaphore_signal(barrier, inc=1, device_id=sibling, device_id_type=MESH)
    def to_lanes(col):
        return jnp.transpose(jnp.broadcast_to(col, (ROWS, 128)))[:8]

    def to_rows(vec):
        return jnp.transpose(jnp.broadcast_to(vec, (128, ROWS)))

    sub8 = lambda n: lax.broadcasted_iota(jnp.int32, (8, n), 0)

    for c in sources:
        c.wait()
    nq = xq[...].astype(f32) * gain[...]
    nd = xd[...].astype(f32) * gain[...]
    lq = to_lanes(jnp.sum(nq * nq, axis=1, keepdims=True))
    ld = to_lanes(jnp.sum(nd * nd, axis=1, keepdims=True))
    e0s[...] = jnp.broadcast_to(gain[...], (8, FEATS))
    e0s[0:1, 0:ROWS] = lq[0:1]
    e0s[1:2, 0:ROWS] = ld[0:1]
    pl.semaphore_wait(barrier, TP + 7)

    def xcopy(i):
        src, dst = (xq, pq) if i < NCH else (xd, pd)
        part = pl.ds((i % NCH) * CHUNK, CHUNK)
        return copy(src.at[part], dst.at[part], x_s.at[i], x_r.at[i], partner)

    def begun(c):
        c.start()
        sent.append(c.wait_send)

    def exchange(src, recv, ss, rs, size, me, dev):
        @pl.loop(1, size)
        def _(k):
            copy(src, recv.at[me], ss.at[k], rs.at[me], dev((me + k) % size)).start()

        @sent.append
        def _():
            @pl.loop(1, size)
            def _(k):
                copy(src, recv.at[me], ss.at[k], rs.at[me], dev((me + k) % size)).wait_send()

    def finish(src, recv, ss, rs, size, me, dev):
        recv[me] = src[...]

        @pl.loop(1, size)
        def _(k):
            s = (me + k) % size
            copy(src, recv.at[s], ss.at[k], rs.at[s], dev(s)).wait_recv()

    by_tensor = lambda s: (d, s)
    by_hz = lambda s: (s * 2 + core, t)

    def total(recv, size):
        acc = recv[0]
        for s in range(1, size):
            acc = acc + recv[s]
        return acc

    e0 = (e0s, e0r, e0_s, e0_r, TP, t, by_tensor)
    begun(xcopy(0))
    exchange(*e0)
    for i in range(1, 2 * NCH):
        begun(xcopy(i))

    mine = begin(d4, t)
    here = place(hz, core, t)
    extra = d4 == third

    def pack(a, k):
        own, part, base = (xq, pq, ROWS) if a == 0 else (xd, pd, 0)
        xcopy(a * NCH + k).wait_recv()
        rs = pl.ds(k * CHUNK, CHUNK)
        eo = own[rs].astype(f32)
        ep = part[rs].astype(f32)
        left = jnp.where(low == 0, eo, ep)
        right = jnp.where(low == 0, ep, eo)
        raw[pl.ds(base + k * CHUNK, CHUNK), lanes(y)] = jnp.concatenate(
            [left, right], axis=1
        ).astype(bf16)

    def normalise(a, k, block):
        inverse, base = (invq, ROWS) if a == 0 else (invd, 0)
        for part in range(2):
            rs = k * CHUNK + part * HALF
            scale = inverse[pl.ds(rs, HALF), 0:1]
            at = pl.ds(base + rs, HALF)
            cs = lanes(block)
            emb[at, cs] = (raw[at, cs].astype(f32) * gfull[:, cs] * scale).astype(bf16)

    def ycopy(a, k, kind):
        base = (ROWS if a == 0 else 0) + k * CHUNK
        i = (a * NCH + k) * 4 + kind
        if kind < 2:
            at, dev, block = pl.ds(base, CHUNK), (up, down)[kind], y
        elif kind == 2:
            at, dev, block = pl.ds(base, HALF), up, (y + 3) % 4
        else:
            at, dev, block = pl.ds(base + HALF, HALF), down, (y + 1) % 4
        ref = raw.at[at, lanes(block)]
        return copy(ref, ref, y_s.at[i], y_r.at[i], dev)

    def yrecv(a, k, kind):
        base = (ROWS if a == 0 else 0) + k * CHUNK
        i = (a * NCH + k) * 4 + kind
        at = pl.ds(base, CHUNK) if kind < 2 else pl.ds(base + (kind - 2) * HALF, HALF)
        block = ((y + 3) % 4, (y + 1) % 4, (y + 2) % 4, (y + 2) % 4)[kind]
        ref = raw.at[at, lanes(block)]
        copy(ref, ref, y_s.at[i], y_r.at[i], up).wait_recv()

    def source(s):
        return (xh + s // 4) % 2 * 4 + (zc + 4 - s % 4) % 4

    def gives(s, core_s):
        return (xh + s // 4) % 2 * 2 + core_s == third

    def device(s):
        return ((xh + s // 4) % 2 * 8 + (zc + s % 4) % 4 * 2 + core, t)

    def spot(i, s, core_s, n):
        block = (y + (0, 3, 1, 2)[i]) % 4
        return qi.at[rows_at(place(source(s), core_s, t), n), lanes(block)]

    def own_rows(i, n):
        block = (y + (0, 3, 1, 2)[i]) % 4
        return emb.at[pl.ds(pl.multiple_of(ROWS + mine * TILE, TILE), n), lanes(block)]

    def give_own(i, slot, dev):
        def c(n):
            return copy(
                own_rows(i, n), spot(i, 0, core, n), a_s.at[i * 16 + slot], a_r.at[i * 16 + slot], dev
            )

        sized(extra, lambda n: c(n).start())
        sent.append(lambda: sized(extra, lambda n: c(n).wait_send()))

    def pass_on(i, s, slot, dev):
        def c(n):
            ref = spot(i, s, core, n)
            return copy(ref, ref, a_s.at[i * 16 + slot], a_r.at[i * 16 + slot], dev)

        sized(gives(s, core), lambda n: c(n).start())
        sent.append(lambda: sized(gives(s, core), lambda n: c(n).wait_send()))

    def agot(i, s):
        def c(n):
            ref = spot(i, s, core, n)
            copy(ref, ref, a_s.at[i * 16 + s], a_r.at[i * 16 + s], sibling).wait_recv()

        sized(gives(s, core), c)

    def alocal(i, n):
        return pltpu.make_async_copy(own_rows(i, n), spot(i, 0, core, n), loc.at[i])

    def astart(i):
        for s in (1, 3, 2, 4) if i < 3 else (4, 1, 3, 2, 5, 7, 6):
            give_own(i, s, device(s))
        give_own(i, 8, sibling)
        sized(extra, lambda n: alocal(i, n).start())

    def amid(i):
        agot(i, 4)
        if i < 3:
            for s in (1, 3, 2):
                pass_on(i, 4, 4 + s, device(s))
        pass_on(i, 4, 12, sibling)
        for s in (1, 3, 2):
            agot(i, s)
            pass_on(i, s, 8 + s, sibling)

    def alast(i):
        for s in (5, 7, 6):
            agot(i, s)
            pass_on(i, s, 8 + s, sibling)

    def afinish(i):
        sized(extra, lambda n: alocal(i, n).wait())

        @pl.loop(0, 8)
        def _(s):
            def c(n):
                ref = spot(i, s, 1 - core, n)
                copy(ref, ref, a_s.at[i * 16], a_r.at[i * 16 + 8 + s], sibling).wait_recv()

            sized(gives(s, 1 - core), c)

    for k in range(NCH):
        pack(0, k)
        begun(ycopy(0, k, 0))
        begun(ycopy(0, k, 1))
    finish(*e0)
    inv = lax.rsqrt(total(e0r, TP)[:, 0:ROWS] + eps_len)
    invq[0:ROWS] = to_rows(inv[0:1])
    invd[...] = to_rows(inv[1:2])
    for b in range(4):
        gfull[:, b * WIDE : (b + 1) * WIDE] = jnp.concatenate(
            [e0r[b, 2:3], e0r[4 + b, 2:3]], axis=1
        )
    for k in range(NCH):
        normalise(0, k, y)
    astart(0)
    ep = (pos, epr, ep_s, ep_r, 8, hz, by_hz)
    exchange(*ep)
    for k in range(NCH):
        yrecv(0, k, 0)
        begun(ycopy(0, k, 2))
        yrecv(0, k, 1)
        begun(ycopy(0, k, 3))
        pack(1, k)
        begun(ycopy(1, k, 0))
        begun(ycopy(1, k, 1))
        normalise(0, k, (y + 3) % 4)
        normalise(0, k, (y + 1) % 4)
    astart(1)
    astart(2)
    amid(0)
    for k in range(NCH):
        normalise(1, k, y)
        yrecv(0, k, 2)
        yrecv(0, k, 3)
        normalise(0, k, (y + 2) % 4)
    astart(3)
    alast(0)
    amid(1)
    amid(2)
    for k in range(NCH):
        yrecv(1, k, 0)
        begun(ycopy(1, k, 2))
        yrecv(1, k, 1)
        begun(ycopy(1, k, 3))
    alast(1)
    alast(2)
    for k in range(NCH):
        normalise(1, k, (y + 3) % 4)
        normalise(1, k, (y + 1) % 4)
    amid(3)
    alast(3)
    for i in range(4):
        afinish(i)

    lane_p = lax.broadcasted_iota(jnp.int32, (1, TAKE), 1)
    tile_p = lane_p // TILE
    w_p = tile_p % 9
    q_p = jnp.where(
        w_p < 2 * third, w_p // 2, jnp.where(w_p <= 2 * third + 2, third, (w_p - 1) // 2)
    )
    off_p = w_p - 2 * q_p - jnp.where(q_p > third, 1, 0)
    dev_p = (q_p // 2) * 8 + (tile_p // 9) * 2 + q_p % 2
    row_p = dev_p * ROWS + (begin(q_p, t) + off_p) * TILE + lane_p % TILE
    finish(*ep)
    epc = copy(epr.at[pl.ds(0, 8)], epr.at[pl.ds(8, 8)], c_s.at[0], c_r.at[0], sibling)
    begun(epc)

    stat[0:1] = jnp.full((1, TAKE), masked, f32)
    stat[1:8] = jnp.zeros((7, TAKE), f32)

    def product(rows, cs):
        return lax.dot_general(
            emb[rows, cs], qi[:, cs], (((1,), (1,)), ((), ())), preferred_element_type=f32
        )

    def statistics(s):
        old = stat[0:1]
        new = jnp.maximum(old, jnp.max(s, axis=0, keepdims=True))
        stat[0:1] = new
        stat[1:2] = stat[1:2] * jnp.exp(old - new) + jnp.sum(
            jnp.exp(s - new), axis=0, keepdims=True
        )

    own_j = d * ROWS + lax.broadcasted_iota(jnp.int32, (ROWS, TAKE), 0)
    logits[ROWS:] = product(pl.ds(ROWS, ROWS), slice(None))
    logits[ROWS:] = jnp.where(own_j == row_p, masked, logits[ROWS:] * inv_temp)
    statistics(logits[ROWS:])
    logits[0:ROWS] = product(pl.ds(0, ROWS), lanes(y))
    for b in (1, 3):
        logits[0:ROWS] = logits[0:ROWS] + product(pl.ds(0, ROWS), lanes((y + b) % 4))

    epc.wait_recv()
    local_p = (begin(q_p, t) + off_p) * TILE + lane_p % TILE
    lane_of = lax.broadcasted_iota(jnp.int32, (128, TAKE), 0)
    spread = jnp.where(lane_of == local_p % 128, 1.0, 0.0).astype(bf16)
    found = jnp.dot(
        epr[...].reshape(DP * 8, 128).astype(bf16), spread, preferred_element_type=f32
    )
    slot_p = jnp.where(dev_p % 2 == core, dev_p // 2, 8 + dev_p // 2) * 8 + local_p // 128
    high = jnp.sum(jnp.where(lane_of == slot_p, found, 0.0), axis=0, keepdims=True)
    rest = jnp.sum(jnp.where(lane_of == slot_p + 3, found, 0.0), axis=0, keepdims=True)
    pos_p = (high * 128.0 + rest).astype(jnp.int32)

    for k in range(NCH):
        yrecv(1, k, 2)
        yrecv(1, k, 3)
        normalise(1, k, (y + 2) % 4)
    logits[0:ROWS] = (logits[0:ROWS] + product(pl.ds(0, ROWS), lanes((y + 2) % 4))) * inv_temp
    stat[2:3] = jnp.sum(jnp.where(own_j == pos_p, logits[0:ROWS], 0.0), axis=0, keepdims=True)
    statistics(logits[0:ROWS])

    sub_t = sub8(TAKE)
    c1 = copy(stat, cr1, c_s.at[1], c_r.at[1], sibling)
    begun(c1)
    c1.wait_recv()
    top, tot, posit = stat[0:1], stat[1:2], stat[2:3]
    top_o = cr1[0:1]
    top_c = jnp.maximum(top, top_o)
    tot = tot * jnp.exp(top - top_c) + cr1[1:2] * jnp.exp(top_o - top_c)
    e1s[...] = jnp.where(sub_t == 0, top_c, jnp.where(sub_t == 1, tot, posit + cr1[2:3]))
    e1 = (e1s, e1r, e1_s, e1_r, 8, hz, by_hz)
    exchange(*e1)
    pick = jnp.where(own_j == row_p, 1.0, 0.0).astype(bf16)
    finish(*e1)
    all_top = e1r[0, 0:1]
    for s in range(1, 8):
        all_top = jnp.maximum(all_top, e1r[s, 0:1])
    all_tot = jnp.zeros_like(all_top)
    all_pos = jnp.zeros_like(all_top)
    for s in range(8):
        all_tot = all_tot + e1r[s, 1:2] * jnp.exp(e1r[s, 0:1] - all_top)
        all_pos = all_pos + e1r[s, 2:3]
    lse = all_top + jnp.log(all_tot)
    loss_part = jnp.sum(lse - all_pos, axis=1, keepdims=True)

    lse1 = lse.astype(bf16).astype(f32)
    lse2 = (lse - lse1).astype(bf16).astype(f32)
    split = jnp.where(
        sub_t == 0, lse1, jnp.where(sub_t == 1, lse2, jnp.where(sub_t == 2, lse - lse1 - lse2, 0.0))
    )
    lse_own = jnp.sum(
        lax.dot_general(
            split.astype(bf16), pick, (((1,), (1,)), ((), ())), preferred_element_type=f32
        ),
        axis=0, keepdims=True,
    )
    e2s[...] = jnp.where(sub8(ROWS) == 0, lse_own, loss_part)
    e2 = (e2s, e2r, e2_s, e2_r, TP, t, by_tensor)
    exchange(*e2)
    wd = (jnp.exp(logits[0:ROWS] - lse) - (own_j == pos_p).astype(f32)) * (1.0 / PAIRS)
    wts[0:ROWS] = wd.astype(bf16)

    def part_d(block):
        return lax.dot_general(
            wts[0:ROWS], qi[:, lanes(block)], (((1,), (0,)), ((), ())),
            preferred_element_type=f32,
        ) * inv_temp

    MID = ROWS // 2
    front, rear = pl.ds(0, MID), pl.ds(MID, MID)
    gc = [
        copy(pd2.at[front], halfs.at[0], g_s.at[0], g_r.at[0], up),
        copy(pd2.at[rear], halfs.at[1], g_s.at[1], g_r.at[1], down),
        copy(pd1.at[rear], r1.at[rear], g_s.at[2], g_r.at[2], up),
        copy(pdm.at[front], r2.at[front], g_s.at[3], g_r.at[3], down),
        copy(pd1.at[front], r1.at[front], g_s.at[4], g_r.at[4], up),
        copy(pdm.at[rear], r2.at[rear], g_s.at[5], g_r.at[5], down),
        copy(xsend, xrecv, g_s.at[6], g_r.at[6], partner),
    ]
    pd2[...] = part_d((y + 2) % 4).astype(bf16)
    begun(gc[0])
    begun(gc[1])
    gd[...] = part_d((y + 1) % 4)
    pd1[rear] = gd[rear].astype(bf16)
    begun(gc[2])
    acc1[...] = gd[front]
    gd[...] = part_d((y + 3) % 4)
    pdm[front] = gd[front].astype(bf16)
    begun(gc[3])
    acc2[...] = gd[rear]
    gd[...] = part_d(y)

    finish(*e2)
    sums = total(e2r, TP)
    oloss[...] = sums[1:2, 0:1] * (1.0 / PAIRS)
    lse_j = to_rows(sums[0:1])[:, 0:1]
    wq = (jnp.exp(logits[ROWS:] - lse) * (1.0 / PAIRS)).astype(bf16).astype(f32)
    wt = (jnp.exp(logits[ROWS:] - lse_j) * (1.0 / PAIRS)).astype(bf16).astype(f32)
    wts[ROWS:] = (wq + wt).astype(bf16)
    wtt[...] = jnp.transpose(wts[...])

    def target(s):
        return (xh + s // 4) % 2 * 4 + (zc + s % 4) % 4

    def cols(f):
        return lanes((y + 1 + f) % 4)

    def bcopy(f, k, n):
        at = rows_at(place(k, 1 - core, t), n)
        return copy(
            partq.at[at, cols(f)], sibr.at[k, pl.ds(0, n), cols(f)],
            b_s.at[f * 8 + k], b_r.at[f * 8 + k], sibling,
        )

    def three(k, core_s):
        return (k // 4) * 2 + core_s == third

    def part_q(f):
        partq[0:TAKE, cols(f)] = (
            jnp.dot(
                wtt[...], emb[0 : 2 * ROWS, cols(f)],
                preferred_element_type=f32,
            ) * inv_temp
        ).astype(bf16)

        @pl.loop(0, 8)
        def _(k):
            sized(three(k, 1 - core), lambda n: bcopy(f, k, n).start())

        @sent.append
        def _():
            @pl.loop(0, 8)
            def _(k):
                sized(three(k, 1 - core), lambda n: bcopy(f, k, n).wait_send())

    N3 = 3 * TILE

    def both(f, s):
        k = target(s)
        sized(three(k, core), lambda n: bcopy(f, k, n).wait_recv())
        cs = cols(f)
        return partq[rows_at(place(k, core, t), N3), cs].astype(f32) + sibr[k, :, cs].astype(f32)

    FLOW = ((2, zup), (6, zdown), (5, zup), (3, zdown), (1, zup), (7, zdown), (4, across))

    def ucopy(f, i, n):
        cs = cols(f)
        return copy(
            sendq.at[i, pl.ds(0, n), cs], recvq.at[i, pl.ds(0, n), cs],
            u_s.at[f * 8 + i], u_r.at[f * 8 + i], FLOW[i][1],
        )

    def usend(f, i, value):
        sendq[i, :, cols(f)] = value.astype(bf16)
        far = three(target(FLOW[i][0]), core)
        sized(far, lambda n: ucopy(f, i, n).start())
        sent.append(lambda: sized(far, lambda n: ucopy(f, i, n).wait_send()))

    def uwait(f, i, s):
        sized(three(target(s), core), lambda n: ucopy(f, i, n).wait_recv())
        return recvq[i, :, cols(f)].astype(f32)

    def q_far(f):
        usend(f, 0, both(f, 2))
        usend(f, 1, both(f, 6))
        usend(f, 2, both(f, 5))
        usend(f, 3, both(f, 3))

    def q_near(f):
        usend(f, 4, both(f, 1) + uwait(f, 0, 1))
        usend(f, 5, both(f, 7) + uwait(f, 1, 7))

    def q_across(f):
        usend(f, 6, both(f, 4) + uwait(f, 2, 4) + uwait(f, 5, 4))

    def tcopy(f, far, n):
        to = (y + 1 + f) % 4 + 4 * ((low + far) % 2)
        return copy(
            asend.at[to, pl.ds(0, n)], arecv.at[rows_at(mine, n)],
            t_s.at[f * 2 + far], t_r.at[f * 2 + far], (d, to),
        )

    def trecv(f, far):
        s = (y + 3 - f) % 4 + 4 * ((low + far) % 2)
        at = lambda n: arecv.at[rows_at(begin(d4, s), n)]
        sized(
            d4 == s // 2,
            lambda n: copy(at(n), at(n), t_s.at[0], t_r.at[f * 2 + far], (d, s)).wait_recv(),
        )

    def direct(f, s, n):
        cs = cols(f)
        return copy(
            sendq.at[s - 1, pl.ds(0, n), cs], recvq.at[s - 1, pl.ds(0, n), cs],
            u_s.at[f * 8 + s - 1], u_r.at[f * 8 + s - 1], device(s),
        )

    def q_direct(f):
        for s in (5, 7, 6, 4, 2, 1, 3):
            sendq[s - 1, :, cols(f)] = both(f, s).astype(bf16)
            far = three(target(s), core)
            sized(far, lambda n: direct(f, s, n).start())
            sent.append(
                lambda s=s, far=far: sized(far, lambda n: direct(f, s, n).wait_send())
            )

    def q_own(f):
        if f < 3:
            g = both(f, 0) + uwait(f, 3, 0) + uwait(f, 4, 0) + uwait(f, 6, 0)
        else:
            g = both(f, 0)
            for s in range(1, 8):
                sized(extra, lambda n: direct(f, s, n).wait_recv())
                g = g + recvq[s - 1, :, cols(f)].astype(f32)
        fb = (y + 1 + f) % 4
        asend[fb] = g[:, :FEATS].astype(bf16)
        asend[4 + fb] = g[:, FEATS:].astype(bf16)
        for far in range(2):
            if f < 3 or far == 1:
                sized(extra, lambda n: tcopy(f, far, n).start())
                sent.append(
                    lambda far=far: sized(extra, lambda n: tcopy(f, far, n).wait_send())
                )
        eq = emb[pl.ds(pl.multiple_of(ROWS + mine * TILE, TILE), N3), lanes(fb)].astype(f32)
        return jnp.sum(g * eq, axis=1, keepdims=True)

    part_q(0)
    gc[0].wait_recv()
    pd1[front] = (acc1[...] + halfs[0].astype(f32)).astype(bf16)
    begun(gc[4])
    gc[1].wait_recv()
    pdm[rear] = (acc2[...] + halfs[1].astype(f32)).astype(bf16)
    begun(gc[5])
    part_q(1)
    q_far(0)
    part_q(2)
    q_far(1)
    part_q(3)
    q_near(0)
    q_far(2)
    q_near(1)
    q_direct(3)
    q_across(0)
    q_near(2)
    for i in range(2, 6):
        gc[i].wait_recv()
    gd[...] = gd[...] + r1[...].astype(f32) + r2[...].astype(f32)
    xsend[...] = jnp.where(low == 0, gd[:, FEATS:], gd[:, :FEATS]).astype(bf16)
    begun(gc[6])
    q_across(1)
    dots = q_own(0)
    q_across(2)
    dots = dots + q_own(1)

    gc[6].wait_recv()
    gd[:, 0:FEATS] = jnp.where(low == 0, gd[:, :FEATS], gd[:, FEATS:]) + xrecv[...].astype(f32)
    fd = jnp.sum(gd[:, 0:FEATS] * (xd[...].astype(f32) * gain[...]), axis=1, keepdims=True)
    e3s[...] = to_lanes(fd)
    e3 = (e3s, e3r, e3_s, e3_r, TP, t, by_tensor)
    exchange(*e3)
    dots = dots + q_own(2)

    dots = dots + q_own(3)
    dsend[...] = jnp.broadcast_to(dots, (N3, 128))

    def vcopy(k, n):
        to = (t + k) % TP
        return copy(
            dsend.at[pl.ds(0, n)], drecv.at[rows_at(mine, n)], v_s.at[k], v_r.at[k], (d, to)
        )

    def vrecv(k, n):
        s = (t + TP - k) % TP
        at = drecv.at[rows_at(begin(d4, s), n)]
        return copy(at, at, v_s.at[k], v_r.at[k], (d, s))

    @pl.loop(1, TP)
    def _(k):
        sized(extra, lambda n: vcopy(k, n).start())

    @sent.append
    def _():
        @pl.loop(1, TP)
        def _(k):
            sized(extra, lambda n: vcopy(k, n).wait_send())

    def tlocal(n):
        arecv[rows_at(mine, n)] = asend[t, pl.ds(0, n)]
        drecv[rows_at(mine, n)] = dsend[pl.ds(0, n)]

    sized(extra, tlocal)

    finish(*e3)
    col = to_rows(total(e3r, TP)[0:1])[:, 0:1]
    iv = invd[:, 0:1]
    h = xd[...].astype(f32)
    gx = iv * gd[:, 0:FEATS] - h * gain[...] * (iv * iv * iv * col)
    outd[...] = (gx * gain[...]).astype(bf16)
    outs = [pltpu.make_async_copy(outd, od, io.at[0]), pltpu.make_async_copy(outq, oq, io.at[1])]
    outs[0].start()
    gg = jnp.sum(gx * h, axis=0, keepdims=True)

    for f in range(4):
        for far in range(2):
            if f < 3 or far == 1:
                trecv(f, far)

    @pl.loop(1, TP)
    def _(k):
        sized(d4 == ((t + TP - k) % TP) // 2, lambda n: vrecv(k, n).wait_recv())

    h = xq[...].astype(f32)
    iv = invq[0:ROWS, 0:1]
    gx = iv * arecv[...].astype(f32) - h * gain[...] * (iv * iv * drecv[:, 0:1])
    gg = gg + jnp.sum(gx * h, axis=0, keepdims=True)
    cs4[...] = jnp.broadcast_to(gg, (8, FEATS))
    c4 = copy(cs4, cr4, c_s.at[2], c_r.at[2], sibling)
    begun(c4)
    outq[...] = (gx * gain[...]).astype(bf16)
    outs[1].start()
    c4.wait_recv()
    e4s[...] = cs4[...] + cr4[...]
    e4 = (e4s, e4r, e4_s, e4_r, 8, hz, by_hz)
    exchange(*e4)
    finish(*e4)
    ogain[...] = total(e4r, 8)[0:1]
    for c in outs:
        c.wait()

    for wait in sent:
        wait()


def shards(query_states, doc_states, gain, positives):
    vm = pl.BlockSpec(memory_space=pltpu.VMEM)
    hbm = pl.BlockSpec(memory_space=pl.ANY)
    S = pltpu.VMEM
    dma = lambda n: pltpu.SemaphoreType.DMA((n,))
    pair = lambda n: [dma(n), dma(n)]
    scratch = [
        S((ROWS, FEATS), bf16), S((ROWS, FEATS), bf16),
        S((ROWS, FEATS), bf16), S((ROWS, FEATS), bf16), S((1, FULL), f32),
        S((2 * ROWS, FULL), bf16), S((2 * ROWS + TILE, FULL), bf16), S((TAKE, FULL), bf16),
        S((ROWS + TILE, 128), f32), S((ROWS, 128), f32),
        S((2 * ROWS, TAKE), f32), S((8, TAKE), f32), S((2 * ROWS, TAKE), bf16), S((TAKE, 2 * ROWS), bf16),
        S((8, FEATS), f32), S((TP, 8, FEATS), f32),
        S((8, TAKE), f32), S((8, TAKE), f32), S((8, 8, TAKE), f32),
        S((8, ROWS), f32), S((TP, 8, ROWS), f32),
        S((8, ROWS), f32), S((TP, 8, ROWS), f32),
        S((8, FEATS), f32), S((8, FEATS), f32), S((8, FEATS), f32), S((8, 8, FEATS), f32),
        S((DP, 8, 128), f32),
        S((TAKE + TILE, FULL), bf16), S((8, 3 * TILE, FULL), bf16),
        S((7, 3 * TILE, FULL), bf16), S((7, 3 * TILE, FULL), bf16),
        S((ROWS // 2, WIDE), f32), S((ROWS // 2, WIDE), f32),
        S((ROWS, WIDE), bf16), S((ROWS, WIDE), bf16), S((ROWS, WIDE), bf16),
        S((2, ROWS // 2, WIDE), bf16), S((ROWS, WIDE), bf16), S((ROWS, WIDE), bf16),
        S((ROWS, WIDE), f32), S((ROWS, FEATS), bf16), S((ROWS, FEATS), bf16),
        S((TP, 3 * TILE, FEATS), bf16), S((ROWS, FEATS), bf16), S((3 * TILE, 128), f32), S((ROWS, 128), f32),
        S((ROWS, FEATS), bf16), S((ROWS, FEATS), bf16),
    ]
    sems = (
        pair(2 * NCH) + pair(TP) + pair(8) + pair(TP) + pair(TP) + pair(8) + pair(8)
        + pair(8 * NCH) + pair(64) + [dma(4)] + pair(32) + pair(32) + pair(7) + pair(TP) + pair(TP)
        + pair(3) + [dma(2)]
    )
    padded = jnp.pad(positives, (0, 3 * 128 - ROWS)).reshape(3, 128)
    parts = jnp.concatenate([padded // 128, padded % 128, jnp.zeros((2, 128), jnp.int32)])
    gq, gdoc, ggain, loss = pl.pallas_call(
        step,
        name="infonce_step",
        out_shape=(
            jax.ShapeDtypeStruct((ROWS, FEATS), bf16),
            jax.ShapeDtypeStruct((ROWS, FEATS), bf16),
            jax.ShapeDtypeStruct((1, FEATS), f32),
            jax.ShapeDtypeStruct((1, 1), f32),
        ),
        in_specs=[hbm, hbm, vm, vm],
        out_specs=(hbm, hbm, vm, vm),
        scratch_shapes=scratch + sems,
        compiler_params=pltpu.CompilerParams(
            collective_id=0, has_side_effects=True, vmem_limit_bytes=56 * 2**20
        ),
        cost_estimate=pl.CostEstimate(
            flops=7_000_000_000, bytes_accessed=3_000_000, transcendentals=1_000_000
        ),
    )(query_states, doc_states, gain[None, :], parts.astype(f32))
    return gq, gdoc, ggain[0], loss[0, 0]


def solution(mesh):
    return jax.shard_map(
        shards,
        mesh=mesh,
        in_specs=(P("dp", "tensor"), P("dp", "tensor"), P("tensor"), P("dp")),
        out_specs=(P("dp", "tensor"), P("dp", "tensor"), P("tensor"), P()),
        check_vma=False,
    )
```

```python
import functools

import jax
import jax.numpy as jnp
from jax import lax
from jax.experimental import pallas as pl
from jax.experimental.pallas import tpu as pltpu
from jax.sharding import PartitionSpec as P

eps_len = 1e-06
inv_temp = 100.0
masked = -1e30

MESH = pl.DeviceIdType.MESH
HIGH = lax.Precision.HIGHEST
f32 = jnp.float32
bf16 = jnp.bfloat16

DP = 16
TP = 8
ROWS = 288
FEATS = 448
WIDE = 2 * FEATS
FULL = TP * FEATS
PAIRS = DP * ROWS
TAKE = DP * ROWS // TP
TILE = 16
CHUNK = 96
NCH = ROWS // CHUNK
HALF = CHUNK // 2


def step(
    hq, hd, gain, pos,
    oq, od, ogain, oloss,
    xq, xd, pq, pd, gfull, raw, emb, qi, invq, invd, logits, stat, wts, wtt,
    e0s, e0r, cr1, e1s, e1r, e2s, e2r, e3s, e3r, cs4, cr4, e4s, e4r, epr, posv,
    partq, sibr, sendq, recvq, acc1, acc2, pd2, pd1, pdm, halfs, r1, r2, gd, xsend, xrecv,
    asend, arecv, dsend, drecv, outq, outd,
    x_s, x_r, e0_s, e0_r, e1_s, e1_r, e2_s, e2_r, e3_s, e3_r, e4_s, e4_r, ep_s, ep_r,
    y_s, y_r, a_s, a_r, loc, b_s, b_r, u_s, u_r, g_s, g_r, t_s, t_r, v_s, v_r, c_s, c_r, io,
):
    d = lax.axis_index("dp")
    t = lax.axis_index("tensor")
    hz = d // 2
    core = d % 2
    zc = hz % 4
    d4 = (hz // 4) * 2 + core
    low = t // 4
    y = t % 4
    xh = hz // 4
    sources = [pltpu.make_async_copy(hq, xq, io.at[0]), pltpu.make_async_copy(hd, xd, io.at[1])]
    for c in sources:
        c.start()
    third = t // 2
    sibling = (hz * 2 + (1 - core), t)
    partner = (d, (t + 4) % TP)
    up = (d, low * 4 + (y + 1) % 4)
    down = (d, low * 4 + (y + 3) % 4)
    zup = ((xh * 4 + (zc + 1) % 4) * 2 + core, t)
    zdown = ((xh * 4 + (zc + 3) % 4) * 2 + core, t)
    across = ((hz + 4) % 8 * 2 + core, t)

    sent = []

    def copy(src, dst, ss, rs, dev):
        return pltpu.make_async_remote_copy(
            src_ref=src, dst_ref=dst, send_sem=ss, recv_sem=rs, device_id=dev, device_id_type=MESH
        )

    def lanes(block):
        return pl.ds(pl.multiple_of(block * WIDE, 128), WIDE)

    def rows_at(tile, n):
        return pl.ds(pl.multiple_of(tile * TILE, TILE), n)

    def place(hz_s, core_s, tens):
        q = (hz_s // 4) * 2 + core_s
        e = tens // 2
        return (hz_s % 4) * 9 + 2 * q + jnp.where(q > e, 1, 0)

    def begin(q, tens):
        return 2 * tens + jnp.clip(tens - 2 * q, 0, 2)

    def sized(extra, fn):
        @pl.when(extra)
        def _():
            fn(3 * TILE)

        @pl.when(jnp.logical_not(extra))
        def _():
            fn(2 * TILE)

    barrier = pltpu.get_barrier_semaphore()

    @pl.loop(1, TP)
    def _(k):
        pl.semaphore_signal(barrier, inc=1, device_id=(d, (t + k) % TP), device_id_type=MESH)

    @pl.loop(1, 8)
    def _(k):
        pl.semaphore_signal(
            barrier, inc=1, device_id=((hz + k) % 8 * 2 + core, t), device_id_type=MESH
        )

    pl.semaphore_signal(barrier, inc=1, device_id=sibling, device_id_type=MESH)
    def to_lanes(col):
        return jnp.transpose(jnp.broadcast_to(col, (ROWS, 128)))[:8]

    def to_rows(vec):
        return jnp.transpose(jnp.broadcast_to(vec, (128, ROWS)))

    sub8 = lambda n: lax.broadcasted_iota(jnp.int32, (8, n), 0)

    posv[...] = jnp.zeros_like(posv)
    for seg in range(3):
        at = slice(128 * seg, min(128 * (seg + 1), ROWS))
        width = at.stop - at.start
        posv[seg : seg + 1, 0:width] = (pos[:, at] // 128).astype(f32)
        posv[3 + seg : 4 + seg, 0:width] = (pos[:, at] % 128).astype(f32)
    for c in sources:
        c.wait()
    nq = xq[...].astype(f32) * gain[...]
    nd = xd[...].astype(f32) * gain[...]
    lq = to_lanes(jnp.sum(nq * nq, axis=1, keepdims=True))
    ld = to_lanes(jnp.sum(nd * nd, axis=1, keepdims=True))
    e0s[...] = jnp.broadcast_to(gain[...], (8, FEATS))
    e0s[0:1, 0:ROWS] = lq[0:1]
    e0s[1:2, 0:ROWS] = ld[0:1]
    pl.semaphore_wait(barrier, TP + 7)

    def xcopy(i):
        src, dst = (xq, pq) if i < NCH else (xd, pd)
        part = pl.ds((i % NCH) * CHUNK, CHUNK)
        return copy(src.at[part], dst.at[part], x_s.at[i], x_r.at[i], partner)

    def begun(c):
        c.start()
        sent.append(c.wait_send)

    def exchange(src, recv, ss, rs, size, me, dev):
        @pl.loop(1, size)
        def _(k):
            copy(src, recv.at[me], ss.at[k], rs.at[me], dev((me + k) % size)).start()

        @sent.append
        def _():
            @pl.loop(1, size)
            def _(k):
                copy(src, recv.at[me], ss.at[k], rs.at[me], dev((me + k) % size)).wait_send()

    def finish(src, recv, ss, rs, size, me, dev):
        recv[me] = src[...]

        @pl.loop(1, size)
        def _(k):
            s = (me + k) % size
            copy(src, recv.at[s], ss.at[k], rs.at[s], dev(s)).wait_recv()

    by_tensor = lambda s: (d, s)
    by_hz = lambda s: (s * 2 + core, t)

    def total(recv, size):
        acc = recv[0]
        for s in range(1, size):
            acc = acc + recv[s]
        return acc

    e0 = (e0s, e0r, e0_s, e0_r, TP, t, by_tensor)
    begun(xcopy(0))
    exchange(*e0)
    for i in range(1, 2 * NCH):
        begun(xcopy(i))

    mine = begin(d4, t)
    here = place(hz, core, t)
    extra = d4 == third

    def pack(a, k):
        own, part, base = (xq, pq, ROWS) if a == 0 else (xd, pd, 0)
        xcopy(a * NCH + k).wait_recv()
        rs = pl.ds(k * CHUNK, CHUNK)
        eo = own[rs].astype(f32)
        ep = part[rs].astype(f32)
        left = jnp.where(low == 0, eo, ep)
        right = jnp.where(low == 0, ep, eo)
        raw[pl.ds(base + k * CHUNK, CHUNK), lanes(y)] = jnp.concatenate(
            [left, right], axis=1
        ).astype(bf16)

    def normalise(a, k, block):
        inverse, base = (invq, ROWS) if a == 0 else (invd, 0)
        for part in range(2):
            rs = k * CHUNK + part * HALF
            scale = inverse[pl.ds(rs, HALF), 0:1]
            at = pl.ds(base + rs, HALF)
            cs = lanes(block)
            emb[at, cs] = (raw[at, cs].astype(f32) * gfull[:, cs] * scale).astype(bf16)

    def ycopy(a, k, kind):
        base = (ROWS if a == 0 else 0) + k * CHUNK
        i = (a * NCH + k) * 4 + kind
        if kind < 2:
            at, dev, block = pl.ds(base, CHUNK), (up, down)[kind], y
        elif kind == 2:
            at, dev, block = pl.ds(base, HALF), up, (y + 3) % 4
        else:
            at, dev, block = pl.ds(base + HALF, HALF), down, (y + 1) % 4
        ref = raw.at[at, lanes(block)]
        return copy(ref, ref, y_s.at[i], y_r.at[i], dev)

    def yrecv(a, k, kind):
        base = (ROWS if a == 0 else 0) + k * CHUNK
        i = (a * NCH + k) * 4 + kind
        at = pl.ds(base, CHUNK) if kind < 2 else pl.ds(base + (kind - 2) * HALF, HALF)
        block = ((y + 3) % 4, (y + 1) % 4, (y + 2) % 4, (y + 2) % 4)[kind]
        ref = raw.at[at, lanes(block)]
        copy(ref, ref, y_s.at[i], y_r.at[i], up).wait_recv()

    def source(s):
        return (xh + s // 4) % 2 * 4 + (zc + 4 - s % 4) % 4

    def gives(s, core_s):
        return (xh + s // 4) % 2 * 2 + core_s == third

    def device(s):
        return ((xh + s // 4) % 2 * 8 + (zc + s % 4) % 4 * 2 + core, t)

    def spot(i, s, core_s, n):
        block = (y + (0, 3, 1, 2)[i]) % 4
        return qi.at[rows_at(place(source(s), core_s, t), n), lanes(block)]

    def own_rows(i, n):
        block = (y + (0, 3, 1, 2)[i]) % 4
        return emb.at[pl.ds(pl.multiple_of(ROWS + mine * TILE, TILE), n), lanes(block)]

    def give_own(i, slot, dev):
        def c(n):
            return copy(
                own_rows(i, n), spot(i, 0, core, n), a_s.at[i * 16 + slot], a_r.at[i * 16 + slot], dev
            )

        sized(extra, lambda n: c(n).start())
        sent.append(lambda: sized(extra, lambda n: c(n).wait_send()))

    def pass_on(i, s, slot, dev):
        def c(n):
            ref = spot(i, s, core, n)
            return copy(ref, ref, a_s.at[i * 16 + slot], a_r.at[i * 16 + slot], dev)

        sized(gives(s, core), lambda n: c(n).start())
        sent.append(lambda: sized(gives(s, core), lambda n: c(n).wait_send()))

    def agot(i, s):
        def c(n):
            ref = spot(i, s, core, n)
            copy(ref, ref, a_s.at[i * 16 + s], a_r.at[i * 16 + s], sibling).wait_recv()

        sized(gives(s, core), c)

    def alocal(i, n):
        return pltpu.make_async_copy(own_rows(i, n), spot(i, 0, core, n), loc.at[i])

    def astart(i):
        for s in (1, 3, 2, 4) if i < 3 else (4, 1, 3, 2, 5, 7, 6):
            give_own(i, s, device(s))
        give_own(i, 8, sibling)
        sized(extra, lambda n: alocal(i, n).start())

    def amid(i):
        agot(i, 4)
        if i < 3:
            for s in (1, 3, 2):
                pass_on(i, 4, 4 + s, device(s))
        pass_on(i, 4, 12, sibling)
        for s in (1, 3, 2):
            agot(i, s)
            pass_on(i, s, 8 + s, sibling)

    def alast(i):
        for s in (5, 7, 6):
            agot(i, s)
            pass_on(i, s, 8 + s, sibling)

    def afinish(i):
        sized(extra, lambda n: alocal(i, n).wait())

        @pl.loop(0, 8)
        def _(s):
            def c(n):
                ref = spot(i, s, 1 - core, n)
                copy(ref, ref, a_s.at[i * 16], a_r.at[i * 16 + 8 + s], sibling).wait_recv()

            sized(gives(s, 1 - core), c)

    for k in range(NCH):
        pack(0, k)
        begun(ycopy(0, k, 0))
        begun(ycopy(0, k, 1))
    finish(*e0)
    inv = lax.rsqrt(total(e0r, TP)[:, 0:ROWS] + eps_len)
    invq[0:ROWS] = to_rows(inv[0:1])
    invd[...] = to_rows(inv[1:2])
    for b in range(4):
        gfull[:, b * WIDE : (b + 1) * WIDE] = jnp.concatenate(
            [e0r[b, 2:3], e0r[4 + b, 2:3]], axis=1
        )
    for k in range(NCH):
        normalise(0, k, y)
    astart(0)
    ep = (posv, epr, ep_s, ep_r, 8, hz, by_hz)
    exchange(*ep)
    for k in range(NCH):
        yrecv(0, k, 0)
        begun(ycopy(0, k, 2))
        yrecv(0, k, 1)
        begun(ycopy(0, k, 3))
    for k in range(NCH):
        pack(1, k)
        begun(ycopy(1, k, 0))
        begun(ycopy(1, k, 1))
    for k in range(NCH):
        normalise(0, k, (y + 3) % 4)
        normalise(0, k, (y + 1) % 4)
    astart(1)
    astart(2)
    amid(0)
    for k in range(NCH):
        yrecv(0, k, 2)
        yrecv(0, k, 3)
        normalise(0, k, (y + 2) % 4)
    astart(3)
    for k in range(NCH):
        normalise(1, k, y)
    alast(0)
    amid(1)
    amid(2)

    def docs_on(k):
        yrecv(1, k, 0)
        begun(ycopy(1, k, 2))
        yrecv(1, k, 1)
        begun(ycopy(1, k, 3))

    docs_on(0)
    alast(1)
    docs_on(1)
    alast(2)
    docs_on(2)
    for k in range(NCH):
        normalise(1, k, (y + 3) % 4)
        normalise(1, k, (y + 1) % 4)
    amid(3)
    alast(3)
    for i in range(4):
        afinish(i)

    lane_p = lax.broadcasted_iota(jnp.int32, (1, TAKE), 1)
    tile_p = lane_p // TILE
    w_p = tile_p % 9
    q_p = jnp.where(
        w_p < 2 * third, w_p // 2, jnp.where(w_p <= 2 * third + 2, third, (w_p - 1) // 2)
    )
    off_p = w_p - 2 * q_p - jnp.where(q_p > third, 1, 0)
    dev_p = (q_p // 2) * 8 + (tile_p // 9) * 2 + q_p % 2
    row_p = dev_p * ROWS + (begin(q_p, t) + off_p) * TILE + lane_p % TILE
    finish(*ep)
    epc = copy(epr.at[pl.ds(0, 8)], epr.at[pl.ds(8, 8)], c_s.at[0], c_r.at[0], sibling)
    begun(epc)

    stat[0:1] = jnp.full((1, TAKE), masked, f32)
    stat[1:8] = jnp.zeros((7, TAKE), f32)

    def product(rows, cs):
        return lax.dot_general(
            emb[rows, cs], qi[:, cs], (((1,), (1,)), ((), ())), preferred_element_type=f32
        )

    def statistics(s):
        old = stat[0:1]
        new = jnp.maximum(old, jnp.max(s, axis=0, keepdims=True))
        stat[0:1] = new
        stat[1:2] = stat[1:2] * jnp.exp(old - new) + jnp.sum(
            jnp.exp(s - new), axis=0, keepdims=True
        )

    own_j = d * ROWS + lax.broadcasted_iota(jnp.int32, (ROWS, TAKE), 0)
    logits[ROWS:] = product(pl.ds(ROWS, ROWS), slice(None))
    logits[ROWS:] = jnp.where(own_j == row_p, masked, logits[ROWS:] * inv_temp)
    statistics(logits[ROWS:])
    logits[0:ROWS] = product(pl.ds(0, ROWS), lanes(y))
    for b in (1, 3):
        logits[0:ROWS] = logits[0:ROWS] + product(pl.ds(0, ROWS), lanes((y + b) % 4))

    epc.wait_recv()
    local_p = (begin(q_p, t) + off_p) * TILE + lane_p % TILE
    lane_of = lax.broadcasted_iota(jnp.int32, (128, TAKE), 0)
    spread = jnp.where(lane_of == local_p % 128, 1.0, 0.0).astype(bf16)
    found = jnp.dot(
        epr[...].reshape(DP * 8, 128).astype(bf16), spread, preferred_element_type=f32
    )
    slot_p = jnp.where(dev_p % 2 == core, dev_p // 2, 8 + dev_p // 2) * 8 + local_p // 128
    high = jnp.sum(jnp.where(lane_of == slot_p, found, 0.0), axis=0, keepdims=True)
    rest = jnp.sum(jnp.where(lane_of == slot_p + 3, found, 0.0), axis=0, keepdims=True)
    pos_p = (high * 128.0 + rest).astype(jnp.int32)

    for k in range(NCH):
        yrecv(1, k, 2)
        yrecv(1, k, 3)
        normalise(1, k, (y + 2) % 4)
    logits[0:ROWS] = (logits[0:ROWS] + product(pl.ds(0, ROWS), lanes((y + 2) % 4))) * inv_temp
    stat[2:3] = jnp.sum(jnp.where(own_j == pos_p, logits[0:ROWS], 0.0), axis=0, keepdims=True)
    statistics(logits[0:ROWS])

    sub_t = sub8(TAKE)
    c1 = copy(stat, cr1, c_s.at[1], c_r.at[1], sibling)
    begun(c1)
    c1.wait_recv()
    top, tot, posit = stat[0:1], stat[1:2], stat[2:3]
    top_o = cr1[0:1]
    top_c = jnp.maximum(top, top_o)
    tot = tot * jnp.exp(top - top_c) + cr1[1:2] * jnp.exp(top_o - top_c)
    e1s[...] = jnp.where(sub_t == 0, top_c, jnp.where(sub_t == 1, tot, posit + cr1[2:3]))
    e1 = (e1s, e1r, e1_s, e1_r, 8, hz, by_hz)
    exchange(*e1)
    pick = jnp.where(own_j == row_p, 1.0, 0.0).astype(bf16)
    finish(*e1)
    all_top = e1r[0, 0:1]
    for s in range(1, 8):
        all_top = jnp.maximum(all_top, e1r[s, 0:1])
    all_tot = jnp.zeros_like(all_top)
    all_pos = jnp.zeros_like(all_top)
    for s in range(8):
        all_tot = all_tot + e1r[s, 1:2] * jnp.exp(e1r[s, 0:1] - all_top)
        all_pos = all_pos + e1r[s, 2:3]
    lse = all_top + jnp.log(all_tot)
    loss_part = jnp.sum(lse - all_pos, axis=1, keepdims=True)

    lse1 = lse.astype(bf16).astype(f32)
    lse2 = (lse - lse1).astype(bf16).astype(f32)
    split = jnp.where(
        sub_t == 0, lse1, jnp.where(sub_t == 1, lse2, jnp.where(sub_t == 2, lse - lse1 - lse2, 0.0))
    )
    lse_own = jnp.sum(
        lax.dot_general(
            split.astype(bf16), pick, (((1,), (1,)), ((), ())), preferred_element_type=f32
        ),
        axis=0, keepdims=True,
    )
    e2s[...] = jnp.where(sub8(ROWS) == 0, lse_own, loss_part)
    e2 = (e2s, e2r, e2_s, e2_r, TP, t, by_tensor)
    exchange(*e2)
    wd = (jnp.exp(logits[0:ROWS] - lse) - (own_j == pos_p).astype(f32)) * (1.0 / PAIRS)
    wts[0:ROWS] = wd.astype(bf16)

    def part_d(block):
        return lax.dot_general(
            wts[0:ROWS], qi[:, lanes(block)], (((1,), (0,)), ((), ())),
            preferred_element_type=f32,
        ) * inv_temp

    MID = ROWS // 2
    front, rear = pl.ds(0, MID), pl.ds(MID, MID)
    gc = [
        copy(pd2.at[front], halfs.at[0], g_s.at[0], g_r.at[0], up),
        copy(pd2.at[rear], halfs.at[1], g_s.at[1], g_r.at[1], down),
        copy(pd1.at[rear], r1.at[rear], g_s.at[2], g_r.at[2], up),
        copy(pdm.at[front], r2.at[front], g_s.at[3], g_r.at[3], down),
        copy(pd1.at[front], r1.at[front], g_s.at[4], g_r.at[4], up),
        copy(pdm.at[rear], r2.at[rear], g_s.at[5], g_r.at[5], down),
        copy(xsend, xrecv, g_s.at[6], g_r.at[6], partner),
    ]
    pd2[...] = part_d((y + 2) % 4).astype(bf16)
    begun(gc[0])
    begun(gc[1])
    gd[...] = part_d((y + 1) % 4)
    pd1[rear] = gd[rear].astype(bf16)
    begun(gc[2])
    acc1[...] = gd[front]
    gd[...] = part_d((y + 3) % 4)
    pdm[front] = gd[front].astype(bf16)
    begun(gc[3])
    acc2[...] = gd[rear]
    gd[...] = part_d(y)

    finish(*e2)
    sums = total(e2r, TP)
    oloss[...] = sums[1:2, 0:1] * (1.0 / PAIRS)
    lse_j = to_rows(sums[0:1])[:, 0:1]
    wq = (jnp.exp(logits[ROWS:] - lse) * (1.0 / PAIRS)).astype(bf16).astype(f32)
    wt = (jnp.exp(logits[ROWS:] - lse_j) * (1.0 / PAIRS)).astype(bf16).astype(f32)
    wts[ROWS:] = (wq + wt).astype(bf16)
    wtt[...] = jnp.transpose(wts[...])

    def target(s):
        return (xh + s // 4) % 2 * 4 + (zc + s % 4) % 4

    def cols(f):
        return lanes((y + 1 + f) % 4)

    def bcopy(f, k, n):
        at = rows_at(place(k, 1 - core, t), n)
        return copy(
            partq.at[at, cols(f)], sibr.at[k, pl.ds(0, n), cols(f)],
            b_s.at[f * 8 + k], b_r.at[f * 8 + k], sibling,
        )

    def three(k, core_s):
        return (k // 4) * 2 + core_s == third

    def part_q(f):
        partq[0:TAKE, cols(f)] = (
            jnp.dot(
                wtt[...], emb[0 : 2 * ROWS, cols(f)],
                preferred_element_type=f32,
            ) * inv_temp
        ).astype(bf16)

        @pl.loop(0, 8)
        def _(k):
            sized(three(k, 1 - core), lambda n: bcopy(f, k, n).start())

        @sent.append
        def _():
            @pl.loop(0, 8)
            def _(k):
                sized(three(k, 1 - core), lambda n: bcopy(f, k, n).wait_send())

    N3 = 3 * TILE

    def both(f, s):
        k = target(s)
        sized(three(k, core), lambda n: bcopy(f, k, n).wait_recv())
        cs = cols(f)
        return partq[rows_at(place(k, core, t), N3), cs].astype(f32) + sibr[k, :, cs].astype(f32)

    FLOW = ((2, zup), (6, zdown), (5, zup), (3, zdown), (1, zup), (7, zdown), (4, across))

    def ucopy(f, i, n):
        cs = cols(f)
        return copy(
            sendq.at[i, pl.ds(0, n), cs], recvq.at[i, pl.ds(0, n), cs],
            u_s.at[f * 8 + i], u_r.at[f * 8 + i], FLOW[i][1],
        )

    def usend(f, i, value):
        sendq[i, :, cols(f)] = value.astype(bf16)
        far = three(target(FLOW[i][0]), core)
        sized(far, lambda n: ucopy(f, i, n).start())
        sent.append(lambda: sized(far, lambda n: ucopy(f, i, n).wait_send()))

    def uwait(f, i, s):
        sized(three(target(s), core), lambda n: ucopy(f, i, n).wait_recv())
        return recvq[i, :, cols(f)].astype(f32)

    def q_far(f):
        usend(f, 0, both(f, 2))
        usend(f, 1, both(f, 6))
        usend(f, 2, both(f, 5))
        usend(f, 3, both(f, 3))

    def q_near(f):
        usend(f, 4, both(f, 1) + uwait(f, 0, 1))
        usend(f, 5, both(f, 7) + uwait(f, 1, 7))

    def q_across(f):
        usend(f, 6, both(f, 4) + uwait(f, 2, 4) + uwait(f, 5, 4))

    def tcopy(f, far, n):
        to = (y + 1 + f) % 4 + 4 * ((low + far) % 2)
        return copy(
            asend.at[to, pl.ds(0, n)], arecv.at[rows_at(mine, n)],
            t_s.at[f * 2 + far], t_r.at[f * 2 + far], (d, to),
        )

    def trecv(f, far):
        s = (y + 3 - f) % 4 + 4 * ((low + far) % 2)
        at = lambda n: arecv.at[rows_at(begin(d4, s), n)]
        sized(
            d4 == s // 2,
            lambda n: copy(at(n), at(n), t_s.at[0], t_r.at[f * 2 + far], (d, s)).wait_recv(),
        )

    def direct(f, s, n):
        cs = cols(f)
        return copy(
            sendq.at[s - 1, pl.ds(0, n), cs], recvq.at[s - 1, pl.ds(0, n), cs],
            u_s.at[f * 8 + s - 1], u_r.at[f * 8 + s - 1], device(s),
        )

    def q_direct(f):
        for s in (5, 7, 6, 4, 2, 1, 3):
            sendq[s - 1, :, cols(f)] = both(f, s).astype(bf16)
            far = three(target(s), core)
            sized(far, lambda n: direct(f, s, n).start())
            sent.append(
                lambda s=s, far=far: sized(far, lambda n: direct(f, s, n).wait_send())
            )

    def q_own(f):
        if f < 3:
            g = both(f, 0) + uwait(f, 3, 0) + uwait(f, 4, 0) + uwait(f, 6, 0)
        else:
            g = both(f, 0)
            for s in range(1, 8):
                sized(extra, lambda n: direct(f, s, n).wait_recv())
                g = g + recvq[s - 1, :, cols(f)].astype(f32)
        fb = (y + 1 + f) % 4
        asend[fb] = g[:, :FEATS].astype(bf16)
        asend[4 + fb] = g[:, FEATS:].astype(bf16)
        for far in range(2):
            if f < 3 or far == 1:
                sized(extra, lambda n: tcopy(f, far, n).start())
                sent.append(
                    lambda far=far: sized(extra, lambda n: tcopy(f, far, n).wait_send())
                )
        eq = emb[pl.ds(pl.multiple_of(ROWS + mine * TILE, TILE), N3), lanes(fb)].astype(f32)
        return jnp.sum(g * eq, axis=1, keepdims=True)

    part_q(0)
    part_q(1)
    q_far(0)
    part_q(2)
    q_far(1)
    gc[0].wait_recv()
    pd1[front] = (acc1[...] + halfs[0].astype(f32)).astype(bf16)
    begun(gc[4])
    gc[1].wait_recv()
    pdm[rear] = (acc2[...] + halfs[1].astype(f32)).astype(bf16)
    begun(gc[5])
    q_far(2)
    part_q(3)
    q_near(0)
    q_near(1)
    q_near(2)
    q_direct(3)
    q_across(0)
    for i in range(2, 6):
        gc[i].wait_recv()
    gd[...] = gd[...] + r1[...].astype(f32) + r2[...].astype(f32)
    xsend[...] = jnp.where(low == 0, gd[:, FEATS:], gd[:, :FEATS]).astype(bf16)
    begun(gc[6])
    q_across(1)
    dots = q_own(0)
    q_across(2)
    dots = dots + q_own(1)

    gc[6].wait_recv()
    gd[:, 0:FEATS] = jnp.where(low == 0, gd[:, :FEATS], gd[:, FEATS:]) + xrecv[...].astype(f32)
    fd = jnp.sum(gd[:, 0:FEATS] * (xd[...].astype(f32) * gain[...]), axis=1, keepdims=True)
    e3s[...] = to_lanes(fd)
    e3 = (e3s, e3r, e3_s, e3_r, TP, t, by_tensor)
    exchange(*e3)
    dots = dots + q_own(2)

    dots = dots + q_own(3)
    dsend[...] = jnp.broadcast_to(dots, (N3, 128))

    def vcopy(k, n):
        to = (t + k) % TP
        return copy(
            dsend.at[pl.ds(0, n)], drecv.at[rows_at(mine, n)], v_s.at[k], v_r.at[k], (d, to)
        )

    def vrecv(k, n):
        s = (t + TP - k) % TP
        at = drecv.at[rows_at(begin(d4, s), n)]
        return copy(at, at, v_s.at[k], v_r.at[k], (d, s))

    @pl.loop(1, TP)
    def _(k):
        sized(extra, lambda n: vcopy(k, n).start())

    @sent.append
    def _():
        @pl.loop(1, TP)
        def _(k):
            sized(extra, lambda n: vcopy(k, n).wait_send())

    def tlocal(n):
        arecv[rows_at(mine, n)] = asend[t, pl.ds(0, n)]
        drecv[rows_at(mine, n)] = dsend[pl.ds(0, n)]

    sized(extra, tlocal)

    finish(*e3)
    col = to_rows(total(e3r, TP)[0:1])[:, 0:1]
    iv = invd[:, 0:1]
    h = xd[...].astype(f32)
    gx = iv * gd[:, 0:FEATS] - h * gain[...] * (iv * iv * iv * col)
    outd[...] = (gx * gain[...]).astype(bf16)
    outs = [pltpu.make_async_copy(outd, od, io.at[0]), pltpu.make_async_copy(outq, oq, io.at[1])]
    outs[0].start()
    gg = jnp.sum(gx * h, axis=0, keepdims=True)

    for f in range(4):
        for far in range(2):
            if f < 3 or far == 1:
                trecv(f, far)

    @pl.loop(1, TP)
    def _(k):
        sized(d4 == ((t + TP - k) % TP) // 2, lambda n: vrecv(k, n).wait_recv())

    h = xq[...].astype(f32)
    iv = invq[0:ROWS, 0:1]
    gx = iv * arecv[...].astype(f32) - h * gain[...] * (iv * iv * drecv[:, 0:1])
    gg = gg + jnp.sum(gx * h, axis=0, keepdims=True)
    cs4[...] = jnp.broadcast_to(gg, (8, FEATS))
    c4 = copy(cs4, cr4, c_s.at[2], c_r.at[2], sibling)
    begun(c4)
    outq[...] = (gx * gain[...]).astype(bf16)
    outs[1].start()
    c4.wait_recv()
    e4s[...] = cs4[...] + cr4[...]
    e4 = (e4s, e4r, e4_s, e4_r, 8, hz, by_hz)
    exchange(*e4)
    finish(*e4)
    ogain[...] = total(e4r, 8)[0:1]
    for c in outs:
        c.wait()

    for wait in sent:
        wait()


def results(gq, gdoc, ggain, loss, oq, od, ogain, oloss):
    oq[...] = gq[...]
    od[...] = gdoc[...]
    ogain[...] = ggain[...]
    oloss[...] = loss[...]


def shards(query_states, doc_states, gain, positives):
    vm = pl.BlockSpec(memory_space=pltpu.VMEM)
    hbm = pl.BlockSpec(memory_space=pl.ANY)
    S = pltpu.VMEM
    dma = lambda n: pltpu.SemaphoreType.DMA((n,))
    pair = lambda n: [dma(n), dma(n)]
    scratch = [
        S((ROWS, FEATS), bf16), S((ROWS, FEATS), bf16),
        S((ROWS, FEATS), bf16), S((ROWS, FEATS), bf16), S((1, FULL), f32),
        S((2 * ROWS, FULL), bf16), S((2 * ROWS + TILE, FULL), bf16), S((TAKE, FULL), bf16),
        S((ROWS + TILE, 128), f32), S((ROWS, 128), f32),
        S((2 * ROWS, TAKE), f32), S((8, TAKE), f32), S((2 * ROWS, TAKE), bf16), S((TAKE, 2 * ROWS), bf16),
        S((8, FEATS), f32), S((TP, 8, FEATS), f32),
        S((8, TAKE), f32), S((8, TAKE), f32), S((8, 8, TAKE), f32),
        S((8, ROWS), f32), S((TP, 8, ROWS), f32),
        S((8, ROWS), f32), S((TP, 8, ROWS), f32),
        S((8, FEATS), f32), S((8, FEATS), f32), S((8, FEATS), f32), S((8, 8, FEATS), f32),
        S((DP, 8, 128), f32), S((8, 128), f32),
        S((TAKE + TILE, FULL), bf16), S((8, 3 * TILE, FULL), bf16),
        S((7, 3 * TILE, FULL), bf16), S((7, 3 * TILE, FULL), bf16),
        S((ROWS // 2, WIDE), f32), S((ROWS // 2, WIDE), f32),
        S((ROWS, WIDE), bf16), S((ROWS, WIDE), bf16), S((ROWS, WIDE), bf16),
        S((2, ROWS // 2, WIDE), bf16), S((ROWS, WIDE), bf16), S((ROWS, WIDE), bf16),
        S((ROWS, WIDE), f32), S((ROWS, FEATS), bf16), S((ROWS, FEATS), bf16),
        S((TP, 3 * TILE, FEATS), bf16), S((ROWS, FEATS), bf16), S((3 * TILE, 128), f32), S((ROWS, 128), f32),
        S((ROWS, FEATS), bf16), S((ROWS, FEATS), bf16),
    ]
    sems = (
        pair(2 * NCH) + pair(TP) + pair(8) + pair(TP) + pair(TP) + pair(8) + pair(8)
        + pair(8 * NCH) + pair(64) + [dma(4)] + pair(32) + pair(32) + pair(7) + pair(TP) + pair(TP)
        + pair(3) + [dma(2)]
    )
    gq, gdoc, ggain, loss = pl.pallas_call(
        step,
        name="infonce_step",
        out_shape=(
            jax.ShapeDtypeStruct((ROWS, FEATS), bf16),
            jax.ShapeDtypeStruct((ROWS, FEATS), bf16),
            jax.ShapeDtypeStruct((1, FEATS), f32),
            jax.ShapeDtypeStruct((1, 1), f32),
        ),
        in_specs=[hbm, hbm, vm, vm],
        out_specs=(hbm, hbm, vm, vm),
        scratch_shapes=scratch + sems,
        compiler_params=pltpu.CompilerParams(
            collective_id=0, has_side_effects=True, vmem_limit_bytes=56 * 2**20
        ),
        cost_estimate=pl.CostEstimate(
            flops=7_000_000_000, bytes_accessed=3_000_000, transcendentals=1_000_000
        ),
    )(query_states, doc_states, gain[None, :], positives[None, :])
    gq, gdoc, ggain, loss = pl.pallas_call(
        results,
        name="results",
        out_shape=(
            jax.ShapeDtypeStruct((ROWS, FEATS), bf16),
            jax.ShapeDtypeStruct((ROWS, FEATS), bf16),
            jax.ShapeDtypeStruct((1, FEATS), f32),
            jax.ShapeDtypeStruct((1, 1), f32),
        ),
        in_specs=[vm] * 4,
        out_specs=(vm,) * 4,
    )(gq, gdoc, ggain, loss)
    return gq, gdoc, ggain[0], loss[0, 0]


def solution(mesh):
    return jax.shard_map(
        shards,
        mesh=mesh,
        in_specs=(P("dp", "tensor"), P("dp", "tensor"), P("tensor"), P("dp")),
        out_specs=(P("dp", "tensor"), P("dp", "tensor"), P("tensor"), P()),
        check_vma=False,
    )
```

```python
import functools

import jax
import jax.numpy as jnp
from jax import lax
from jax.experimental import pallas as pl
from jax.experimental.pallas import tpu as pltpu
from jax.sharding import PartitionSpec as P

eps_len = 1e-06
inv_temp = 100.0
masked = -1e30

MESH = pl.DeviceIdType.MESH
HIGH = lax.Precision.HIGHEST
f32 = jnp.float32
bf16 = jnp.bfloat16

DP = 16
TP = 8
ROWS = 288
FEATS = 448
WIDE = 2 * FEATS
FULL = TP * FEATS
PAIRS = DP * ROWS
TAKE = DP * ROWS // TP
TILE = 16
CHUNK = 96
NCH = ROWS // CHUNK
HALF = CHUNK // 2


def step(
    hq, hd, gain, pos,
    oq, od, ogain, oloss,
    xq, xd, pq, pd, gfull, raw, emb, qi, invq, invd, logits, stat, wts, wtt,
    e0s, e0r, cr1, e1s, e1r, e2s, e2r, e3s, e3r, cs4, cr4, e4s, e4r, epr, posv,
    partq, sibr, sendq, recvq, acc1, acc2, pd2, pd1, pdm, halfs, r1, r2, gd, xsend, xrecv,
    asend, arecv, pick, cs5, cr5, e5s, e5r, outq, outd,
    x_s, x_r, e0_s, e0_r, e1_s, e1_r, e2_s, e2_r, e3_s, e3_r, e4_s, e4_r, ep_s, ep_r,
    y_s, y_r, a_s, a_r, loc, b_s, b_r, u_s, u_r, g_s, g_r, t_s, t_r, e5_s, e5_r, c_s, c_r, io,
):
    d = lax.axis_index("dp")
    t = lax.axis_index("tensor")
    hz = d // 2
    core = d % 2
    zc = hz % 4
    d4 = (hz // 4) * 2 + core
    low = t // 4
    y = t % 4
    xh = hz // 4
    sources = [pltpu.make_async_copy(hq, xq, io.at[0]), pltpu.make_async_copy(hd, xd, io.at[1])]
    for c in sources:
        c.start()
    third = t // 2
    sibling = (hz * 2 + (1 - core), t)
    partner = (d, (t + 4) % TP)
    up = (d, low * 4 + (y + 1) % 4)
    down = (d, low * 4 + (y + 3) % 4)
    zup = ((xh * 4 + (zc + 1) % 4) * 2 + core, t)
    zdown = ((xh * 4 + (zc + 3) % 4) * 2 + core, t)
    across = ((hz + 4) % 8 * 2 + core, t)

    sent = []

    def copy(src, dst, ss, rs, dev):
        return pltpu.make_async_remote_copy(
            src_ref=src, dst_ref=dst, send_sem=ss, recv_sem=rs, device_id=dev, device_id_type=MESH
        )

    def lanes(block):
        return pl.ds(pl.multiple_of(block * WIDE, 128), WIDE)

    def rows_at(tile, n):
        return pl.ds(pl.multiple_of(tile * TILE, TILE), n)

    def place(hz_s, core_s, tens):
        q = (hz_s // 4) * 2 + core_s
        e = tens // 2
        return (hz_s % 4) * 9 + 2 * q + jnp.where(q > e, 1, 0)

    def begin(q, tens):
        return 2 * tens + jnp.clip(tens - 2 * q, 0, 2)

    def sized(extra, fn):
        @pl.when(extra)
        def _():
            fn(3 * TILE)

        @pl.when(jnp.logical_not(extra))
        def _():
            fn(2 * TILE)

    barrier = pltpu.get_barrier_semaphore()

    @pl.loop(1, TP)
    def _(k):
        pl.semaphore_signal(barrier, inc=1, device_id=(d, (t + k) % TP), device_id_type=MESH)

    @pl.loop(1, 8)
    def _(k):
        pl.semaphore_signal(
            barrier, inc=1, device_id=((hz + k) % 8 * 2 + core, t), device_id_type=MESH
        )

    pl.semaphore_signal(barrier, inc=1, device_id=sibling, device_id_type=MESH)
    def to_lanes(col):
        return jnp.transpose(jnp.broadcast_to(col, (ROWS, 128)))[:8]

    def to_rows(vec):
        return jnp.transpose(jnp.broadcast_to(vec, (128, ROWS)))

    sub8 = lambda n: lax.broadcasted_iota(jnp.int32, (8, n), 0)

    posv[...] = jnp.zeros_like(posv)
    for seg in range(3):
        at = slice(128 * seg, min(128 * (seg + 1), ROWS))
        width = at.stop - at.start
        posv[seg : seg + 1, 0:width] = (pos[:, at] // 128).astype(f32)
        posv[3 + seg : 4 + seg, 0:width] = (pos[:, at] % 128).astype(f32)
    pl.semaphore_wait(barrier, TP + 7)

    def xcopy(i):
        src, dst = (hq, pq) if i < NCH else (hd, pd)
        part = pl.ds((i % NCH) * CHUNK, CHUNK)
        return copy(src.at[part], dst.at[part], x_s.at[i], x_r.at[i], partner)

    def begun(c):
        c.start()
        sent.append(c.wait_send)

    def exchange(src, recv, ss, rs, size, me, dev):
        @pl.loop(1, size)
        def _(k):
            copy(src, recv.at[me], ss.at[k], rs.at[me], dev((me + k) % size)).start()

        @sent.append
        def _():
            @pl.loop(1, size)
            def _(k):
                copy(src, recv.at[me], ss.at[k], rs.at[me], dev((me + k) % size)).wait_send()

    def finish(src, recv, ss, rs, size, me, dev):
        recv[me] = src[...]

        @pl.loop(1, size)
        def _(k):
            s = (me + k) % size
            copy(src, recv.at[s], ss.at[k], rs.at[s], dev(s)).wait_recv()

    by_tensor = lambda s: (d, s)
    by_hz = lambda s: (s * 2 + core, t)

    def total(recv, size):
        acc = recv[0]
        for s in range(1, size):
            acc = acc + recv[s]
        return acc

    e0 = (e0s, e0r, e0_s, e0_r, TP, t, by_tensor)
    begun(xcopy(0))
    for c in sources:
        c.wait()
    nq = xq[...].astype(f32) * gain[...]
    nd = xd[...].astype(f32) * gain[...]
    lq = to_lanes(jnp.sum(nq * nq, axis=1, keepdims=True))
    ld = to_lanes(jnp.sum(nd * nd, axis=1, keepdims=True))
    e0s[...] = jnp.broadcast_to(gain[...], (8, FEATS))
    e0s[0:1, 0:ROWS] = lq[0:1]
    e0s[1:2, 0:ROWS] = ld[0:1]
    exchange(*e0)
    for i in range(1, 2 * NCH):
        begun(xcopy(i))

    mine = begin(d4, t)
    here = place(hz, core, t)
    extra = d4 == third

    def pack(a, k):
        own, part, base = (xq, pq, ROWS) if a == 0 else (xd, pd, 0)
        xcopy(a * NCH + k).wait_recv()
        rs = pl.ds(k * CHUNK, CHUNK)
        eo = own[rs].astype(f32)
        ep = part[rs].astype(f32)
        left = jnp.where(low == 0, eo, ep)
        right = jnp.where(low == 0, ep, eo)
        raw[pl.ds(base + k * CHUNK, CHUNK), lanes(y)] = jnp.concatenate(
            [left, right], axis=1
        ).astype(bf16)

    def normalise(a, k, block):
        inverse, base = (invq, ROWS) if a == 0 else (invd, 0)
        for part in range(2):
            rs = k * CHUNK + part * HALF
            scale = inverse[pl.ds(rs, HALF), 0:1]
            at = pl.ds(base + rs, HALF)
            cs = lanes(block)
            emb[at, cs] = (raw[at, cs].astype(f32) * gfull[:, cs] * scale).astype(bf16)

    def ycopy(a, k, kind):
        base = (ROWS if a == 0 else 0) + k * CHUNK
        i = (a * NCH + k) * 4 + kind
        if kind < 2:
            at, dev, block = pl.ds(base, CHUNK), (up, down)[kind], y
        elif kind == 2:
            at, dev, block = pl.ds(base, HALF), up, (y + 3) % 4
        else:
            at, dev, block = pl.ds(base + HALF, HALF), down, (y + 1) % 4
        ref = raw.at[at, lanes(block)]
        return copy(ref, ref, y_s.at[i], y_r.at[i], dev)

    def yrecv(a, k, kind):
        base = (ROWS if a == 0 else 0) + k * CHUNK
        i = (a * NCH + k) * 4 + kind
        at = pl.ds(base, CHUNK) if kind < 2 else pl.ds(base + (kind - 2) * HALF, HALF)
        block = ((y + 3) % 4, (y + 1) % 4, (y + 2) % 4, (y + 2) % 4)[kind]
        ref = raw.at[at, lanes(block)]
        copy(ref, ref, y_s.at[i], y_r.at[i], up).wait_recv()

    def source(s):
        return (xh + s // 4) % 2 * 4 + (zc + 4 - s % 4) % 4

    def gives(s, core_s):
        return (xh + s // 4) % 2 * 2 + core_s == third

    def device(s):
        return ((xh + s // 4) % 2 * 8 + (zc + s % 4) % 4 * 2 + core, t)

    def spot(i, s, core_s, n):
        block = (y + (0, 3, 1, 2)[i]) % 4
        return qi.at[rows_at(place(source(s), core_s, t), n), lanes(block)]

    def own_rows(i, n):
        block = (y + (0, 3, 1, 2)[i]) % 4
        return emb.at[pl.ds(pl.multiple_of(ROWS + mine * TILE, TILE), n), lanes(block)]

    def give_own(i, slot, dev):
        def c(n):
            return copy(
                own_rows(i, n), spot(i, 0, core, n), a_s.at[i * 16 + slot], a_r.at[i * 16 + slot], dev
            )

        sized(extra, lambda n: c(n).start())
        sent.append(lambda: sized(extra, lambda n: c(n).wait_send()))

    def pass_on(i, s, slot, dev):
        def c(n):
            ref = spot(i, s, core, n)
            return copy(ref, ref, a_s.at[i * 16 + slot], a_r.at[i * 16 + slot], dev)

        sized(gives(s, core), lambda n: c(n).start())
        sent.append(lambda: sized(gives(s, core), lambda n: c(n).wait_send()))

    def agot(i, s):
        def c(n):
            ref = spot(i, s, core, n)
            copy(ref, ref, a_s.at[i * 16 + s], a_r.at[i * 16 + s], sibling).wait_recv()

        sized(gives(s, core), c)

    def alocal(i, n):
        return pltpu.make_async_copy(own_rows(i, n), spot(i, 0, core, n), loc.at[i])

    def astart(i):
        for s in (1, 3, 2, 4) if i < 3 else (4, 1, 3, 2, 5, 7, 6):
            give_own(i, s, device(s))
        give_own(i, 8, sibling)
        sized(extra, lambda n: alocal(i, n).start())

    def amid(i):
        agot(i, 4)
        if i < 3:
            for s in (1, 3, 2):
                pass_on(i, 4, 4 + s, device(s))
        pass_on(i, 4, 12, sibling)
        for s in (1, 3, 2):
            agot(i, s)
            pass_on(i, s, 8 + s, sibling)

    def alast(i):
        for s in (5, 7, 6):
            agot(i, s)
            pass_on(i, s, 8 + s, sibling)

    def afinish(i):
        sized(extra, lambda n: alocal(i, n).wait())

        @pl.loop(0, 8)
        def _(s):
            def c(n):
                ref = spot(i, s, 1 - core, n)
                copy(ref, ref, a_s.at[i * 16], a_r.at[i * 16 + 8 + s], sibling).wait_recv()

            sized(gives(s, 1 - core), c)

    for k in range(NCH):
        pack(0, k)
        begun(ycopy(0, k, 0))
        begun(ycopy(0, k, 1))
    finish(*e0)
    inv = lax.rsqrt(total(e0r, TP)[:, 0:ROWS] + eps_len)
    invq[0:ROWS] = to_rows(inv[0:1])
    invd[...] = to_rows(inv[1:2])
    for b in range(4):
        gfull[:, b * WIDE : (b + 1) * WIDE] = jnp.concatenate(
            [e0r[b, 2:3], e0r[4 + b, 2:3]], axis=1
        )
    for k in range(NCH):
        normalise(0, k, y)
    astart(0)
    ep = (posv, epr, ep_s, ep_r, 8, hz, by_hz)
    exchange(*ep)
    for k in range(NCH):
        yrecv(0, k, 0)
        begun(ycopy(0, k, 2))
        yrecv(0, k, 1)
        begun(ycopy(0, k, 3))
    for k in range(NCH):
        pack(1, k)
        begun(ycopy(1, k, 0))
        begun(ycopy(1, k, 1))
    for k in range(NCH):
        normalise(0, k, (y + 3) % 4)
        normalise(0, k, (y + 1) % 4)
    astart(1)
    astart(2)
    amid(0)
    for k in range(NCH):
        yrecv(0, k, 2)
        yrecv(0, k, 3)
        normalise(0, k, (y + 2) % 4)
    astart(3)
    for k in range(NCH):
        normalise(1, k, y)
    alast(0)
    amid(1)
    amid(2)

    def docs_on(k):
        yrecv(1, k, 0)
        begun(ycopy(1, k, 2))
        yrecv(1, k, 1)
        begun(ycopy(1, k, 3))

    docs_on(0)
    alast(1)
    docs_on(1)
    alast(2)
    docs_on(2)
    for k in range(NCH):
        normalise(1, k, (y + 3) % 4)
        normalise(1, k, (y + 1) % 4)
    amid(3)
    alast(3)
    for i in range(4):
        afinish(i)

    lane_p = lax.broadcasted_iota(jnp.int32, (1, TAKE), 1)
    tile_p = lane_p // TILE
    w_p = tile_p % 9
    q_p = jnp.where(
        w_p < 2 * third, w_p // 2, jnp.where(w_p <= 2 * third + 2, third, (w_p - 1) // 2)
    )
    off_p = w_p - 2 * q_p - jnp.where(q_p > third, 1, 0)
    dev_p = (q_p // 2) * 8 + (tile_p // 9) * 2 + q_p % 2
    row_p = dev_p * ROWS + (begin(q_p, t) + off_p) * TILE + lane_p % TILE
    finish(*ep)
    epc = copy(epr.at[pl.ds(0, 8)], epr.at[pl.ds(8, 8)], c_s.at[0], c_r.at[0], sibling)
    begun(epc)

    stat[0:1] = jnp.full((1, TAKE), masked, f32)
    stat[1:8] = jnp.zeros((7, TAKE), f32)

    def product(rows, cs):
        return lax.dot_general(
            emb[rows, cs], qi[:, cs], (((1,), (1,)), ((), ())), preferred_element_type=f32
        )

    def statistics(s):
        old = stat[0:1]
        new = jnp.maximum(old, jnp.max(s, axis=0, keepdims=True))
        stat[0:1] = new
        stat[1:2] = stat[1:2] * jnp.exp(old - new) + jnp.sum(
            jnp.exp(s - new), axis=0, keepdims=True
        )

    own_j = d * ROWS + lax.broadcasted_iota(jnp.int32, (ROWS, TAKE), 0)
    logits[ROWS:] = product(pl.ds(ROWS, ROWS), slice(None))
    logits[ROWS:] = jnp.where(own_j == row_p, masked, logits[ROWS:] * inv_temp)
    statistics(logits[ROWS:])
    logits[0:ROWS] = product(pl.ds(0, ROWS), lanes(y))
    for b in (1, 3):
        logits[0:ROWS] = logits[0:ROWS] + product(pl.ds(0, ROWS), lanes((y + b) % 4))

    epc.wait_recv()
    local_p = (begin(q_p, t) + off_p) * TILE + lane_p % TILE
    lane_of = lax.broadcasted_iota(jnp.int32, (128, TAKE), 0)
    spread = jnp.where(lane_of == local_p % 128, 1.0, 0.0).astype(bf16)
    found = jnp.dot(
        epr[...].reshape(DP * 8, 128).astype(bf16), spread, preferred_element_type=f32
    )
    slot_p = jnp.where(dev_p % 2 == core, dev_p // 2, 8 + dev_p // 2) * 8 + local_p // 128
    high = jnp.sum(jnp.where(lane_of == slot_p, found, 0.0), axis=0, keepdims=True)
    rest = jnp.sum(jnp.where(lane_of == slot_p + 3, found, 0.0), axis=0, keepdims=True)
    pos_p = (high * 128.0 + rest).astype(jnp.int32)

    for k in range(NCH):
        yrecv(1, k, 2)
        yrecv(1, k, 3)
        normalise(1, k, (y + 2) % 4)
    logits[0:ROWS] = (logits[0:ROWS] + product(pl.ds(0, ROWS), lanes((y + 2) % 4))) * inv_temp
    stat[2:3] = jnp.sum(jnp.where(own_j == pos_p, logits[0:ROWS], 0.0), axis=0, keepdims=True)
    statistics(logits[0:ROWS])

    sub_t = sub8(TAKE)
    c1 = copy(stat, cr1, c_s.at[1], c_r.at[1], sibling)
    begun(c1)
    c1.wait_recv()
    top, tot, posit = stat[0:1], stat[1:2], stat[2:3]
    top_o = cr1[0:1]
    top_c = jnp.maximum(top, top_o)
    tot = tot * jnp.exp(top - top_c) + cr1[1:2] * jnp.exp(top_o - top_c)
    e1s[...] = jnp.where(sub_t == 0, top_c, jnp.where(sub_t == 1, tot, posit + cr1[2:3]))
    e1 = (e1s, e1r, e1_s, e1_r, 8, hz, by_hz)
    exchange(*e1)
    pick[...] = jnp.where(own_j == row_p, 1.0, 0.0).astype(bf16)
    finish(*e1)
    all_top = e1r[0, 0:1]
    for s in range(1, 8):
        all_top = jnp.maximum(all_top, e1r[s, 0:1])
    all_tot = jnp.zeros_like(all_top)
    all_pos = jnp.zeros_like(all_top)
    for s in range(8):
        all_tot = all_tot + e1r[s, 1:2] * jnp.exp(e1r[s, 0:1] - all_top)
        all_pos = all_pos + e1r[s, 2:3]
    lse = all_top + jnp.log(all_tot)
    loss_part = jnp.sum(lse - all_pos, axis=1, keepdims=True)

    def own_lanes(vec):
        p1 = vec.astype(bf16).astype(f32)
        p2 = (vec - p1).astype(bf16).astype(f32)
        split = jnp.where(
            sub_t == 0, p1, jnp.where(sub_t == 1, p2, jnp.where(sub_t == 2, vec - p1 - p2, 0.0))
        )
        return jnp.sum(
            lax.dot_general(
                split.astype(bf16), pick[...], (((1,), (1,)), ((), ())),
                preferred_element_type=f32,
            ),
            axis=0, keepdims=True,
        )

    lse_own = own_lanes(lse)
    e2s[...] = jnp.where(sub8(ROWS) == 0, lse_own, loss_part)
    e2 = (e2s, e2r, e2_s, e2_r, TP, t, by_tensor)
    exchange(*e2)
    wd = (jnp.exp(logits[0:ROWS] - lse) - (own_j == pos_p).astype(f32)) * (1.0 / PAIRS)
    wts[0:ROWS] = wd.astype(bf16)

    def part_d(block):
        return lax.dot_general(
            wts[0:ROWS], qi[:, lanes(block)], (((1,), (0,)), ((), ())),
            preferred_element_type=f32,
        ) * inv_temp

    MID = ROWS // 2
    front, rear = pl.ds(0, MID), pl.ds(MID, MID)
    gc = [
        copy(pd2.at[front], halfs.at[0], g_s.at[0], g_r.at[0], up),
        copy(pd2.at[rear], halfs.at[1], g_s.at[1], g_r.at[1], down),
        copy(pd1.at[rear], r1.at[rear], g_s.at[2], g_r.at[2], up),
        copy(pdm.at[front], r2.at[front], g_s.at[3], g_r.at[3], down),
        copy(pd1.at[front], r1.at[front], g_s.at[4], g_r.at[4], up),
        copy(pdm.at[rear], r2.at[rear], g_s.at[5], g_r.at[5], down),
        copy(xsend, xrecv, g_s.at[6], g_r.at[6], partner),
    ]
    pd2[...] = part_d((y + 2) % 4).astype(bf16)
    begun(gc[0])
    begun(gc[1])
    gd[...] = part_d((y + 1) % 4)
    pd1[rear] = gd[rear].astype(bf16)
    begun(gc[2])
    acc1[...] = gd[front]
    gd[...] = part_d((y + 3) % 4)
    pdm[front] = gd[front].astype(bf16)
    begun(gc[3])
    acc2[...] = gd[rear]
    gd[...] = part_d(y)

    finish(*e2)
    sums = total(e2r, TP)
    oloss[...] = sums[1:2, 0:1] * (1.0 / PAIRS)
    lse_j = to_rows(sums[0:1])[:, 0:1]
    wq = (jnp.exp(logits[ROWS:] - lse) * (1.0 / PAIRS)).astype(bf16).astype(f32)
    wt = (jnp.exp(logits[ROWS:] - lse_j) * (1.0 / PAIRS)).astype(bf16).astype(f32)
    wts[ROWS:] = (wq + wt).astype(bf16)
    wtt[...] = jnp.transpose(wts[...])

    weighed = wts[...].astype(f32) * logits[...]
    cs5[...] = jnp.broadcast_to(jnp.sum(weighed, axis=0, keepdims=True), (8, TAKE))
    c5 = copy(cs5, cr5, c_s.at[3], c_r.at[3], sibling)
    begun(c5)
    e3s[...] = to_lanes(jnp.sum(weighed[0:ROWS], axis=1, keepdims=True))

    def target(s):
        return (xh + s // 4) % 2 * 4 + (zc + s % 4) % 4

    def cols(f):
        return lanes((y + 1 + f) % 4)

    def bcopy(f, k, n):
        at = rows_at(place(k, 1 - core, t), n)
        return copy(
            partq.at[at, cols(f)], sibr.at[k, pl.ds(0, n), cols(f)],
            b_s.at[f * 8 + k], b_r.at[f * 8 + k], sibling,
        )

    def three(k, core_s):
        return (k // 4) * 2 + core_s == third

    def part_q(f):
        partq[0:TAKE, cols(f)] = (
            jnp.dot(
                wtt[...], emb[0 : 2 * ROWS, cols(f)],
                preferred_element_type=f32,
            ) * inv_temp
        ).astype(bf16)

        @pl.loop(0, 8)
        def _(k):
            sized(three(k, 1 - core), lambda n: bcopy(f, k, n).start())

        @sent.append
        def _():
            @pl.loop(0, 8)
            def _(k):
                sized(three(k, 1 - core), lambda n: bcopy(f, k, n).wait_send())

    N3 = 3 * TILE

    def both(f, s):
        k = target(s)
        sized(three(k, core), lambda n: bcopy(f, k, n).wait_recv())
        cs = cols(f)
        return partq[rows_at(place(k, core, t), N3), cs].astype(f32) + sibr[k, :, cs].astype(f32)

    FLOW = ((2, zup), (6, zdown), (5, zup), (3, zdown), (1, zup), (7, zdown), (4, across))

    def ucopy(f, i, n):
        cs = cols(f)
        return copy(
            sendq.at[i, pl.ds(0, n), cs], recvq.at[i, pl.ds(0, n), cs],
            u_s.at[f * 8 + i], u_r.at[f * 8 + i], FLOW[i][1],
        )

    def usend(f, i, value):
        sendq[i, :, cols(f)] = value.astype(bf16)
        far = three(target(FLOW[i][0]), core)
        sized(far, lambda n: ucopy(f, i, n).start())
        sent.append(lambda: sized(far, lambda n: ucopy(f, i, n).wait_send()))

    def uwait(f, i, s):
        sized(three(target(s), core), lambda n: ucopy(f, i, n).wait_recv())
        return recvq[i, :, cols(f)].astype(f32)

    def q_far(f):
        usend(f, 0, both(f, 2))
        usend(f, 1, both(f, 6))
        usend(f, 2, both(f, 5))
        usend(f, 3, both(f, 3))

    def q_near(f):
        usend(f, 4, both(f, 1) + uwait(f, 0, 1))
        usend(f, 5, both(f, 7) + uwait(f, 1, 7))

    def q_across(f):
        usend(f, 6, both(f, 4) + uwait(f, 2, 4) + uwait(f, 5, 4))

    def tcopy(f, far, n):
        to = (y + 1 + f) % 4 + 4 * ((low + far) % 2)
        return copy(
            asend.at[to, pl.ds(0, n)], arecv.at[rows_at(mine, n)],
            t_s.at[f * 2 + far], t_r.at[f * 2 + far], (d, to),
        )

    def trecv(f, far):
        s = (y + 3 - f) % 4 + 4 * ((low + far) % 2)
        at = lambda n: arecv.at[rows_at(begin(d4, s), n)]
        sized(
            d4 == s // 2,
            lambda n: copy(at(n), at(n), t_s.at[0], t_r.at[f * 2 + far], (d, s)).wait_recv(),
        )

    def direct(f, s, n):
        cs = cols(f)
        return copy(
            sendq.at[s - 1, pl.ds(0, n), cs], recvq.at[s - 1, pl.ds(0, n), cs],
            u_s.at[f * 8 + s - 1], u_r.at[f * 8 + s - 1], device(s),
        )

    def q_direct(f):
        for s in (5, 7, 6, 4, 2, 1, 3):
            sendq[s - 1, :, cols(f)] = both(f, s).astype(bf16)
            far = three(target(s), core)
            sized(far, lambda n: direct(f, s, n).start())
            sent.append(
                lambda s=s, far=far: sized(far, lambda n: direct(f, s, n).wait_send())
            )

    def q_own(f):
        if f < 3:
            g = both(f, 0) + uwait(f, 3, 0) + uwait(f, 4, 0) + uwait(f, 6, 0)
        else:
            g = both(f, 0)
            for s in range(1, 8):
                sized(extra, lambda n: direct(f, s, n).wait_recv())
                g = g + recvq[s - 1, :, cols(f)].astype(f32)
        fb = (y + 1 + f) % 4
        asend[fb] = g[:, :FEATS].astype(bf16)
        asend[4 + fb] = g[:, FEATS:].astype(bf16)
        for far in range(2):
            if f < 3 or far == 1:
                sized(extra, lambda n: tcopy(f, far, n).start())
                sent.append(
                    lambda far=far: sized(extra, lambda n: tcopy(f, far, n).wait_send())
                )

    part_q(0)
    part_q(1)
    q_far(0)
    c5.wait_recv()
    e5s[...] = cs5[...] + cr5[...]
    e5 = (e5s, e5r, e5_s, e5_r, 8, hz, by_hz)
    exchange(*e5)
    part_q(2)
    q_far(1)
    gc[0].wait_recv()
    pd1[front] = (acc1[...] + halfs[0].astype(f32)).astype(bf16)
    begun(gc[4])
    gc[1].wait_recv()
    pdm[rear] = (acc2[...] + halfs[1].astype(f32)).astype(bf16)
    begun(gc[5])
    q_far(2)
    part_q(3)
    q_near(0)
    q_near(1)
    q_near(2)
    q_direct(3)
    finish(*e5)
    e3s[0:1] = own_lanes(total(e5r, 8)[0:1])
    e3 = (e3s, e3r, e3_s, e3_r, TP, t, by_tensor)
    exchange(*e3)
    q_across(0)
    for i in range(2, 6):
        gc[i].wait_recv()
    gd[...] = gd[...] + r1[...].astype(f32) + r2[...].astype(f32)
    xsend[...] = jnp.where(low == 0, gd[:, FEATS:], gd[:, :FEATS]).astype(bf16)
    begun(gc[6])
    q_across(1)
    q_own(0)
    q_across(2)
    q_own(1)

    gc[6].wait_recv()
    gd[:, 0:FEATS] = jnp.where(low == 0, gd[:, :FEATS], gd[:, FEATS:]) + xrecv[...].astype(f32)
    q_own(2)
    q_own(3)

    def tlocal(n):
        arecv[rows_at(mine, n)] = asend[t, pl.ds(0, n)]

    sized(extra, tlocal)

    finish(*e3)
    dots = total(e3r, TP)
    col = to_rows(dots[1:2])[:, 0:1]
    iv = invd[:, 0:1]
    h = xd[...].astype(f32)
    gx = iv * gd[:, 0:FEATS] - h * gain[...] * (iv * iv * col)
    outd[...] = (gx * gain[...]).astype(bf16)
    outs = [pltpu.make_async_copy(outd, od, io.at[0]), pltpu.make_async_copy(outq, oq, io.at[1])]
    outs[0].start()
    gg = jnp.sum(gx * h, axis=0, keepdims=True)

    for f in range(4):
        for far in range(2):
            if f < 3 or far == 1:
                trecv(f, far)

    col = to_rows(dots[0:1])[:, 0:1]
    h = xq[...].astype(f32)
    iv = invq[0:ROWS, 0:1]
    gx = iv * arecv[...].astype(f32) - h * gain[...] * (iv * iv * col)
    gg = gg + jnp.sum(gx * h, axis=0, keepdims=True)
    cs4[...] = jnp.broadcast_to(gg, (8, FEATS))
    c4 = copy(cs4, cr4, c_s.at[2], c_r.at[2], sibling)
    begun(c4)
    outq[...] = (gx * gain[...]).astype(bf16)
    outs[1].start()
    c4.wait_recv()
    e4s[...] = cs4[...] + cr4[...]
    e4 = (e4s, e4r, e4_s, e4_r, 8, hz, by_hz)
    exchange(*e4)
    finish(*e4)
    ogain[...] = total(e4r, 8)[0:1]
    for c in outs:
        c.wait()

    for wait in sent:
        wait()


def results(gq, gdoc, ggain, loss, oq, od, ogain, oloss, sems):
    pairs = ((gq, oq), (gdoc, od), (ggain, ogain), (loss, oloss))
    copies = [pltpu.make_async_copy(a, b, sems.at[i]) for i, (a, b) in enumerate(pairs)]
    for c in copies:
        c.start()
    for c in copies:
        c.wait()


def shards(query_states, doc_states, gain, positives):
    vm = pl.BlockSpec(memory_space=pltpu.VMEM)
    hbm = pl.BlockSpec(memory_space=pl.ANY)
    S = pltpu.VMEM
    dma = lambda n: pltpu.SemaphoreType.DMA((n,))
    pair = lambda n: [dma(n), dma(n)]
    scratch = [
        S((ROWS, FEATS), bf16), S((ROWS, FEATS), bf16),
        S((ROWS, FEATS), bf16), S((ROWS, FEATS), bf16), S((1, FULL), f32),
        S((2 * ROWS, FULL), bf16), S((2 * ROWS + TILE, FULL), bf16), S((TAKE, FULL), bf16),
        S((ROWS + TILE, 128), f32), S((ROWS, 128), f32),
        S((2 * ROWS, TAKE), f32), S((8, TAKE), f32), S((2 * ROWS, TAKE), bf16), S((TAKE, 2 * ROWS), bf16),
        S((8, FEATS), f32), S((TP, 8, FEATS), f32),
        S((8, TAKE), f32), S((8, TAKE), f32), S((8, 8, TAKE), f32),
        S((8, ROWS), f32), S((TP, 8, ROWS), f32),
        S((8, ROWS), f32), S((TP, 8, ROWS), f32),
        S((8, FEATS), f32), S((8, FEATS), f32), S((8, FEATS), f32), S((8, 8, FEATS), f32),
        S((DP, 8, 128), f32), S((8, 128), f32),
        S((TAKE + TILE, FULL), bf16), S((8, 3 * TILE, FULL), bf16),
        S((7, 3 * TILE, FULL), bf16), S((7, 3 * TILE, FULL), bf16),
        S((ROWS // 2, WIDE), f32), S((ROWS // 2, WIDE), f32),
        S((ROWS, WIDE), bf16), S((ROWS, WIDE), bf16), S((ROWS, WIDE), bf16),
        S((2, ROWS // 2, WIDE), bf16), S((ROWS, WIDE), bf16), S((ROWS, WIDE), bf16),
        S((ROWS, WIDE), f32), S((ROWS, FEATS), bf16), S((ROWS, FEATS), bf16),
        S((TP, 3 * TILE, FEATS), bf16), S((ROWS, FEATS), bf16), S((ROWS, TAKE), bf16),
        S((8, TAKE), f32), S((8, TAKE), f32), S((8, TAKE), f32), S((8, 8, TAKE), f32),
        S((ROWS, FEATS), bf16), S((ROWS, FEATS), bf16),
    ]
    sems = (
        pair(2 * NCH) + pair(TP) + pair(8) + pair(TP) + pair(TP) + pair(8) + pair(8)
        + pair(8 * NCH) + pair(64) + [dma(4)] + pair(32) + pair(32) + pair(7) + pair(TP) + pair(8)
        + pair(4) + [dma(2)]
    )
    gq, gdoc, ggain, loss = pl.pallas_call(
        step,
        name="infonce_step",
        out_shape=(
            jax.ShapeDtypeStruct((ROWS, FEATS), bf16),
            jax.ShapeDtypeStruct((ROWS, FEATS), bf16),
            jax.ShapeDtypeStruct((1, FEATS), f32),
            jax.ShapeDtypeStruct((1, 1), f32),
        ),
        in_specs=[hbm, hbm, vm, vm],
        out_specs=(hbm, hbm, vm, vm),
        scratch_shapes=scratch + sems,
        compiler_params=pltpu.CompilerParams(
            collective_id=0, has_side_effects=True, vmem_limit_bytes=56 * 2**20
        ),
        cost_estimate=pl.CostEstimate(
            flops=7_000_000_000, bytes_accessed=3_000_000, transcendentals=1_000_000
        ),
    )(query_states, doc_states, gain[None, :], positives[None, :])
    gq, gdoc, ggain, loss = pl.pallas_call(
        results,
        name="results",
        out_shape=(
            jax.ShapeDtypeStruct((ROWS, FEATS), bf16),
            jax.ShapeDtypeStruct((ROWS, FEATS), bf16),
            jax.ShapeDtypeStruct((1, FEATS), f32),
            jax.ShapeDtypeStruct((1, 1), f32),
        ),
        in_specs=[hbm] * 4,
        out_specs=(hbm,) * 4,
        scratch_shapes=[dma(4)],
    )(gq, gdoc, ggain, loss)
    return gq, gdoc, ggain[0], loss[0, 0]


def solution(mesh):
    return jax.shard_map(
        shards,
        mesh=mesh,
        in_specs=(P("dp", "tensor"), P("dp", "tensor"), P("tensor"), P("dp")),
        out_specs=(P("dp", "tensor"), P("dp", "tensor"), P("tensor"), P()),
        check_vma=False,
    )
```

```python
import functools

import jax
import jax.numpy as jnp
from jax import lax
from jax.experimental import pallas as pl
from jax.experimental.pallas import tpu as pltpu
from jax.sharding import PartitionSpec as P

eps_len = 1e-06
inv_temp = 100.0
masked = -1e30

MESH = pl.DeviceIdType.MESH
HIGH = lax.Precision.HIGHEST
f32 = jnp.float32
bf16 = jnp.bfloat16

DP = 16
TP = 8
ROWS = 288
FEATS = 448
WIDE = 2 * FEATS
FULL = TP * FEATS
PAIRS = DP * ROWS
TAKE = DP * ROWS // TP
TILE = 16
CHUNK = 96
NCH = ROWS // CHUNK
HALF = CHUNK // 2


def step(
    hq, hd, gain, pos,
    oq, od, ogain, oloss,
    xq, xd, pq, pd, gfull, raw, emb, qi, invq, invd, logits, stat, wts, wtt,
    e0s, e0r, cs1, cr1, e1s, e1r, e2s, e2r, e3s, e3r, cs4, cr4, e4s, e4r, epr, posv,
    partq, sibr, sendq, recvq, acc1, acc2, pd2, pd1, pdm, halfs, r1, r2, gd, xsend, xrecv,
    asend, arecv, pick, cs5, cr5, e5s, e5r, outq, outd,
    x_s, x_r, e0_s, e0_r, e1_s, e1_r, e2_s, e2_r, e3_s, e3_r, e4_s, e4_r, ep_s, ep_r,
    y_s, y_r, a_s, a_r, loc, b_s, b_r, u_s, u_r, g_s, g_r, t_s, t_r, e5_s, e5_r, c_s, c_r, io,
):
    d = lax.axis_index("dp")
    t = lax.axis_index("tensor")
    hz = d // 2
    core = d % 2
    zc = hz % 4
    d4 = (hz // 4) * 2 + core
    low = t // 4
    y = t % 4
    xh = hz // 4
    sources = [pltpu.make_async_copy(hq, xq, io.at[0]), pltpu.make_async_copy(hd, xd, io.at[1])]
    for c in sources:
        c.start()
    third = t // 2
    sibling = (hz * 2 + (1 - core), t)
    partner = (d, (t + 4) % TP)
    up = (d, low * 4 + (y + 1) % 4)
    down = (d, low * 4 + (y + 3) % 4)
    zup = ((xh * 4 + (zc + 1) % 4) * 2 + core, t)
    zdown = ((xh * 4 + (zc + 3) % 4) * 2 + core, t)
    across = ((hz + 4) % 8 * 2 + core, t)

    sent = []

    def copy(src, dst, ss, rs, dev):
        return pltpu.make_async_remote_copy(
            src_ref=src, dst_ref=dst, send_sem=ss, recv_sem=rs, device_id=dev, device_id_type=MESH
        )

    def lanes(block):
        return pl.ds(pl.multiple_of(block * WIDE, 128), WIDE)

    def rows_at(tile, n):
        return pl.ds(pl.multiple_of(tile * TILE, TILE), n)

    def place(hz_s, core_s, tens):
        q = (hz_s // 4) * 2 + core_s
        e = tens // 2
        return (hz_s % 4) * 9 + 2 * q + jnp.where(q > e, 1, 0)

    def begin(q, tens):
        return 2 * tens + jnp.clip(tens - 2 * q, 0, 2)

    def sized(extra, fn):
        @pl.when(extra)
        def _():
            fn(3 * TILE)

        @pl.when(jnp.logical_not(extra))
        def _():
            fn(2 * TILE)

    barrier = pltpu.get_barrier_semaphore()

    @pl.loop(1, TP)
    def _(k):
        pl.semaphore_signal(barrier, inc=1, device_id=(d, (t + k) % TP), device_id_type=MESH)

    @pl.loop(1, 8)
    def _(k):
        pl.semaphore_signal(
            barrier, inc=1, device_id=((hz + k) % 8 * 2 + core, t), device_id_type=MESH
        )

    pl.semaphore_signal(barrier, inc=1, device_id=sibling, device_id_type=MESH)
    def fold(ref, row, vec):
        for k in range(-(-vec.shape[1] // 128)):
            part = vec[:, 128 * k : 128 * (k + 1)]
            ref[row + k : row + k + 1, 0 : part.shape[1]] = part

    def unfold(tile, row, size):
        return jnp.concatenate(
            [
                tile[row + k : row + k + 1, 0 : min(128, size - 128 * k)]
                for k in range(-(-size // 128))
            ],
            axis=1,
        )

    def to_lanes(col):
        return jnp.transpose(jnp.broadcast_to(col, (ROWS, 128)))[:8]

    def to_rows(vec):
        return jnp.transpose(jnp.broadcast_to(vec, (128, ROWS)))

    sub8 = lambda n: lax.broadcasted_iota(jnp.int32, (8, n), 0)

    posv[...] = jnp.zeros_like(posv)
    for seg in range(3):
        at = slice(128 * seg, min(128 * (seg + 1), ROWS))
        width = at.stop - at.start
        posv[seg : seg + 1, 0:width] = (pos[:, at] // 128).astype(f32)
        posv[3 + seg : 4 + seg, 0:width] = (pos[:, at] % 128).astype(f32)
    pl.semaphore_wait(barrier, TP + 7)

    def xcopy(i):
        src, dst = (hq, pq) if i < NCH else (hd, pd)
        part = pl.ds((i % NCH) * CHUNK, CHUNK)
        return copy(src.at[part], dst.at[part], x_s.at[i], x_r.at[i], partner)

    def begun(c):
        c.start()
        sent.append(c.wait_send)

    def exchange(src, recv, ss, rs, size, me, dev):
        @pl.loop(1, size)
        def _(k):
            copy(src, recv.at[me], ss.at[k], rs.at[me], dev((me + k) % size)).start()

        @sent.append
        def _():
            @pl.loop(1, size)
            def _(k):
                copy(src, recv.at[me], ss.at[k], rs.at[me], dev((me + k) % size)).wait_send()

    def finish(src, recv, ss, rs, size, me, dev):
        recv[me] = src[...]

        @pl.loop(1, size)
        def _(k):
            s = (me + k) % size
            copy(src, recv.at[s], ss.at[k], rs.at[s], dev(s)).wait_recv()

    by_tensor = lambda s: (d, s)
    by_hz = lambda s: (s * 2 + core, t)

    def total(recv, size):
        acc = recv[0]
        for s in range(1, size):
            acc = acc + recv[s]
        return acc

    e0 = (e0s, e0r, e0_s, e0_r, TP, t, by_tensor)
    begun(xcopy(0))
    for c in sources:
        c.wait()
    nq = xq[...].astype(f32) * gain[...]
    nd = xd[...].astype(f32) * gain[...]
    lq = to_lanes(jnp.sum(nq * nq, axis=1, keepdims=True))
    ld = to_lanes(jnp.sum(nd * nd, axis=1, keepdims=True))
    e0s[...] = jnp.broadcast_to(gain[...], (8, FEATS))
    e0s[0:1, 0:ROWS] = lq[0:1]
    e0s[1:2, 0:ROWS] = ld[0:1]
    exchange(*e0)
    for i in range(1, 2 * NCH):
        begun(xcopy(i))

    mine = begin(d4, t)
    here = place(hz, core, t)
    extra = d4 == third

    def pack(a, k):
        own, part, base = (xq, pq, ROWS) if a == 0 else (xd, pd, 0)
        xcopy(a * NCH + k).wait_recv()
        rs = pl.ds(k * CHUNK, CHUNK)
        eo = own[rs].astype(f32)
        ep = part[rs].astype(f32)
        left = jnp.where(low == 0, eo, ep)
        right = jnp.where(low == 0, ep, eo)
        raw[pl.ds(base + k * CHUNK, CHUNK), lanes(y)] = jnp.concatenate(
            [left, right], axis=1
        ).astype(bf16)

    def normalise(a, k, block):
        inverse, base = (invq, ROWS) if a == 0 else (invd, 0)
        for part in range(2):
            rs = k * CHUNK + part * HALF
            scale = inverse[pl.ds(rs, HALF), 0:1]
            at = pl.ds(base + rs, HALF)
            cs = lanes(block)
            emb[at, cs] = (raw[at, cs].astype(f32) * gfull[:, cs] * scale).astype(bf16)

    def ycopy(a, k, kind):
        base = (ROWS if a == 0 else 0) + k * CHUNK
        i = (a * NCH + k) * 4 + kind
        if kind < 2:
            at, dev, block = pl.ds(base, CHUNK), (up, down)[kind], y
        elif kind == 2:
            at, dev, block = pl.ds(base, HALF), up, (y + 3) % 4
        else:
            at, dev, block = pl.ds(base + HALF, HALF), down, (y + 1) % 4
        ref = raw.at[at, lanes(block)]
        return copy(ref, ref, y_s.at[i], y_r.at[i], dev)

    def yrecv(a, k, kind):
        base = (ROWS if a == 0 else 0) + k * CHUNK
        i = (a * NCH + k) * 4 + kind
        at = pl.ds(base, CHUNK) if kind < 2 else pl.ds(base + (kind - 2) * HALF, HALF)
        block = ((y + 3) % 4, (y + 1) % 4, (y + 2) % 4, (y + 2) % 4)[kind]
        ref = raw.at[at, lanes(block)]
        copy(ref, ref, y_s.at[i], y_r.at[i], up).wait_recv()

    def source(s):
        return (xh + s // 4) % 2 * 4 + (zc + 4 - s % 4) % 4

    def gives(s, core_s):
        return (xh + s // 4) % 2 * 2 + core_s == third

    def device(s):
        return ((xh + s // 4) % 2 * 8 + (zc + s % 4) % 4 * 2 + core, t)

    def spot(i, s, core_s, n):
        block = (y + (0, 3, 1, 2)[i]) % 4
        return qi.at[rows_at(place(source(s), core_s, t), n), lanes(block)]

    def own_rows(i, n):
        block = (y + (0, 3, 1, 2)[i]) % 4
        return emb.at[pl.ds(pl.multiple_of(ROWS + mine * TILE, TILE), n), lanes(block)]

    def give_own(i, slot, dev):
        def c(n):
            return copy(
                own_rows(i, n), spot(i, 0, core, n), a_s.at[i * 16 + slot], a_r.at[i * 16 + slot], dev
            )

        sized(extra, lambda n: c(n).start())
        sent.append(lambda: sized(extra, lambda n: c(n).wait_send()))

    def pass_on(i, s, slot, dev):
        def c(n):
            ref = spot(i, s, core, n)
            return copy(ref, ref, a_s.at[i * 16 + slot], a_r.at[i * 16 + slot], dev)

        sized(gives(s, core), lambda n: c(n).start())
        sent.append(lambda: sized(gives(s, core), lambda n: c(n).wait_send()))

    def agot(i, s):
        def c(n):
            ref = spot(i, s, core, n)
            copy(ref, ref, a_s.at[i * 16 + s], a_r.at[i * 16 + s], sibling).wait_recv()

        sized(gives(s, core), c)

    def alocal(i, n):
        return pltpu.make_async_copy(own_rows(i, n), spot(i, 0, core, n), loc.at[i])

    def astart(i):
        for s in (1, 3, 2, 4) if i < 3 else (4, 1, 3, 2, 5, 7, 6):
            give_own(i, s, device(s))
        give_own(i, 8, sibling)
        sized(extra, lambda n: alocal(i, n).start())

    def amid(i):
        agot(i, 4)
        if i < 3:
            for s in (1, 3, 2):
                pass_on(i, 4, 4 + s, device(s))
        pass_on(i, 4, 12, sibling)
        for s in (1, 3, 2):
            agot(i, s)
            pass_on(i, s, 8 + s, sibling)

    def alast(i):
        for s in (5, 7, 6):
            agot(i, s)
            pass_on(i, s, 8 + s, sibling)

    def afinish(i):
        sized(extra, lambda n: alocal(i, n).wait())

        @pl.loop(0, 8)
        def _(s):
            def c(n):
                ref = spot(i, s, 1 - core, n)
                copy(ref, ref, a_s.at[i * 16], a_r.at[i * 16 + 8 + s], sibling).wait_recv()

            sized(gives(s, 1 - core), c)

    for k in range(NCH):
        pack(0, k)
        begun(ycopy(0, k, 0))
        begun(ycopy(0, k, 1))
    finish(*e0)
    inv = lax.rsqrt(total(e0r, TP)[:, 0:ROWS] + eps_len)
    invq[0:ROWS] = to_rows(inv[0:1])
    invd[...] = to_rows(inv[1:2])
    for b in range(4):
        gfull[:, b * WIDE : (b + 1) * WIDE] = jnp.concatenate(
            [e0r[b, 2:3], e0r[4 + b, 2:3]], axis=1
        )
    for k in range(NCH):
        normalise(0, k, y)
    astart(0)
    ep = (posv, epr, ep_s, ep_r, 8, hz, by_hz)
    exchange(*ep)
    for k in range(NCH):
        yrecv(0, k, 0)
        begun(ycopy(0, k, 2))
        yrecv(0, k, 1)
        begun(ycopy(0, k, 3))
    for k in range(NCH):
        pack(1, k)
        begun(ycopy(1, k, 0))
        begun(ycopy(1, k, 1))
    for k in range(NCH):
        normalise(0, k, (y + 3) % 4)
        normalise(0, k, (y + 1) % 4)
    astart(1)
    astart(2)
    amid(0)
    for k in range(NCH):
        yrecv(0, k, 2)
        yrecv(0, k, 3)
        normalise(0, k, (y + 2) % 4)
    astart(3)
    for k in range(NCH):
        normalise(1, k, y)
    alast(0)
    amid(1)
    amid(2)

    def docs_on(k):
        yrecv(1, k, 0)
        begun(ycopy(1, k, 2))
        yrecv(1, k, 1)
        begun(ycopy(1, k, 3))

    docs_on(0)
    alast(1)
    docs_on(1)
    alast(2)
    docs_on(2)
    for k in range(NCH):
        normalise(1, k, (y + 3) % 4)
        normalise(1, k, (y + 1) % 4)
    amid(3)
    alast(3)
    for i in range(4):
        afinish(i)

    lane_p = lax.broadcasted_iota(jnp.int32, (1, TAKE), 1)
    tile_p = lane_p // TILE
    w_p = tile_p % 9
    q_p = jnp.where(
        w_p < 2 * third, w_p // 2, jnp.where(w_p <= 2 * third + 2, third, (w_p - 1) // 2)
    )
    off_p = w_p - 2 * q_p - jnp.where(q_p > third, 1, 0)
    dev_p = (q_p // 2) * 8 + (tile_p // 9) * 2 + q_p % 2
    row_p = dev_p * ROWS + (begin(q_p, t) + off_p) * TILE + lane_p % TILE
    finish(*ep)
    epc = copy(epr.at[pl.ds(0, 8)], epr.at[pl.ds(8, 8)], c_s.at[0], c_r.at[0], sibling)
    begun(epc)

    stat[0:1] = jnp.full((1, TAKE), masked, f32)
    stat[1:8] = jnp.zeros((7, TAKE), f32)

    def product(rows, cs):
        return lax.dot_general(
            emb[rows, cs], qi[:, cs], (((1,), (1,)), ((), ())), preferred_element_type=f32
        )

    def statistics(s):
        old = stat[0:1]
        new = jnp.maximum(old, jnp.max(s, axis=0, keepdims=True))
        stat[0:1] = new
        stat[1:2] = stat[1:2] * jnp.exp(old - new) + jnp.sum(
            jnp.exp(s - new), axis=0, keepdims=True
        )

    own_j = d * ROWS + lax.broadcasted_iota(jnp.int32, (ROWS, TAKE), 0)
    logits[ROWS:] = product(pl.ds(ROWS, ROWS), slice(None))
    logits[ROWS:] = jnp.where(own_j == row_p, masked, logits[ROWS:] * inv_temp)
    statistics(logits[ROWS:])
    logits[0:ROWS] = product(pl.ds(0, ROWS), lanes(y))
    for b in (1, 3):
        logits[0:ROWS] = logits[0:ROWS] + product(pl.ds(0, ROWS), lanes((y + b) % 4))

    epc.wait_recv()
    local_p = (begin(q_p, t) + off_p) * TILE + lane_p % TILE
    lane_of = lax.broadcasted_iota(jnp.int32, (128, TAKE), 0)
    spread = jnp.where(lane_of == local_p % 128, 1.0, 0.0).astype(bf16)
    found = jnp.dot(
        epr[...].reshape(DP * 8, 128).astype(bf16), spread, preferred_element_type=f32
    )
    slot_p = jnp.where(dev_p % 2 == core, dev_p // 2, 8 + dev_p // 2) * 8 + local_p // 128
    high = jnp.sum(jnp.where(lane_of == slot_p, found, 0.0), axis=0, keepdims=True)
    rest = jnp.sum(jnp.where(lane_of == slot_p + 3, found, 0.0), axis=0, keepdims=True)
    pos_p = (high * 128.0 + rest).astype(jnp.int32)

    for k in range(NCH):
        yrecv(1, k, 2)
        yrecv(1, k, 3)
        normalise(1, k, (y + 2) % 4)
    logits[0:ROWS] = (logits[0:ROWS] + product(pl.ds(0, ROWS), lanes((y + 2) % 4))) * inv_temp
    stat[2:3] = jnp.sum(jnp.where(own_j == pos_p, logits[0:ROWS], 0.0), axis=0, keepdims=True)
    statistics(logits[0:ROWS])

    sub_t = sub8(TAKE)
    cs1[...] = jnp.zeros_like(cs1)
    for i in range(3):
        fold(cs1, 5 * i, stat[i : i + 1])
    c1 = copy(cs1, cr1, c_s.at[1], c_r.at[1], sibling)
    begun(c1)
    c1.wait_recv()
    top, top_o = cs1[0:5], cr1[0:5]
    top_c = jnp.maximum(top, top_o)
    e1s[0:5] = top_c
    e1s[5:10] = cs1[5:10] * jnp.exp(top - top_c) + cr1[5:10] * jnp.exp(top_o - top_c)
    e1s[10:15] = cs1[10:15] + cr1[10:15]
    e1s[15:16] = jnp.zeros((1, 128), f32)
    e1 = (e1s, e1r, e1_s, e1_r, 8, hz, by_hz)
    exchange(*e1)
    pick[...] = jnp.where(own_j == row_p, 1.0, 0.0).astype(bf16)
    finish(*e1)
    all_top = e1r[0, 0:5]
    for s in range(1, 8):
        all_top = jnp.maximum(all_top, e1r[s, 0:5])
    all_tot = jnp.zeros_like(all_top)
    all_pos = jnp.zeros_like(all_top)
    for s in range(8):
        all_tot = all_tot + e1r[s, 5:10] * jnp.exp(e1r[s, 0:5] - all_top)
        all_pos = all_pos + e1r[s, 10:15]
    lse = unfold(all_top, 0, TAKE) + jnp.log(unfold(all_tot, 0, TAKE))
    loss_part = jnp.sum(lse - unfold(all_pos, 0, TAKE), axis=1, keepdims=True)
    sub_t = sub8(TAKE)

    def own_lanes(vec):
        p1 = vec.astype(bf16).astype(f32)
        p2 = (vec - p1).astype(bf16).astype(f32)
        split = jnp.where(
            sub_t == 0, p1, jnp.where(sub_t == 1, p2, jnp.where(sub_t == 2, vec - p1 - p2, 0.0))
        )
        return jnp.sum(
            lax.dot_general(
                split.astype(bf16), pick[...], (((1,), (1,)), ((), ())),
                preferred_element_type=f32,
            ),
            axis=0, keepdims=True,
        )

    lse_own = own_lanes(lse)
    e2s[...] = jnp.broadcast_to(loss_part, (8, 128))
    fold(e2s, 0, lse_own)
    e2 = (e2s, e2r, e2_s, e2_r, TP, t, by_tensor)
    exchange(*e2)
    wd = (jnp.exp(logits[0:ROWS] - lse) - (own_j == pos_p).astype(f32)) * (1.0 / PAIRS)
    wts[0:ROWS] = wd.astype(bf16)

    def part_d(block):
        return lax.dot_general(
            wts[0:ROWS], qi[:, lanes(block)], (((1,), (0,)), ((), ())),
            preferred_element_type=f32,
        ) * inv_temp

    MID = ROWS // 2
    front, rear = pl.ds(0, MID), pl.ds(MID, MID)
    gc = [
        copy(pd2.at[front], halfs.at[0], g_s.at[0], g_r.at[0], up),
        copy(pd2.at[rear], halfs.at[1], g_s.at[1], g_r.at[1], down),
        copy(pd1.at[rear], r1.at[rear], g_s.at[2], g_r.at[2], up),
        copy(pdm.at[front], r2.at[front], g_s.at[3], g_r.at[3], down),
        copy(pd1.at[front], r1.at[front], g_s.at[4], g_r.at[4], up),
        copy(pdm.at[rear], r2.at[rear], g_s.at[5], g_r.at[5], down),
        copy(xsend, xrecv, g_s.at[6], g_r.at[6], partner),
    ]
    pd2[...] = part_d((y + 2) % 4).astype(bf16)
    begun(gc[0])
    begun(gc[1])
    gd[...] = part_d((y + 1) % 4)
    pd1[rear] = gd[rear].astype(bf16)
    begun(gc[2])
    acc1[...] = gd[front]
    gd[...] = part_d((y + 3) % 4)
    pdm[front] = gd[front].astype(bf16)
    begun(gc[3])
    acc2[...] = gd[rear]
    gd[...] = part_d(y)

    finish(*e2)
    sums = total(e2r, TP)
    oloss[...] = sums[3:4, 0:1] * (1.0 / PAIRS)
    lse_j = to_rows(unfold(sums, 0, ROWS))[:, 0:1]
    wq = (jnp.exp(logits[ROWS:] - lse) * (1.0 / PAIRS)).astype(bf16).astype(f32)
    wt = (jnp.exp(logits[ROWS:] - lse_j) * (1.0 / PAIRS)).astype(bf16).astype(f32)
    wts[ROWS:] = (wq + wt).astype(bf16)
    wtt[...] = jnp.transpose(wts[...])

    weighed = wts[...].astype(f32) * logits[...]
    cs5[...] = jnp.zeros_like(cs5)
    fold(cs5, 0, jnp.sum(weighed, axis=0, keepdims=True))
    c5 = copy(cs5, cr5, c_s.at[3], c_r.at[3], sibling)
    begun(c5)
    e3s[...] = jnp.zeros_like(e3s)
    fold(e3s, 3, to_lanes(jnp.sum(weighed[0:ROWS], axis=1, keepdims=True))[0:1])

    def target(s):
        return (xh + s // 4) % 2 * 4 + (zc + s % 4) % 4

    def cols(f):
        return lanes((y + 1 + f) % 4)

    def bcopy(f, k, n):
        at = rows_at(place(k, 1 - core, t), n)
        return copy(
            partq.at[at, cols(f)], sibr.at[k, pl.ds(0, n), cols(f)],
            b_s.at[f * 8 + k], b_r.at[f * 8 + k], sibling,
        )

    def three(k, core_s):
        return (k // 4) * 2 + core_s == third

    def part_q(f):
        partq[0:TAKE, cols(f)] = (
            jnp.dot(
                wtt[...], emb[0 : 2 * ROWS, cols(f)],
                preferred_element_type=f32,
            ) * inv_temp
        ).astype(bf16)

        @pl.loop(0, 8)
        def _(k):
            sized(three(k, 1 - core), lambda n: bcopy(f, k, n).start())

        @sent.append
        def _():
            @pl.loop(0, 8)
            def _(k):
                sized(three(k, 1 - core), lambda n: bcopy(f, k, n).wait_send())

    N3 = 3 * TILE

    def both(f, s):
        k = target(s)
        sized(three(k, core), lambda n: bcopy(f, k, n).wait_recv())
        cs = cols(f)
        return partq[rows_at(place(k, core, t), N3), cs].astype(f32) + sibr[k, :, cs].astype(f32)

    FLOW = ((2, zup), (6, zdown), (5, zup), (3, zdown), (1, zup), (7, zdown), (4, across))

    def ucopy(f, i, n):
        cs = cols(f)
        return copy(
            sendq.at[i, pl.ds(0, n), cs], recvq.at[i, pl.ds(0, n), cs],
            u_s.at[f * 8 + i], u_r.at[f * 8 + i], FLOW[i][1],
        )

    def usend(f, i, value):
        sendq[i, :, cols(f)] = value.astype(bf16)
        far = three(target(FLOW[i][0]), core)
        sized(far, lambda n: ucopy(f, i, n).start())
        sent.append(lambda: sized(far, lambda n: ucopy(f, i, n).wait_send()))

    def uwait(f, i, s):
        sized(three(target(s), core), lambda n: ucopy(f, i, n).wait_recv())
        return recvq[i, :, cols(f)].astype(f32)

    def q_far(f):
        usend(f, 0, both(f, 2))
        usend(f, 1, both(f, 6))
        usend(f, 2, both(f, 5))
        usend(f, 3, both(f, 3))

    def q_near(f):
        usend(f, 4, both(f, 1) + uwait(f, 0, 1))
        usend(f, 5, both(f, 7) + uwait(f, 1, 7))

    def q_across(f):
        usend(f, 6, both(f, 4) + uwait(f, 2, 4) + uwait(f, 5, 4))

    def tcopy(f, far, n):
        to = (y + 1 + f) % 4 + 4 * ((low + far) % 2)
        return copy(
            asend.at[to, pl.ds(0, n)], arecv.at[rows_at(mine, n)],
            t_s.at[f * 2 + far], t_r.at[f * 2 + far], (d, to),
        )

    def trecv(f, far):
        s = (y + 3 - f) % 4 + 4 * ((low + far) % 2)
        at = lambda n: arecv.at[rows_at(begin(d4, s), n)]
        sized(
            d4 == s // 2,
            lambda n: copy(at(n), at(n), t_s.at[0], t_r.at[f * 2 + far], (d, s)).wait_recv(),
        )

    def direct(f, s, n):
        cs = cols(f)
        return copy(
            sendq.at[s - 1, pl.ds(0, n), cs], recvq.at[s - 1, pl.ds(0, n), cs],
            u_s.at[f * 8 + s - 1], u_r.at[f * 8 + s - 1], device(s),
        )

    def q_direct(f):
        for s in (5, 7, 6, 4, 2, 1, 3):
            sendq[s - 1, :, cols(f)] = both(f, s).astype(bf16)
            far = three(target(s), core)
            sized(far, lambda n: direct(f, s, n).start())
            sent.append(
                lambda s=s, far=far: sized(far, lambda n: direct(f, s, n).wait_send())
            )

    def q_own(f):
        if f < 3:
            g = both(f, 0) + uwait(f, 3, 0) + uwait(f, 4, 0) + uwait(f, 6, 0)
        else:
            g = both(f, 0)
            for s in range(1, 8):
                sized(extra, lambda n: direct(f, s, n).wait_recv())
                g = g + recvq[s - 1, :, cols(f)].astype(f32)
        fb = (y + 1 + f) % 4
        asend[fb] = g[:, :FEATS].astype(bf16)
        asend[4 + fb] = g[:, FEATS:].astype(bf16)
        for far in range(2):
            if f < 3 or far == 1:
                sized(extra, lambda n: tcopy(f, far, n).start())
                sent.append(
                    lambda far=far: sized(extra, lambda n: tcopy(f, far, n).wait_send())
                )

    part_q(0)
    part_q(1)
    q_far(0)
    c5.wait_recv()
    e5s[...] = cs5[...] + cr5[...]
    e5 = (e5s, e5r, e5_s, e5_r, 8, hz, by_hz)
    exchange(*e5)
    part_q(2)
    q_far(1)
    gc[0].wait_recv()
    pd1[front] = (acc1[...] + halfs[0].astype(f32)).astype(bf16)
    begun(gc[4])
    gc[1].wait_recv()
    pdm[rear] = (acc2[...] + halfs[1].astype(f32)).astype(bf16)
    begun(gc[5])
    q_far(2)
    part_q(3)
    q_near(0)
    q_near(1)
    q_near(2)
    q_direct(3)
    finish(*e5)
    fold(e3s, 0, own_lanes(unfold(total(e5r, 8), 0, TAKE)))
    e3 = (e3s, e3r, e3_s, e3_r, TP, t, by_tensor)
    exchange(*e3)
    q_across(0)
    for i in range(2, 6):
        gc[i].wait_recv()
    gd[...] = gd[...] + r1[...].astype(f32) + r2[...].astype(f32)
    xsend[...] = jnp.where(low == 0, gd[:, FEATS:], gd[:, :FEATS]).astype(bf16)
    begun(gc[6])
    q_across(1)
    q_own(0)
    q_across(2)
    q_own(1)

    gc[6].wait_recv()
    gd[:, 0:FEATS] = jnp.where(low == 0, gd[:, :FEATS], gd[:, FEATS:]) + xrecv[...].astype(f32)
    q_own(2)
    q_own(3)

    def tlocal(n):
        arecv[rows_at(mine, n)] = asend[t, pl.ds(0, n)]

    sized(extra, tlocal)

    finish(*e3)
    dots = total(e3r, TP)
    col = to_rows(unfold(dots, 3, ROWS))[:, 0:1]
    iv = invd[:, 0:1]
    h = xd[...].astype(f32)
    gx = iv * gd[:, 0:FEATS] - h * gain[...] * (iv * iv * col)
    outd[...] = (gx * gain[...]).astype(bf16)
    outs = [pltpu.make_async_copy(outd, od, io.at[0]), pltpu.make_async_copy(outq, oq, io.at[1])]
    outs[0].start()
    gg = jnp.sum(gx * h, axis=0, keepdims=True)

    for f in range(4):
        for far in range(2):
            if f < 3 or far == 1:
                trecv(f, far)

    col = to_rows(unfold(dots, 0, ROWS))[:, 0:1]
    h = xq[...].astype(f32)
    iv = invq[0:ROWS, 0:1]
    gx = iv * arecv[...].astype(f32) - h * gain[...] * (iv * iv * col)
    gg = gg + jnp.sum(gx * h, axis=0, keepdims=True)
    cs4[...] = jnp.zeros_like(cs4)
    fold(cs4, 0, gg)
    c4 = copy(cs4, cr4, c_s.at[2], c_r.at[2], sibling)
    begun(c4)
    outq[...] = (gx * gain[...]).astype(bf16)
    outs[1].start()
    c4.wait_recv()
    e4s[...] = cs4[...] + cr4[...]
    e4 = (e4s, e4r, e4_s, e4_r, 8, hz, by_hz)
    exchange(*e4)
    finish(*e4)
    ogain[...] = unfold(total(e4r, 8), 0, FEATS)
    for c in outs:
        c.wait()

    for wait in sent:
        wait()


def results(gq, gdoc, ggain, loss, oq, od, ogain, oloss):
    oq[...] = gq[...]
    od[...] = gdoc[...]
    ogain[...] = ggain[...]
    oloss[...] = loss[...]


def shards(query_states, doc_states, gain, positives):
    vm = pl.BlockSpec(memory_space=pltpu.VMEM)
    hbm = pl.BlockSpec(memory_space=pl.ANY)
    S = pltpu.VMEM
    dma = lambda n: pltpu.SemaphoreType.DMA((n,))
    pair = lambda n: [dma(n), dma(n)]
    scratch = [
        S((ROWS, FEATS), bf16), S((ROWS, FEATS), bf16),
        S((ROWS, FEATS), bf16), S((ROWS, FEATS), bf16), S((1, FULL), f32),
        S((2 * ROWS, FULL), bf16), S((2 * ROWS + TILE, FULL), bf16), S((TAKE, FULL), bf16),
        S((ROWS + TILE, 128), f32), S((ROWS, 128), f32),
        S((2 * ROWS, TAKE), f32), S((8, TAKE), f32), S((2 * ROWS, TAKE), bf16), S((TAKE, 2 * ROWS), bf16),
        S((8, FEATS), f32), S((TP, 8, FEATS), f32),
        S((16, 128), f32), S((16, 128), f32), S((16, 128), f32), S((8, 16, 128), f32),
        S((8, 128), f32), S((TP, 8, 128), f32),
        S((8, 128), f32), S((TP, 8, 128), f32),
        S((8, 128), f32), S((8, 128), f32), S((8, 128), f32), S((8, 8, 128), f32),
        S((DP, 8, 128), f32), S((8, 128), f32),
        S((TAKE + TILE, FULL), bf16), S((8, 3 * TILE, FULL), bf16),
        S((7, 3 * TILE, FULL), bf16), S((7, 3 * TILE, FULL), bf16),
        S((ROWS // 2, WIDE), f32), S((ROWS // 2, WIDE), f32),
        S((ROWS, WIDE), bf16), S((ROWS, WIDE), bf16), S((ROWS, WIDE), bf16),
        S((2, ROWS // 2, WIDE), bf16), S((ROWS, WIDE), bf16), S((ROWS, WIDE), bf16),
        S((ROWS, WIDE), f32), S((ROWS, FEATS), bf16), S((ROWS, FEATS), bf16),
        S((TP, 3 * TILE, FEATS), bf16), S((ROWS, FEATS), bf16), S((ROWS, TAKE), bf16),
        S((8, 128), f32), S((8, 128), f32), S((8, 128), f32), S((8, 8, 128), f32),
        S((ROWS, FEATS), bf16), S((ROWS, FEATS), bf16),
    ]
    sems = (
        pair(2 * NCH) + pair(TP) + pair(8) + pair(TP) + pair(TP) + pair(8) + pair(8)
        + pair(8 * NCH) + pair(64) + [dma(4)] + pair(32) + pair(32) + pair(7) + pair(TP) + pair(8)
        + pair(4) + [dma(2)]
    )
    gq, gdoc, ggain, loss = pl.pallas_call(
        step,
        name="infonce_step",
        out_shape=(
            jax.ShapeDtypeStruct((ROWS, FEATS), bf16),
            jax.ShapeDtypeStruct((ROWS, FEATS), bf16),
            jax.ShapeDtypeStruct((1, FEATS), f32),
            jax.ShapeDtypeStruct((1, 1), f32),
        ),
        in_specs=[hbm, hbm, vm, vm],
        out_specs=(hbm, hbm, vm, vm),
        scratch_shapes=scratch + sems,
        compiler_params=pltpu.CompilerParams(
            collective_id=0, has_side_effects=True, vmem_limit_bytes=56 * 2**20
        ),
        cost_estimate=pl.CostEstimate(
            flops=7_000_000_000, bytes_accessed=3_000_000, transcendentals=1_000_000
        ),
    )(query_states, doc_states, gain[None, :], positives[None, :])
    gq, gdoc, ggain, loss = pl.pallas_call(
        results,
        name="results",
        out_shape=(
            jax.ShapeDtypeStruct((ROWS, FEATS), bf16),
            jax.ShapeDtypeStruct((ROWS, FEATS), bf16),
            jax.ShapeDtypeStruct((1, FEATS), f32),
            jax.ShapeDtypeStruct((1, 1), f32),
        ),
        in_specs=[vm] * 4,
        out_specs=(vm,) * 4,
    )(gq, gdoc, ggain, loss)
    return gq, gdoc, ggain[0], loss[0, 0]


def solution(mesh):
    return jax.shard_map(
        shards,
        mesh=mesh,
        in_specs=(P("dp", "tensor"), P("dp", "tensor"), P("tensor"), P("dp")),
        out_specs=(P("dp", "tensor"), P("dp", "tensor"), P("tensor"), P()),
        check_vma=False,
    )
```

```python
import functools

import jax
import jax.numpy as jnp
from jax import lax
from jax.experimental import pallas as pl
from jax.experimental.pallas import tpu as pltpu
from jax.sharding import PartitionSpec as P

eps_len = 1e-06
inv_temp = 100.0
masked = -1e30

MESH = pl.DeviceIdType.MESH
HIGH = lax.Precision.HIGHEST
f32 = jnp.float32
bf16 = jnp.bfloat16

DP = 16
TP = 8
ROWS = 288
FEATS = 448
WIDE = 2 * FEATS
FULL = TP * FEATS
PAIRS = DP * ROWS
TAKE = DP * ROWS // TP
TILE = 16
CHUNK = 96
NCH = ROWS // CHUNK
HALF = CHUNK // 2


def step(
    hq, hd, gain, pos,
    oq, od, ogain, oloss,
    xq, xd, pq, pd, gfull, raw, emb, qi, invq, invd, logits, stat, wts, wtt,
    e0s, e0r, cs1, cr1, e1s, e1r, e2s, e2r, e3s, e3r, cs4, cr4, e4s, e4r, epr, posv,
    partq, sibr, sendq, recvq, acc1, acc2, pd2, pd1, pdm, halfs, r1, r2, gd, xsend, xrecv,
    asend, arecv, pick, cs5, cr5, e5s, e5r, outq, outd,
    x_s, x_r, e0_s, e0_r, e1_s, e1_r, e2_s, e2_r, e3_s, e3_r, e4_s, e4_r, ep_s, ep_r,
    y_s, y_r, a_s, a_r, loc, b_s, b_r, u_s, u_r, g_s, g_r, t_s, t_r, e5_s, e5_r, c_s, c_r, io,
):
    d = lax.axis_index("dp")
    t = lax.axis_index("tensor")
    hz = d // 2
    core = d % 2
    zc = hz % 4
    d4 = (hz // 4) * 2 + core
    low = t // 4
    y = t % 4
    xh = hz // 4
    sources = [pltpu.make_async_copy(hq, xq, io.at[0]), pltpu.make_async_copy(hd, xd, io.at[1])]
    for c in sources:
        c.start()
    third = t // 2
    sibling = (hz * 2 + (1 - core), t)
    partner = (d, (t + 4) % TP)
    up = (d, low * 4 + (y + 1) % 4)
    down = (d, low * 4 + (y + 3) % 4)
    zup = ((xh * 4 + (zc + 1) % 4) * 2 + core, t)
    zdown = ((xh * 4 + (zc + 3) % 4) * 2 + core, t)
    across = ((hz + 4) % 8 * 2 + core, t)

    sent = []

    def copy(src, dst, ss, rs, dev):
        return pltpu.make_async_remote_copy(
            src_ref=src, dst_ref=dst, send_sem=ss, recv_sem=rs, device_id=dev, device_id_type=MESH
        )

    def lanes(block):
        return pl.ds(pl.multiple_of(block * WIDE, 128), WIDE)

    def rows_at(tile, n):
        return pl.ds(pl.multiple_of(tile * TILE, TILE), n)

    def place(hz_s, core_s, tens):
        q = (hz_s // 4) * 2 + core_s
        e = tens // 2
        return (hz_s % 4) * 9 + 2 * q + jnp.where(q > e, 1, 0)

    def begin(q, tens):
        return 2 * tens + jnp.clip(tens - 2 * q, 0, 2)

    def sized(extra, fn):
        @pl.when(extra)
        def _():
            fn(3 * TILE)

        @pl.when(jnp.logical_not(extra))
        def _():
            fn(2 * TILE)

    barrier = pltpu.get_barrier_semaphore()

    @pl.loop(1, TP)
    def _(k):
        pl.semaphore_signal(barrier, inc=1, device_id=(d, (t + k) % TP), device_id_type=MESH)

    @pl.loop(1, 8)
    def _(k):
        pl.semaphore_signal(
            barrier, inc=1, device_id=((hz + k) % 8 * 2 + core, t), device_id_type=MESH
        )

    pl.semaphore_signal(barrier, inc=1, device_id=sibling, device_id_type=MESH)
    def fold(ref, row, vec):
        for k in range(-(-vec.shape[1] // 128)):
            part = vec[:, 128 * k : 128 * (k + 1)]
            ref[row + k : row + k + 1, 0 : part.shape[1]] = part

    def unfold(tile, row, size):
        return jnp.concatenate(
            [
                tile[row + k : row + k + 1, 0 : min(128, size - 128 * k)]
                for k in range(-(-size // 128))
            ],
            axis=1,
        )

    def to_lanes(col):
        return jnp.transpose(jnp.broadcast_to(col, (ROWS, 128)))[:8]

    def to_rows(vec):
        return jnp.transpose(jnp.broadcast_to(vec, (128, ROWS)))

    sub8 = lambda n: lax.broadcasted_iota(jnp.int32, (8, n), 0)

    posv[...] = jnp.zeros_like(posv)
    for seg in range(3):
        at = slice(128 * seg, min(128 * (seg + 1), ROWS))
        width = at.stop - at.start
        posv[seg : seg + 1, 0:width] = (pos[at] // 128).astype(f32)[None, :]
        posv[3 + seg : 4 + seg, 0:width] = (pos[at] % 128).astype(f32)[None, :]
    pl.semaphore_wait(barrier, TP + 7)

    def xcopy(i):
        src, dst = (hq, pq) if i < NCH else (hd, pd)
        part = pl.ds((i % NCH) * CHUNK, CHUNK)
        return copy(src.at[part], dst.at[part], x_s.at[i], x_r.at[i], partner)

    def begun(c):
        c.start()
        sent.append(c.wait_send)

    def exchange(src, recv, ss, rs, size, me, dev):
        @pl.loop(1, size)
        def _(k):
            copy(src, recv.at[me], ss.at[k], rs.at[me], dev((me + k) % size)).start()

        @sent.append
        def _():
            @pl.loop(1, size)
            def _(k):
                copy(src, recv.at[me], ss.at[k], rs.at[me], dev((me + k) % size)).wait_send()

    def finish(src, recv, ss, rs, size, me, dev):
        recv[me] = src[...]

        @pl.loop(1, size)
        def _(k):
            s = (me + k) % size
            copy(src, recv.at[s], ss.at[k], rs.at[s], dev(s)).wait_recv()

    by_tensor = lambda s: (d, s)
    by_hz = lambda s: (s * 2 + core, t)

    def total(recv, size):
        acc = recv[0]
        for s in range(1, size):
            acc = acc + recv[s]
        return acc

    e0 = (e0s, e0r, e0_s, e0_r, TP, t, by_tensor)
    begun(xcopy(0))
    for c in sources:
        c.wait()
    nq = xq[...].astype(f32) * gain[...]
    nd = xd[...].astype(f32) * gain[...]
    lq = to_lanes(jnp.sum(nq * nq, axis=1, keepdims=True))
    ld = to_lanes(jnp.sum(nd * nd, axis=1, keepdims=True))
    e0s[...] = jnp.broadcast_to(gain[...], (8, FEATS))
    e0s[0:1, 0:ROWS] = lq[0:1]
    e0s[1:2, 0:ROWS] = ld[0:1]
    exchange(*e0)
    for i in range(1, 2 * NCH):
        begun(xcopy(i))

    mine = begin(d4, t)
    here = place(hz, core, t)
    extra = d4 == third

    def pack(a, k):
        own, part, base = (xq, pq, ROWS) if a == 0 else (xd, pd, 0)
        xcopy(a * NCH + k).wait_recv()
        rs = pl.ds(k * CHUNK, CHUNK)
        eo = own[rs].astype(f32)
        ep = part[rs].astype(f32)
        left = jnp.where(low == 0, eo, ep)
        right = jnp.where(low == 0, ep, eo)
        raw[pl.ds(base + k * CHUNK, CHUNK), lanes(y)] = jnp.concatenate(
            [left, right], axis=1
        ).astype(bf16)

    def normalise(a, k, block):
        inverse, base = (invq, ROWS) if a == 0 else (invd, 0)
        for part in range(2):
            rs = k * CHUNK + part * HALF
            scale = inverse[pl.ds(rs, HALF), 0:1]
            at = pl.ds(base + rs, HALF)
            cs = lanes(block)
            emb[at, cs] = (raw[at, cs].astype(f32) * gfull[:, cs] * scale).astype(bf16)

    def ycopy(a, k, kind):
        base = (ROWS if a == 0 else 0) + k * CHUNK
        i = (a * NCH + k) * 4 + kind
        if kind < 2:
            at, dev, block = pl.ds(base, CHUNK), (up, down)[kind], y
        elif kind == 2:
            at, dev, block = pl.ds(base, HALF), up, (y + 3) % 4
        else:
            at, dev, block = pl.ds(base + HALF, HALF), down, (y + 1) % 4
        ref = raw.at[at, lanes(block)]
        return copy(ref, ref, y_s.at[i], y_r.at[i], dev)

    def yrecv(a, k, kind):
        base = (ROWS if a == 0 else 0) + k * CHUNK
        i = (a * NCH + k) * 4 + kind
        at = pl.ds(base, CHUNK) if kind < 2 else pl.ds(base + (kind - 2) * HALF, HALF)
        block = ((y + 3) % 4, (y + 1) % 4, (y + 2) % 4, (y + 2) % 4)[kind]
        ref = raw.at[at, lanes(block)]
        copy(ref, ref, y_s.at[i], y_r.at[i], up).wait_recv()

    def source(s):
        return (xh + s // 4) % 2 * 4 + (zc + 4 - s % 4) % 4

    def gives(s, core_s):
        return (xh + s // 4) % 2 * 2 + core_s == third

    def device(s):
        return ((xh + s // 4) % 2 * 8 + (zc + s % 4) % 4 * 2 + core, t)

    def spot(i, s, core_s, n):
        block = (y + (0, 3, 1, 2)[i]) % 4
        return qi.at[rows_at(place(source(s), core_s, t), n), lanes(block)]

    def own_rows(i, n):
        block = (y + (0, 3, 1, 2)[i]) % 4
        return emb.at[pl.ds(pl.multiple_of(ROWS + mine * TILE, TILE), n), lanes(block)]

    def give_own(i, slot, dev):
        def c(n):
            return copy(
                own_rows(i, n), spot(i, 0, core, n), a_s.at[i * 16 + slot], a_r.at[i * 16 + slot], dev
            )

        sized(extra, lambda n: c(n).start())
        sent.append(lambda: sized(extra, lambda n: c(n).wait_send()))

    def pass_on(i, s, slot, dev):
        def c(n):
            ref = spot(i, s, core, n)
            return copy(ref, ref, a_s.at[i * 16 + slot], a_r.at[i * 16 + slot], dev)

        sized(gives(s, core), lambda n: c(n).start())
        sent.append(lambda: sized(gives(s, core), lambda n: c(n).wait_send()))

    def agot(i, s):
        def c(n):
            ref = spot(i, s, core, n)
            copy(ref, ref, a_s.at[i * 16 + s], a_r.at[i * 16 + s], sibling).wait_recv()

        sized(gives(s, core), c)

    def alocal(i, n):
        return pltpu.make_async_copy(own_rows(i, n), spot(i, 0, core, n), loc.at[i])

    def astart(i):
        for s in (1, 3, 2, 4) if i < 3 else (4, 1, 3, 2, 5, 7, 6):
            give_own(i, s, device(s))
        give_own(i, 8, sibling)
        sized(extra, lambda n: alocal(i, n).start())

    def amid(i):
        agot(i, 4)
        if i < 3:
            for s in (1, 3, 2):
                pass_on(i, 4, 4 + s, device(s))
        pass_on(i, 4, 12, sibling)
        for s in (1, 3, 2):
            agot(i, s)
            pass_on(i, s, 8 + s, sibling)

    def alast(i):
        for s in (5, 7, 6):
            agot(i, s)
            pass_on(i, s, 8 + s, sibling)

    def afinish(i):
        sized(extra, lambda n: alocal(i, n).wait())

        @pl.loop(0, 8)
        def _(s):
            def c(n):
                ref = spot(i, s, 1 - core, n)
                copy(ref, ref, a_s.at[i * 16], a_r.at[i * 16 + 8 + s], sibling).wait_recv()

            sized(gives(s, 1 - core), c)

    for k in range(NCH):
        pack(0, k)
        begun(ycopy(0, k, 0))
        begun(ycopy(0, k, 1))
    finish(*e0)
    inv = lax.rsqrt(total(e0r, TP)[:, 0:ROWS] + eps_len)
    invq[0:ROWS] = to_rows(inv[0:1])
    invd[...] = to_rows(inv[1:2])
    for b in range(4):
        gfull[:, b * WIDE : (b + 1) * WIDE] = jnp.concatenate(
            [e0r[b, 2:3], e0r[4 + b, 2:3]], axis=1
        )
    for k in range(NCH):
        normalise(0, k, y)
    astart(0)
    ep = (posv, epr, ep_s, ep_r, 8, hz, by_hz)
    exchange(*ep)
    for k in range(NCH):
        yrecv(0, k, 0)
        begun(ycopy(0, k, 2))
        yrecv(0, k, 1)
        begun(ycopy(0, k, 3))
    for k in range(NCH):
        pack(1, k)
        begun(ycopy(1, k, 0))
        begun(ycopy(1, k, 1))
    for k in range(NCH):
        normalise(0, k, (y + 3) % 4)
        normalise(0, k, (y + 1) % 4)
    astart(1)
    astart(2)
    amid(0)
    for k in range(NCH):
        yrecv(0, k, 2)
        yrecv(0, k, 3)
        normalise(0, k, (y + 2) % 4)
    astart(3)
    for k in range(NCH):
        normalise(1, k, y)
    alast(0)
    amid(1)
    amid(2)

    def docs_on(k):
        yrecv(1, k, 0)
        begun(ycopy(1, k, 2))
        yrecv(1, k, 1)
        begun(ycopy(1, k, 3))

    docs_on(0)
    alast(1)
    docs_on(1)
    alast(2)
    docs_on(2)
    for k in range(NCH):
        normalise(1, k, (y + 3) % 4)
        normalise(1, k, (y + 1) % 4)
    amid(3)
    alast(3)
    for i in range(4):
        afinish(i)

    lane_p = lax.broadcasted_iota(jnp.int32, (1, TAKE), 1)
    tile_p = lane_p // TILE
    w_p = tile_p % 9
    q_p = jnp.where(
        w_p < 2 * third, w_p // 2, jnp.where(w_p <= 2 * third + 2, third, (w_p - 1) // 2)
    )
    off_p = w_p - 2 * q_p - jnp.where(q_p > third, 1, 0)
    dev_p = (q_p // 2) * 8 + (tile_p // 9) * 2 + q_p % 2
    row_p = dev_p * ROWS + (begin(q_p, t) + off_p) * TILE + lane_p % TILE
    finish(*ep)
    epc = copy(epr.at[pl.ds(0, 8)], epr.at[pl.ds(8, 8)], c_s.at[0], c_r.at[0], sibling)
    begun(epc)

    stat[0:1] = jnp.full((1, TAKE), masked, f32)
    stat[1:8] = jnp.zeros((7, TAKE), f32)

    def product(rows, cs):
        return lax.dot_general(
            emb[rows, cs], qi[:, cs], (((1,), (1,)), ((), ())), preferred_element_type=f32
        )

    def statistics(s):
        old = stat[0:1]
        new = jnp.maximum(old, jnp.max(s, axis=0, keepdims=True))
        stat[0:1] = new
        stat[1:2] = stat[1:2] * jnp.exp(old - new) + jnp.sum(
            jnp.exp(s - new), axis=0, keepdims=True
        )

    own_j = d * ROWS + lax.broadcasted_iota(jnp.int32, (ROWS, TAKE), 0)
    logits[ROWS:] = product(pl.ds(ROWS, ROWS), slice(None))
    logits[ROWS:] = jnp.where(own_j == row_p, masked, logits[ROWS:] * inv_temp)
    statistics(logits[ROWS:])
    logits[0:ROWS] = product(pl.ds(0, ROWS), lanes(y))
    for b in (1, 3):
        logits[0:ROWS] = logits[0:ROWS] + product(pl.ds(0, ROWS), lanes((y + b) % 4))

    epc.wait_recv()
    local_p = (begin(q_p, t) + off_p) * TILE + lane_p % TILE
    lane_of = lax.broadcasted_iota(jnp.int32, (128, TAKE), 0)
    spread = jnp.where(lane_of == local_p % 128, 1.0, 0.0).astype(bf16)
    found = jnp.dot(
        epr[...].reshape(DP * 8, 128).astype(bf16), spread, preferred_element_type=f32
    )
    slot_p = jnp.where(dev_p % 2 == core, dev_p // 2, 8 + dev_p // 2) * 8 + local_p // 128
    high = jnp.sum(jnp.where(lane_of == slot_p, found, 0.0), axis=0, keepdims=True)
    rest = jnp.sum(jnp.where(lane_of == slot_p + 3, found, 0.0), axis=0, keepdims=True)
    pos_p = (high * 128.0 + rest).astype(jnp.int32)

    for k in range(NCH):
        yrecv(1, k, 2)
        yrecv(1, k, 3)
        normalise(1, k, (y + 2) % 4)
    logits[0:ROWS] = (logits[0:ROWS] + product(pl.ds(0, ROWS), lanes((y + 2) % 4))) * inv_temp
    stat[2:3] = jnp.sum(jnp.where(own_j == pos_p, logits[0:ROWS], 0.0), axis=0, keepdims=True)
    statistics(logits[0:ROWS])

    sub_t = sub8(TAKE)
    cs1[...] = jnp.zeros_like(cs1)
    for i in range(3):
        fold(cs1, 5 * i, stat[i : i + 1])
    c1 = copy(cs1, cr1, c_s.at[1], c_r.at[1], sibling)
    begun(c1)
    c1.wait_recv()
    top, top_o = cs1[0:5], cr1[0:5]
    top_c = jnp.maximum(top, top_o)
    e1s[0:5] = top_c
    e1s[5:10] = cs1[5:10] * jnp.exp(top - top_c) + cr1[5:10] * jnp.exp(top_o - top_c)
    e1s[10:15] = cs1[10:15] + cr1[10:15]
    e1s[15:16] = jnp.zeros((1, 128), f32)
    e1 = (e1s, e1r, e1_s, e1_r, 8, hz, by_hz)
    exchange(*e1)
    pick[...] = jnp.where(own_j == row_p, 1.0, 0.0).astype(bf16)
    finish(*e1)
    all_top = e1r[0, 0:5]
    for s in range(1, 8):
        all_top = jnp.maximum(all_top, e1r[s, 0:5])
    all_tot = jnp.zeros_like(all_top)
    all_pos = jnp.zeros_like(all_top)
    for s in range(8):
        all_tot = all_tot + e1r[s, 5:10] * jnp.exp(e1r[s, 0:5] - all_top)
        all_pos = all_pos + e1r[s, 10:15]
    lse = unfold(all_top, 0, TAKE) + jnp.log(unfold(all_tot, 0, TAKE))
    loss_part = jnp.sum(lse - unfold(all_pos, 0, TAKE), axis=1, keepdims=True)
    sub_t = sub8(TAKE)

    def own_lanes(vec):
        p1 = vec.astype(bf16).astype(f32)
        p2 = (vec - p1).astype(bf16).astype(f32)
        split = jnp.where(
            sub_t == 0, p1, jnp.where(sub_t == 1, p2, jnp.where(sub_t == 2, vec - p1 - p2, 0.0))
        )
        return jnp.sum(
            lax.dot_general(
                split.astype(bf16), pick[...], (((1,), (1,)), ((), ())),
                preferred_element_type=f32,
            ),
            axis=0, keepdims=True,
        )

    lse_own = own_lanes(lse)
    e2s[...] = jnp.broadcast_to(loss_part, (8, 128))
    fold(e2s, 0, lse_own)
    e2 = (e2s, e2r, e2_s, e2_r, TP, t, by_tensor)
    exchange(*e2)
    wd = (jnp.exp(logits[0:ROWS] - lse) - (own_j == pos_p).astype(f32)) * (1.0 / PAIRS)
    wts[0:ROWS] = wd.astype(bf16)

    def part_d(block):
        return lax.dot_general(
            wts[0:ROWS], qi[:, lanes(block)], (((1,), (0,)), ((), ())),
            preferred_element_type=f32,
        ) * inv_temp

    MID = ROWS // 2
    front, rear = pl.ds(0, MID), pl.ds(MID, MID)
    gc = [
        copy(pd2.at[front], halfs.at[0], g_s.at[0], g_r.at[0], up),
        copy(pd2.at[rear], halfs.at[1], g_s.at[1], g_r.at[1], down),
        copy(pd1.at[rear], r1.at[rear], g_s.at[2], g_r.at[2], up),
        copy(pdm.at[front], r2.at[front], g_s.at[3], g_r.at[3], down),
        copy(pd1.at[front], r1.at[front], g_s.at[4], g_r.at[4], up),
        copy(pdm.at[rear], r2.at[rear], g_s.at[5], g_r.at[5], down),
        copy(xsend, xrecv, g_s.at[6], g_r.at[6], partner),
    ]
    pd2[...] = part_d((y + 2) % 4).astype(bf16)
    begun(gc[0])
    begun(gc[1])
    gd[...] = part_d((y + 1) % 4)
    pd1[rear] = gd[rear].astype(bf16)
    begun(gc[2])
    acc1[...] = gd[front]
    gd[...] = part_d((y + 3) % 4)
    pdm[front] = gd[front].astype(bf16)
    begun(gc[3])
    acc2[...] = gd[rear]

    finish(*e2)
    sums = total(e2r, TP)
    oloss[...] = sums[3:4, 0:1] * (1.0 / PAIRS)
    lse_j = to_rows(unfold(sums, 0, ROWS))[:, 0:1]
    wq = (jnp.exp(logits[ROWS:] - lse) * (1.0 / PAIRS)).astype(bf16).astype(f32)
    wt = (jnp.exp(logits[ROWS:] - lse_j) * (1.0 / PAIRS)).astype(bf16).astype(f32)
    wts[ROWS:] = (wq + wt).astype(bf16)
    wtt[...] = jnp.transpose(wts[...])

    def target(s):
        return (xh + s // 4) % 2 * 4 + (zc + s % 4) % 4

    def cols(f):
        return lanes((y + 1 + f) % 4)

    def bcopy(f, k, n):
        at = rows_at(place(k, 1 - core, t), n)
        return copy(
            partq.at[at, cols(f)], sibr.at[k, pl.ds(0, n), cols(f)],
            b_s.at[f * 8 + k], b_r.at[f * 8 + k], sibling,
        )

    def three(k, core_s):
        return (k // 4) * 2 + core_s == third

    def part_q(f):
        partq[0:TAKE, cols(f)] = (
            jnp.dot(
                wtt[...], emb[0 : 2 * ROWS, cols(f)],
                preferred_element_type=f32,
            ) * inv_temp
        ).astype(bf16)

        @pl.loop(0, 8)
        def _(k):
            sized(three(k, 1 - core), lambda n: bcopy(f, k, n).start())

        @sent.append
        def _():
            @pl.loop(0, 8)
            def _(k):
                sized(three(k, 1 - core), lambda n: bcopy(f, k, n).wait_send())

    N3 = 3 * TILE

    def both(f, s):
        k = target(s)
        sized(three(k, core), lambda n: bcopy(f, k, n).wait_recv())
        cs = cols(f)
        return partq[rows_at(place(k, core, t), N3), cs].astype(f32) + sibr[k, :, cs].astype(f32)

    FLOW = ((2, zup), (6, zdown), (5, zup), (3, zdown), (1, zup), (7, zdown), (4, across))

    def ucopy(f, i, n):
        cs = cols(f)
        return copy(
            sendq.at[i, pl.ds(0, n), cs], recvq.at[i, pl.ds(0, n), cs],
            u_s.at[f * 8 + i], u_r.at[f * 8 + i], FLOW[i][1],
        )

    def usend(f, i, value):
        sendq[i, :, cols(f)] = value.astype(bf16)
        far = three(target(FLOW[i][0]), core)
        sized(far, lambda n: ucopy(f, i, n).start())
        sent.append(lambda: sized(far, lambda n: ucopy(f, i, n).wait_send()))

    def uwait(f, i, s):
        sized(three(target(s), core), lambda n: ucopy(f, i, n).wait_recv())
        return recvq[i, :, cols(f)].astype(f32)

    def q_far(f):
        usend(f, 0, both(f, 2))
        usend(f, 1, both(f, 6))
        usend(f, 2, both(f, 5))
        usend(f, 3, both(f, 3))

    def q_near(f):
        usend(f, 4, both(f, 1) + uwait(f, 0, 1))
        usend(f, 5, both(f, 7) + uwait(f, 1, 7))

    def q_across(f):
        usend(f, 6, both(f, 4) + uwait(f, 2, 4) + uwait(f, 5, 4))

    def tcopy(f, far, n):
        to = (y + 1 + f) % 4 + 4 * ((low + far) % 2)
        return copy(
            asend.at[to, pl.ds(0, n)], arecv.at[rows_at(mine, n)],
            t_s.at[f * 2 + far], t_r.at[f * 2 + far], (d, to),
        )

    def trecv(f, far):
        s = (y + 3 - f) % 4 + 4 * ((low + far) % 2)
        at = lambda n: arecv.at[rows_at(begin(d4, s), n)]
        sized(
            d4 == s // 2,
            lambda n: copy(at(n), at(n), t_s.at[0], t_r.at[f * 2 + far], (d, s)).wait_recv(),
        )

    def direct(f, s, n):
        cs = cols(f)
        return copy(
            sendq.at[s - 1, pl.ds(0, n), cs], recvq.at[s - 1, pl.ds(0, n), cs],
            u_s.at[f * 8 + s - 1], u_r.at[f * 8 + s - 1], device(s),
        )

    def q_direct(f):
        for s in (5, 7, 6, 4, 2, 1, 3):
            sendq[s - 1, :, cols(f)] = both(f, s).astype(bf16)
            far = three(target(s), core)
            sized(far, lambda n: direct(f, s, n).start())
            sent.append(
                lambda s=s, far=far: sized(far, lambda n: direct(f, s, n).wait_send())
            )

    def q_own(f):
        if f < 3:
            g = both(f, 0) + uwait(f, 3, 0) + uwait(f, 4, 0) + uwait(f, 6, 0)
        else:
            g = both(f, 0)
            for s in range(1, 8):
                sized(extra, lambda n: direct(f, s, n).wait_recv())
                g = g + recvq[s - 1, :, cols(f)].astype(f32)
        fb = (y + 1 + f) % 4
        asend[fb] = g[:, :FEATS].astype(bf16)
        asend[4 + fb] = g[:, FEATS:].astype(bf16)
        for far in range(2):
            if f < 3 or far == 1:
                sized(extra, lambda n: tcopy(f, far, n).start())
                sent.append(
                    lambda far=far: sized(extra, lambda n: tcopy(f, far, n).wait_send())
                )

    part_q(0)
    part_q(1)
    q_far(0)

    weighed = wts[...].astype(f32) * logits[...]
    cs5[...] = jnp.zeros_like(cs5)
    fold(cs5, 0, jnp.sum(weighed, axis=0, keepdims=True))
    c5 = copy(cs5, cr5, c_s.at[3], c_r.at[3], sibling)
    begun(c5)
    e3s[...] = jnp.zeros_like(e3s)
    fold(e3s, 3, to_lanes(jnp.sum(weighed[0:ROWS], axis=1, keepdims=True))[0:1])
    part_q(2)
    q_far(1)
    c5.wait_recv()
    e5s[...] = cs5[...] + cr5[...]
    e5 = (e5s, e5r, e5_s, e5_r, 8, hz, by_hz)
    exchange(*e5)
    gc[0].wait_recv()
    pd1[front] = (acc1[...] + halfs[0].astype(f32)).astype(bf16)
    begun(gc[4])
    gc[1].wait_recv()
    pdm[rear] = (acc2[...] + halfs[1].astype(f32)).astype(bf16)
    begun(gc[5])
    q_far(2)
    part_q(3)
    q_near(0)
    q_near(1)
    q_near(2)
    q_direct(3)
    gd[...] = part_d(y)
    finish(*e5)
    fold(e3s, 0, own_lanes(unfold(total(e5r, 8), 0, TAKE)))
    e3 = (e3s, e3r, e3_s, e3_r, TP, t, by_tensor)
    exchange(*e3)
    q_across(0)
    for i in range(2, 6):
        gc[i].wait_recv()
    gd[...] = gd[...] + r1[...].astype(f32) + r2[...].astype(f32)
    xsend[...] = jnp.where(low == 0, gd[:, FEATS:], gd[:, :FEATS]).astype(bf16)
    begun(gc[6])
    q_across(1)
    q_own(0)
    q_across(2)
    q_own(1)

    gc[6].wait_recv()
    gd[:, 0:FEATS] = jnp.where(low == 0, gd[:, :FEATS], gd[:, FEATS:]) + xrecv[...].astype(f32)
    q_own(2)
    q_own(3)

    def tlocal(n):
        arecv[rows_at(mine, n)] = asend[t, pl.ds(0, n)]

    sized(extra, tlocal)

    finish(*e3)
    dots = total(e3r, TP)
    col = to_rows(unfold(dots, 3, ROWS))[:, 0:1]
    iv = invd[:, 0:1]
    h = xd[...].astype(f32)
    gx = iv * gd[:, 0:FEATS] - h * gain[...] * (iv * iv * col)
    outd[...] = (gx * gain[...]).astype(bf16)
    outs = [pltpu.make_async_copy(outd, od, io.at[0]), pltpu.make_async_copy(outq, oq, io.at[1])]
    outs[0].start()
    gg = jnp.sum(gx * h, axis=0, keepdims=True)

    for f in range(4):
        for far in range(2):
            if f < 3 or far == 1:
                trecv(f, far)

    col = to_rows(unfold(dots, 0, ROWS))[:, 0:1]
    h = xq[...].astype(f32)
    iv = invq[0:ROWS, 0:1]
    gx = iv * arecv[...].astype(f32) - h * gain[...] * (iv * iv * col)
    gg = gg + jnp.sum(gx * h, axis=0, keepdims=True)
    cs4[...] = jnp.zeros_like(cs4)
    fold(cs4, 0, gg)
    c4 = copy(cs4, cr4, c_s.at[2], c_r.at[2], sibling)
    begun(c4)
    outq[...] = (gx * gain[...]).astype(bf16)
    outs[1].start()
    c4.wait_recv()
    e4s[...] = cs4[...] + cr4[...]
    e4 = (e4s, e4r, e4_s, e4_r, 8, hz, by_hz)
    exchange(*e4)
    finish(*e4)
    ogain[...] = unfold(total(e4r, 8), 0, FEATS)
    for c in outs:
        c.wait()

    for wait in sent:
        wait()


def results(gq, gdoc, ggain, loss, oq, od, ogain, oloss):
    oq[...] = gq[...]
    od[...] = gdoc[...]
    ogain[...] = ggain[...]
    oloss[...] = loss[...]


def shards(query_states, doc_states, gain, positives):
    vm = pl.BlockSpec(memory_space=pltpu.VMEM)
    hbm = pl.BlockSpec(memory_space=pl.ANY)
    S = pltpu.VMEM
    dma = lambda n: pltpu.SemaphoreType.DMA((n,))
    pair = lambda n: [dma(n), dma(n)]
    scratch = [
        S((ROWS, FEATS), bf16), S((ROWS, FEATS), bf16),
        S((ROWS, FEATS), bf16), S((ROWS, FEATS), bf16), S((1, FULL), f32),
        S((2 * ROWS, FULL), bf16), S((2 * ROWS + TILE, FULL), bf16), S((TAKE, FULL), bf16),
        S((ROWS + TILE, 128), f32), S((ROWS, 128), f32),
        S((2 * ROWS, TAKE), f32), S((8, TAKE), f32), S((2 * ROWS, TAKE), bf16), S((TAKE, 2 * ROWS), bf16),
        S((8, FEATS), f32), S((TP, 8, FEATS), f32),
        S((16, 128), f32), S((16, 128), f32), S((16, 128), f32), S((8, 16, 128), f32),
        S((8, 128), f32), S((TP, 8, 128), f32),
        S((8, 128), f32), S((TP, 8, 128), f32),
        S((8, 128), f32), S((8, 128), f32), S((8, 128), f32), S((8, 8, 128), f32),
        S((DP, 8, 128), f32), S((8, 128), f32),
        S((TAKE + TILE, FULL), bf16), S((8, 3 * TILE, FULL), bf16),
        S((7, 3 * TILE, FULL), bf16), S((7, 3 * TILE, FULL), bf16),
        S((ROWS // 2, WIDE), f32), S((ROWS // 2, WIDE), f32),
        S((ROWS, WIDE), bf16), S((ROWS, WIDE), bf16), S((ROWS, WIDE), bf16),
        S((2, ROWS // 2, WIDE), bf16), S((ROWS, WIDE), bf16), S((ROWS, WIDE), bf16),
        S((ROWS, WIDE), f32), S((ROWS, FEATS), bf16), S((ROWS, FEATS), bf16),
        S((TP, 3 * TILE, FEATS), bf16), S((ROWS, FEATS), bf16), S((ROWS, TAKE), bf16),
        S((8, 128), f32), S((8, 128), f32), S((8, 128), f32), S((8, 8, 128), f32),
        S((ROWS, FEATS), bf16), S((ROWS, FEATS), bf16),
    ]
    sems = (
        pair(2 * NCH) + pair(TP) + pair(8) + pair(TP) + pair(TP) + pair(8) + pair(8)
        + pair(8 * NCH) + pair(64) + [dma(4)] + pair(32) + pair(32) + pair(7) + pair(TP) + pair(8)
        + pair(4) + [dma(2)]
    )
    gq, gdoc, ggain, loss = pl.pallas_call(
        step,
        name="infonce_step",
        out_shape=(
            jax.ShapeDtypeStruct((ROWS, FEATS), bf16),
            jax.ShapeDtypeStruct((ROWS, FEATS), bf16),
            jax.ShapeDtypeStruct((1, FEATS), f32),
            jax.ShapeDtypeStruct((1, 1), f32),
        ),
        in_specs=[hbm, hbm, vm, vm],
        out_specs=(hbm, hbm, vm, vm),
        scratch_shapes=scratch + sems,
        compiler_params=pltpu.CompilerParams(
            collective_id=0, has_side_effects=True, vmem_limit_bytes=56 * 2**20
        ),
        cost_estimate=pl.CostEstimate(
            flops=7_000_000_000, bytes_accessed=3_000_000, transcendentals=1_000_000
        ),
    )(query_states, doc_states, gain[None, :], positives)
    gq, gdoc, ggain, loss = pl.pallas_call(
        results,
        name="results",
        out_shape=(
            jax.ShapeDtypeStruct((ROWS, FEATS), bf16),
            jax.ShapeDtypeStruct((ROWS, FEATS), bf16),
            jax.ShapeDtypeStruct((1, FEATS), f32),
            jax.ShapeDtypeStruct((1, 1), f32),
        ),
        in_specs=[vm] * 4,
        out_specs=(vm,) * 4,
    )(gq, gdoc, ggain, loss)
    return gq, gdoc, ggain[0], loss[0, 0]


def solution(mesh):
    return jax.shard_map(
        shards,
        mesh=mesh,
        in_specs=(P("dp", "tensor"), P("dp", "tensor"), P("tensor"), P("dp")),
        out_specs=(P("dp", "tensor"), P("dp", "tensor"), P("tensor"), P()),
        check_vma=False,
    )
```

```python
import functools

import jax
import jax.numpy as jnp
from jax import lax
from jax.experimental import pallas as pl
from jax.experimental.pallas import tpu as pltpu
from jax.sharding import PartitionSpec as P

eps_len = 1e-06
inv_temp = 100.0
masked = -1e30

MESH = pl.DeviceIdType.MESH
HIGH = lax.Precision.HIGHEST
f32 = jnp.float32
bf16 = jnp.bfloat16

DP = 16
TP = 8
ROWS = 288
FEATS = 448
WIDE = 2 * FEATS
FULL = TP * FEATS
PAIRS = DP * ROWS
TAKE = DP * ROWS // TP
TILE = 16
CHUNK = 96
NCH = ROWS // CHUNK
HALF = CHUNK // 2


def step(
    hq, hd, gain, pos,
    oq, od, ogain, oloss,
    xq, xd, pq, pd, gfull, raw, emb, qi, invq, invd, logits, stat, wts, wtt,
    e0s, e0r, cs1, cr1, e1s, e1r, e2s, e2r, e3s, e3r, cs4, cr4, e4s, e4r, epr, posv,
    partq, sibr, sendq, recvq, acc1, acc2, pd2, pd1, pdm, halfs, r1, r2, gd, xsend, xrecv,
    asend, arecv, pick, cs5, cr5, e5s, e5r, outq, outd,
    x_s, x_r, e0_s, e0_r, e1_s, e1_r, e2_s, e2_r, e3_s, e3_r, e4_s, e4_r, ep_s, ep_r,
    y_s, y_r, a_s, a_r, loc, b_s, b_r, u_s, u_r, g_s, g_r, t_s, t_r, e5_s, e5_r, c_s, c_r, io,
):
    d = lax.axis_index("dp")
    t = lax.axis_index("tensor")
    hz = d // 2
    core = d % 2
    zc = hz % 4
    d4 = (hz // 4) * 2 + core
    low = t // 4
    y = t % 4
    xh = hz // 4
    sources = [pltpu.make_async_copy(hq, xq, io.at[0]), pltpu.make_async_copy(hd, xd, io.at[1])]
    for c in sources:
        c.start()
    third = t // 2
    sibling = (hz * 2 + (1 - core), t)
    partner = (d, (t + 4) % TP)
    up = (d, low * 4 + (y + 1) % 4)
    down = (d, low * 4 + (y + 3) % 4)
    zup = ((xh * 4 + (zc + 1) % 4) * 2 + core, t)
    zdown = ((xh * 4 + (zc + 3) % 4) * 2 + core, t)
    across = ((hz + 4) % 8 * 2 + core, t)

    sent = []

    def drain(count):
        for _ in range(min(count, len(sent))):
            sent.pop(0)()

    def copy(src, dst, ss, rs, dev):
        return pltpu.make_async_remote_copy(
            src_ref=src, dst_ref=dst, send_sem=ss, recv_sem=rs, device_id=dev, device_id_type=MESH
        )

    def lanes(block):
        return pl.ds(pl.multiple_of(block * WIDE, 128), WIDE)

    def rows_at(tile, n):
        return pl.ds(pl.multiple_of(tile * TILE, TILE), n)

    def place(hz_s, core_s, tens):
        q = (hz_s // 4) * 2 + core_s
        e = tens // 2
        return (hz_s % 4) * 9 + 2 * q + jnp.where(q > e, 1, 0)

    def begin(q, tens):
        return 2 * tens + jnp.clip(tens - 2 * q, 0, 2)

    def sized(extra, fn):
        @pl.when(extra)
        def _():
            fn(3 * TILE)

        @pl.when(jnp.logical_not(extra))
        def _():
            fn(2 * TILE)

    barrier = pltpu.get_barrier_semaphore()

    @pl.loop(1, TP)
    def _(k):
        pl.semaphore_signal(barrier, inc=1, device_id=(d, (t + k) % TP), device_id_type=MESH)

    @pl.loop(1, 8)
    def _(k):
        pl.semaphore_signal(
            barrier, inc=1, device_id=((hz + k) % 8 * 2 + core, t), device_id_type=MESH
        )

    pl.semaphore_signal(barrier, inc=1, device_id=sibling, device_id_type=MESH)
    def fold(ref, row, vec):
        for k in range(-(-vec.shape[1] // 128)):
            part = vec[:, 128 * k : 128 * (k + 1)]
            ref[row + k : row + k + 1, 0 : part.shape[1]] = part

    def unfold(tile, row, size):
        return jnp.concatenate(
            [
                tile[row + k : row + k + 1, 0 : min(128, size - 128 * k)]
                for k in range(-(-size // 128))
            ],
            axis=1,
        )

    def to_lanes(col):
        return jnp.transpose(jnp.broadcast_to(col, (ROWS, 128)))[:8]

    def to_rows(vec):
        return jnp.transpose(jnp.broadcast_to(vec, (128, ROWS)))

    sub8 = lambda n: lax.broadcasted_iota(jnp.int32, (8, n), 0)

    posv[...] = jnp.zeros_like(posv)
    for seg in range(3):
        at = slice(128 * seg, min(128 * (seg + 1), ROWS))
        width = at.stop - at.start
        posv[seg : seg + 1, 0:width] = (pos[at] // 128).astype(f32)[None, :]
        posv[3 + seg : 4 + seg, 0:width] = (pos[at] % 128).astype(f32)[None, :]
    pl.semaphore_wait(barrier, TP + 7)

    def xcopy(i):
        src, dst = (hq, pq) if i < NCH else (hd, pd)
        part = pl.ds((i % NCH) * CHUNK, CHUNK)
        return copy(src.at[part], dst.at[part], x_s.at[i], x_r.at[i], partner)

    def begun(c):
        c.start()
        sent.append(c.wait_send)

    def exchange(src, recv, ss, rs, size, me, dev):
        @pl.loop(1, size)
        def _(k):
            copy(src, recv.at[me], ss.at[k], rs.at[me], dev((me + k) % size)).start()

        @sent.append
        def _():
            @pl.loop(1, size)
            def _(k):
                copy(src, recv.at[me], ss.at[k], rs.at[me], dev((me + k) % size)).wait_send()

    def finish(src, recv, ss, rs, size, me, dev):
        recv[me] = src[...]

        @pl.loop(1, size)
        def _(k):
            s = (me + k) % size
            copy(src, recv.at[s], ss.at[k], rs.at[s], dev(s)).wait_recv()

    by_tensor = lambda s: (d, s)
    by_hz = lambda s: (s * 2 + core, t)

    def total(recv, size):
        acc = recv[0]
        for s in range(1, size):
            acc = acc + recv[s]
        return acc

    e0 = (e0s, e0r, e0_s, e0_r, TP, t, by_tensor)
    begun(xcopy(0))
    for c in sources:
        c.wait()
    nq = xq[...].astype(f32) * gain[...]
    nd = xd[...].astype(f32) * gain[...]
    lq = to_lanes(jnp.sum(nq * nq, axis=1, keepdims=True))
    ld = to_lanes(jnp.sum(nd * nd, axis=1, keepdims=True))
    e0s[...] = jnp.broadcast_to(gain[...], (8, FEATS))
    e0s[0:1, 0:ROWS] = lq[0:1]
    e0s[1:2, 0:ROWS] = ld[0:1]
    exchange(*e0)
    for i in range(1, 2 * NCH):
        begun(xcopy(i))

    mine = begin(d4, t)
    here = place(hz, core, t)
    extra = d4 == third

    def pack(a, k):
        own, part, base = (xq, pq, ROWS) if a == 0 else (xd, pd, 0)
        xcopy(a * NCH + k).wait_recv()
        rs = pl.ds(k * CHUNK, CHUNK)
        eo = own[rs].astype(f32)
        ep = part[rs].astype(f32)
        left = jnp.where(low == 0, eo, ep)
        right = jnp.where(low == 0, ep, eo)
        raw[pl.ds(base + k * CHUNK, CHUNK), lanes(y)] = jnp.concatenate(
            [left, right], axis=1
        ).astype(bf16)

    def normalise(a, k, block):
        inverse, base = (invq, ROWS) if a == 0 else (invd, 0)
        for part in range(2):
            rs = k * CHUNK + part * HALF
            scale = inverse[pl.ds(rs, HALF), 0:1]
            at = pl.ds(base + rs, HALF)
            cs = lanes(block)
            emb[at, cs] = (raw[at, cs].astype(f32) * gfull[:, cs] * scale).astype(bf16)

    def ycopy(a, k, kind):
        base = (ROWS if a == 0 else 0) + k * CHUNK
        i = (a * NCH + k) * 4 + kind
        if kind < 2:
            at, dev, block = pl.ds(base, CHUNK), (up, down)[kind], y
        elif kind == 2:
            at, dev, block = pl.ds(base, HALF), up, (y + 3) % 4
        else:
            at, dev, block = pl.ds(base + HALF, HALF), down, (y + 1) % 4
        ref = raw.at[at, lanes(block)]
        return copy(ref, ref, y_s.at[i], y_r.at[i], dev)

    def yrecv(a, k, kind):
        base = (ROWS if a == 0 else 0) + k * CHUNK
        i = (a * NCH + k) * 4 + kind
        at = pl.ds(base, CHUNK) if kind < 2 else pl.ds(base + (kind - 2) * HALF, HALF)
        block = ((y + 3) % 4, (y + 1) % 4, (y + 2) % 4, (y + 2) % 4)[kind]
        ref = raw.at[at, lanes(block)]
        copy(ref, ref, y_s.at[i], y_r.at[i], up).wait_recv()

    def source(s):
        return (xh + s // 4) % 2 * 4 + (zc + 4 - s % 4) % 4

    def gives(s, core_s):
        return (xh + s // 4) % 2 * 2 + core_s == third

    def device(s):
        return ((xh + s // 4) % 2 * 8 + (zc + s % 4) % 4 * 2 + core, t)

    def spot(i, s, core_s, n):
        block = (y + (0, 3, 1, 2)[i]) % 4
        return qi.at[rows_at(place(source(s), core_s, t), n), lanes(block)]

    def own_rows(i, n):
        block = (y + (0, 3, 1, 2)[i]) % 4
        return emb.at[pl.ds(pl.multiple_of(ROWS + mine * TILE, TILE), n), lanes(block)]

    def give_own(i, slot, dev):
        def c(n):
            return copy(
                own_rows(i, n), spot(i, 0, core, n), a_s.at[i * 16 + slot], a_r.at[i * 16 + slot], dev
            )

        sized(extra, lambda n: c(n).start())
        sent.append(lambda: sized(extra, lambda n: c(n).wait_send()))

    def pass_on(i, s, slot, dev):
        def c(n):
            ref = spot(i, s, core, n)
            return copy(ref, ref, a_s.at[i * 16 + slot], a_r.at[i * 16 + slot], dev)

        sized(gives(s, core), lambda n: c(n).start())
        sent.append(lambda: sized(gives(s, core), lambda n: c(n).wait_send()))

    def agot(i, s):
        def c(n):
            ref = spot(i, s, core, n)
            copy(ref, ref, a_s.at[i * 16 + s], a_r.at[i * 16 + s], sibling).wait_recv()

        sized(gives(s, core), c)

    def alocal(i, n):
        return pltpu.make_async_copy(own_rows(i, n), spot(i, 0, core, n), loc.at[i])

    def astart(i):
        for s in (1, 3, 2, 4) if i < 3 else (4, 1, 3, 2, 5, 7, 6):
            give_own(i, s, device(s))
        give_own(i, 8, sibling)
        sized(extra, lambda n: alocal(i, n).start())

    def amid(i):
        agot(i, 4)
        if i < 3:
            for s in (1, 3, 2):
                pass_on(i, 4, 4 + s, device(s))
        pass_on(i, 4, 12, sibling)
        for s in (1, 3, 2):
            agot(i, s)
            pass_on(i, s, 8 + s, sibling)

    def alast(i):
        for s in (5, 7, 6):
            agot(i, s)
            pass_on(i, s, 8 + s, sibling)

    def afinish(i):
        sized(extra, lambda n: alocal(i, n).wait())

        @pl.loop(0, 8)
        def _(s):
            def c(n):
                ref = spot(i, s, 1 - core, n)
                copy(ref, ref, a_s.at[i * 16], a_r.at[i * 16 + 8 + s], sibling).wait_recv()

            sized(gives(s, 1 - core), c)

    for k in range(NCH):
        pack(0, k)
        begun(ycopy(0, k, 0))
        begun(ycopy(0, k, 1))
    finish(*e0)
    inv = lax.rsqrt(total(e0r, TP)[:, 0:ROWS] + eps_len)
    invq[0:ROWS] = to_rows(inv[0:1])
    invd[...] = to_rows(inv[1:2])
    for b in range(4):
        gfull[:, b * WIDE : (b + 1) * WIDE] = jnp.concatenate(
            [e0r[b, 2:3], e0r[4 + b, 2:3]], axis=1
        )
    for k in range(NCH):
        normalise(0, k, y)
    astart(0)
    ep = (posv, epr, ep_s, ep_r, 8, hz, by_hz)
    exchange(*ep)
    for k in range(NCH):
        yrecv(0, k, 0)
        begun(ycopy(0, k, 2))
        yrecv(0, k, 1)
        begun(ycopy(0, k, 3))
    for k in range(NCH):
        pack(1, k)
        begun(ycopy(1, k, 0))
        begun(ycopy(1, k, 1))
    for k in range(NCH):
        normalise(0, k, (y + 3) % 4)
        normalise(0, k, (y + 1) % 4)
    astart(1)
    astart(2)
    amid(0)
    for k in range(NCH):
        yrecv(0, k, 2)
        yrecv(0, k, 3)
        normalise(0, k, (y + 2) % 4)
    astart(3)
    for k in range(NCH):
        normalise(1, k, y)
    alast(0)
    amid(1)
    amid(2)

    def docs_on(k):
        yrecv(1, k, 0)
        begun(ycopy(1, k, 2))
        yrecv(1, k, 1)
        begun(ycopy(1, k, 3))

    docs_on(0)
    alast(1)
    docs_on(1)
    alast(2)
    docs_on(2)
    for k in range(NCH):
        normalise(1, k, (y + 3) % 4)
        normalise(1, k, (y + 1) % 4)
    amid(3)
    alast(3)
    for i in range(4):
        afinish(i)

    lane_p = lax.broadcasted_iota(jnp.int32, (1, TAKE), 1)
    tile_p = lane_p // TILE
    w_p = tile_p % 9
    q_p = jnp.where(
        w_p < 2 * third, w_p // 2, jnp.where(w_p <= 2 * third + 2, third, (w_p - 1) // 2)
    )
    off_p = w_p - 2 * q_p - jnp.where(q_p > third, 1, 0)
    dev_p = (q_p // 2) * 8 + (tile_p // 9) * 2 + q_p % 2
    row_p = dev_p * ROWS + (begin(q_p, t) + off_p) * TILE + lane_p % TILE
    finish(*ep)
    epc = copy(epr.at[pl.ds(0, 8)], epr.at[pl.ds(8, 8)], c_s.at[0], c_r.at[0], sibling)
    begun(epc)

    stat[0:1] = jnp.full((1, TAKE), masked, f32)
    stat[1:8] = jnp.zeros((7, TAKE), f32)

    def product(rows, cs):
        return lax.dot_general(
            emb[rows, cs], qi[:, cs], (((1,), (1,)), ((), ())), preferred_element_type=f32
        )

    def statistics(s):
        old = stat[0:1]
        new = jnp.maximum(old, jnp.max(s, axis=0, keepdims=True))
        stat[0:1] = new
        stat[1:2] = stat[1:2] * jnp.exp(old - new) + jnp.sum(
            jnp.exp(s - new), axis=0, keepdims=True
        )

    own_j = d * ROWS + lax.broadcasted_iota(jnp.int32, (ROWS, TAKE), 0)
    logits[ROWS:] = product(pl.ds(ROWS, ROWS), slice(None))
    logits[ROWS:] = jnp.where(own_j == row_p, masked, logits[ROWS:] * inv_temp)
    statistics(logits[ROWS:])
    logits[0:ROWS] = product(pl.ds(0, ROWS), lanes(y))
    for b in (1, 3):
        logits[0:ROWS] = logits[0:ROWS] + product(pl.ds(0, ROWS), lanes((y + b) % 4))

    epc.wait_recv()
    local_p = (begin(q_p, t) + off_p) * TILE + lane_p % TILE
    lane_of = lax.broadcasted_iota(jnp.int32, (128, TAKE), 0)
    spread = jnp.where(lane_of == local_p % 128, 1.0, 0.0).astype(bf16)
    found = jnp.dot(
        epr[...].reshape(DP * 8, 128).astype(bf16), spread, preferred_element_type=f32
    )
    slot_p = jnp.where(dev_p % 2 == core, dev_p // 2, 8 + dev_p // 2) * 8 + local_p // 128
    high = jnp.sum(jnp.where(lane_of == slot_p, found, 0.0), axis=0, keepdims=True)
    rest = jnp.sum(jnp.where(lane_of == slot_p + 3, found, 0.0), axis=0, keepdims=True)
    pos_p = (high * 128.0 + rest).astype(jnp.int32)

    for k in range(NCH):
        yrecv(1, k, 2)
        yrecv(1, k, 3)
        normalise(1, k, (y + 2) % 4)
    logits[0:ROWS] = (logits[0:ROWS] + product(pl.ds(0, ROWS), lanes((y + 2) % 4))) * inv_temp
    stat[2:3] = jnp.sum(jnp.where(own_j == pos_p, logits[0:ROWS], 0.0), axis=0, keepdims=True)
    statistics(logits[0:ROWS])

    sub_t = sub8(TAKE)
    cs1[...] = jnp.zeros_like(cs1)
    for i in range(3):
        fold(cs1, 5 * i, stat[i : i + 1])
    c1 = copy(cs1, cr1, c_s.at[1], c_r.at[1], sibling)
    begun(c1)
    drain(30)
    c1.wait_recv()
    top, top_o = cs1[0:5], cr1[0:5]
    top_c = jnp.maximum(top, top_o)
    e1s[0:5] = top_c
    e1s[5:10] = cs1[5:10] * jnp.exp(top - top_c) + cr1[5:10] * jnp.exp(top_o - top_c)
    e1s[10:15] = cs1[10:15] + cr1[10:15]
    e1s[15:16] = jnp.zeros((1, 128), f32)
    e1 = (e1s, e1r, e1_s, e1_r, 8, hz, by_hz)
    exchange(*e1)
    drain(60)
    pick[...] = jnp.where(own_j == row_p, 1.0, 0.0).astype(bf16)
    finish(*e1)
    all_top = e1r[0, 0:5]
    for s in range(1, 8):
        all_top = jnp.maximum(all_top, e1r[s, 0:5])
    all_tot = jnp.zeros_like(all_top)
    all_pos = jnp.zeros_like(all_top)
    for s in range(8):
        all_tot = all_tot + e1r[s, 5:10] * jnp.exp(e1r[s, 0:5] - all_top)
        all_pos = all_pos + e1r[s, 10:15]
    lse = unfold(all_top, 0, TAKE) + jnp.log(unfold(all_tot, 0, TAKE))
    loss_part = jnp.sum(lse - unfold(all_pos, 0, TAKE), axis=1, keepdims=True)
    sub_t = sub8(TAKE)

    def own_lanes(vec):
        p1 = vec.astype(bf16).astype(f32)
        p2 = (vec - p1).astype(bf16).astype(f32)
        split = jnp.where(
            sub_t == 0, p1, jnp.where(sub_t == 1, p2, jnp.where(sub_t == 2, vec - p1 - p2, 0.0))
        )
        return jnp.sum(
            lax.dot_general(
                split.astype(bf16), pick[...], (((1,), (1,)), ((), ())),
                preferred_element_type=f32,
            ),
            axis=0, keepdims=True,
        )

    lse_own = own_lanes(lse)
    e2s[...] = jnp.broadcast_to(loss_part, (8, 128))
    fold(e2s, 0, lse_own)
    e2 = (e2s, e2r, e2_s, e2_r, TP, t, by_tensor)
    exchange(*e2)
    wd = (jnp.exp(logits[0:ROWS] - lse) - (own_j == pos_p).astype(f32)) * (1.0 / PAIRS)
    wts[0:ROWS] = wd.astype(bf16)

    def part_d(block):
        return lax.dot_general(
            wts[0:ROWS], qi[:, lanes(block)], (((1,), (0,)), ((), ())),
            preferred_element_type=f32,
        ) * inv_temp

    MID = ROWS // 2
    front, rear = pl.ds(0, MID), pl.ds(MID, MID)
    gc = [
        copy(pd2.at[front], halfs.at[0], g_s.at[0], g_r.at[0], up),
        copy(pd2.at[rear], halfs.at[1], g_s.at[1], g_r.at[1], down),
        copy(pd1.at[rear], r1.at[rear], g_s.at[2], g_r.at[2], up),
        copy(pdm.at[front], r2.at[front], g_s.at[3], g_r.at[3], down),
        copy(pd1.at[front], r1.at[front], g_s.at[4], g_r.at[4], up),
        copy(pdm.at[rear], r2.at[rear], g_s.at[5], g_r.at[5], down),
        copy(xsend, xrecv, g_s.at[6], g_r.at[6], partner),
    ]
    pd2[...] = part_d((y + 2) % 4).astype(bf16)
    begun(gc[0])
    begun(gc[1])
    gd[...] = part_d((y + 1) % 4)
    pd1[rear] = gd[rear].astype(bf16)
    begun(gc[2])
    acc1[...] = gd[front]
    gd[...] = part_d((y + 3) % 4)
    pdm[front] = gd[front].astype(bf16)
    begun(gc[3])
    acc2[...] = gd[rear]

    finish(*e2)
    sums = total(e2r, TP)
    oloss[...] = sums[3:4, 0:1] * (1.0 / PAIRS)
    lse_j = to_rows(unfold(sums, 0, ROWS))[:, 0:1]
    wq = (jnp.exp(logits[ROWS:] - lse) * (1.0 / PAIRS)).astype(bf16).astype(f32)
    wt = (jnp.exp(logits[ROWS:] - lse_j) * (1.0 / PAIRS)).astype(bf16).astype(f32)
    wts[ROWS:] = (wq + wt).astype(bf16)
    wtt[...] = jnp.transpose(wts[...])

    def target(s):
        return (xh + s // 4) % 2 * 4 + (zc + s % 4) % 4

    def cols(f):
        return lanes((y + 1 + f) % 4)

    def bcopy(f, k, n):
        at = rows_at(place(k, 1 - core, t), n)
        return copy(
            partq.at[at, cols(f)], sibr.at[k, pl.ds(0, n), cols(f)],
            b_s.at[f * 8 + k], b_r.at[f * 8 + k], sibling,
        )

    def three(k, core_s):
        return (k // 4) * 2 + core_s == third

    def part_q(f):
        partq[0:TAKE, cols(f)] = (
            jnp.dot(
                wtt[...], emb[0 : 2 * ROWS, cols(f)],
                preferred_element_type=f32,
            ) * inv_temp
        ).astype(bf16)

        @pl.loop(0, 8)
        def _(k):
            sized(three(k, 1 - core), lambda n: bcopy(f, k, n).start())

        @sent.append
        def _():
            @pl.loop(0, 8)
            def _(k):
                sized(three(k, 1 - core), lambda n: bcopy(f, k, n).wait_send())

    N3 = 3 * TILE

    def both(f, s):
        k = target(s)
        sized(three(k, core), lambda n: bcopy(f, k, n).wait_recv())
        cs = cols(f)
        return partq[rows_at(place(k, core, t), N3), cs].astype(f32) + sibr[k, :, cs].astype(f32)

    FLOW = ((2, zup), (6, zdown), (5, zup), (3, zdown), (1, zup), (7, zdown), (4, across))

    def ucopy(f, i, n):
        cs = cols(f)
        return copy(
            sendq.at[i, pl.ds(0, n), cs], recvq.at[i, pl.ds(0, n), cs],
            u_s.at[f * 8 + i], u_r.at[f * 8 + i], FLOW[i][1],
        )

    def usend(f, i, value):
        sendq[i, :, cols(f)] = value.astype(bf16)
        far = three(target(FLOW[i][0]), core)
        sized(far, lambda n: ucopy(f, i, n).start())
        sent.append(lambda: sized(far, lambda n: ucopy(f, i, n).wait_send()))

    def uwait(f, i, s):
        sized(three(target(s), core), lambda n: ucopy(f, i, n).wait_recv())
        return recvq[i, :, cols(f)].astype(f32)

    def q_far(f):
        usend(f, 0, both(f, 2))
        usend(f, 1, both(f, 6))
        usend(f, 2, both(f, 5))
        usend(f, 3, both(f, 3))

    def q_near(f):
        usend(f, 4, both(f, 1) + uwait(f, 0, 1))
        usend(f, 5, both(f, 7) + uwait(f, 1, 7))

    def q_across(f):
        usend(f, 6, both(f, 4) + uwait(f, 2, 4) + uwait(f, 5, 4))

    def tcopy(f, far, n):
        to = (y + 1 + f) % 4 + 4 * ((low + far) % 2)
        return copy(
            asend.at[to, pl.ds(0, n)], arecv.at[rows_at(mine, n)],
            t_s.at[f * 2 + far], t_r.at[f * 2 + far], (d, to),
        )

    def trecv(f, far):
        s = (y + 3 - f) % 4 + 4 * ((low + far) % 2)
        at = lambda n: arecv.at[rows_at(begin(d4, s), n)]
        sized(
            d4 == s // 2,
            lambda n: copy(at(n), at(n), t_s.at[0], t_r.at[f * 2 + far], (d, s)).wait_recv(),
        )

    def direct(f, s, n):
        cs = cols(f)
        return copy(
            sendq.at[s - 1, pl.ds(0, n), cs], recvq.at[s - 1, pl.ds(0, n), cs],
            u_s.at[f * 8 + s - 1], u_r.at[f * 8 + s - 1], device(s),
        )

    def q_direct(f):
        for s in (5, 7, 6, 4, 2, 1, 3):
            sendq[s - 1, :, cols(f)] = both(f, s).astype(bf16)
            far = three(target(s), core)
            sized(far, lambda n: direct(f, s, n).start())
            sent.append(
                lambda s=s, far=far: sized(far, lambda n: direct(f, s, n).wait_send())
            )

    def q_own(f):
        if f < 3:
            g = both(f, 0) + uwait(f, 3, 0) + uwait(f, 4, 0) + uwait(f, 6, 0)
        else:
            g = both(f, 0)
            for s in range(1, 8):
                sized(extra, lambda n: direct(f, s, n).wait_recv())
                g = g + recvq[s - 1, :, cols(f)].astype(f32)
        fb = (y + 1 + f) % 4
        asend[fb] = g[:, :FEATS].astype(bf16)
        asend[4 + fb] = g[:, FEATS:].astype(bf16)
        for far in range(2):
            if f < 3 or far == 1:
                sized(extra, lambda n: tcopy(f, far, n).start())
                sent.append(
                    lambda far=far: sized(extra, lambda n: tcopy(f, far, n).wait_send())
                )

    part_q(0)
    part_q(1)
    q_far(0)

    weighed = wts[...].astype(f32) * logits[...]
    cs5[...] = jnp.zeros_like(cs5)
    fold(cs5, 0, jnp.sum(weighed, axis=0, keepdims=True))
    c5 = copy(cs5, cr5, c_s.at[3], c_r.at[3], sibling)
    begun(c5)
    e3s[...] = jnp.zeros_like(e3s)
    fold(e3s, 3, to_lanes(jnp.sum(weighed[0:ROWS], axis=1, keepdims=True))[0:1])
    part_q(2)
    q_far(1)
    c5.wait_recv()
    e5s[...] = cs5[...] + cr5[...]
    e5 = (e5s, e5r, e5_s, e5_r, 8, hz, by_hz)
    exchange(*e5)
    gc[0].wait_recv()
    pd1[front] = (acc1[...] + halfs[0].astype(f32)).astype(bf16)
    begun(gc[4])
    gc[1].wait_recv()
    pdm[rear] = (acc2[...] + halfs[1].astype(f32)).astype(bf16)
    begun(gc[5])
    q_far(2)
    part_q(3)
    q_near(0)
    q_near(1)
    q_near(2)
    q_direct(3)
    gd[...] = part_d(y)
    finish(*e5)
    fold(e3s, 0, own_lanes(unfold(total(e5r, 8), 0, TAKE)))
    e3 = (e3s, e3r, e3_s, e3_r, TP, t, by_tensor)
    exchange(*e3)
    q_across(0)
    for i in range(2, 6):
        gc[i].wait_recv()
    gd[...] = gd[...] + r1[...].astype(f32) + r2[...].astype(f32)
    xsend[...] = jnp.where(low == 0, gd[:, FEATS:], gd[:, :FEATS]).astype(bf16)
    begun(gc[6])
    q_across(1)
    q_own(0)
    q_across(2)
    q_own(1)

    gc[6].wait_recv()
    gd[:, 0:FEATS] = jnp.where(low == 0, gd[:, :FEATS], gd[:, FEATS:]) + xrecv[...].astype(f32)
    q_own(2)
    q_own(3)

    def tlocal(n):
        arecv[rows_at(mine, n)] = asend[t, pl.ds(0, n)]

    sized(extra, tlocal)

    finish(*e3)
    dots = total(e3r, TP)
    col = to_rows(unfold(dots, 3, ROWS))[:, 0:1]
    iv = invd[:, 0:1]
    h = xd[...].astype(f32)
    gx = iv * gd[:, 0:FEATS] - h * gain[...] * (iv * iv * col)
    outd[...] = (gx * gain[...]).astype(bf16)
    outs = [pltpu.make_async_copy(outd, od, io.at[0]), pltpu.make_async_copy(outq, oq, io.at[1])]
    outs[0].start()
    gg = jnp.sum(gx * h, axis=0, keepdims=True)

    for f in range(4):
        for far in range(2):
            if f < 3 or far == 1:
                trecv(f, far)

    col = to_rows(unfold(dots, 0, ROWS))[:, 0:1]
    h = xq[...].astype(f32)
    iv = invq[0:ROWS, 0:1]
    gx = iv * arecv[...].astype(f32) - h * gain[...] * (iv * iv * col)
    gg = gg + jnp.sum(gx * h, axis=0, keepdims=True)
    cs4[...] = jnp.zeros_like(cs4)
    fold(cs4, 0, gg)
    c4 = copy(cs4, cr4, c_s.at[2], c_r.at[2], sibling)
    begun(c4)
    outq[...] = (gx * gain[...]).astype(bf16)
    outs[1].start()
    drain(30)
    c4.wait_recv()
    e4s[...] = cs4[...] + cr4[...]
    e4 = (e4s, e4r, e4_s, e4_r, 8, hz, by_hz)
    exchange(*e4)
    drain(len(sent))
    finish(*e4)
    ogain[...] = unfold(total(e4r, 8), 0, FEATS)
    for c in outs:
        c.wait()

    drain(len(sent))


def results(gq, gdoc, ggain, loss, oq, od, ogain, oloss):
    oq[...] = gq[...]
    od[...] = gdoc[...]
    ogain[...] = ggain[...]
    oloss[...] = loss[...]


def shards(query_states, doc_states, gain, positives):
    vm = pl.BlockSpec(memory_space=pltpu.VMEM)
    hbm = pl.BlockSpec(memory_space=pl.ANY)
    S = pltpu.VMEM
    dma = lambda n: pltpu.SemaphoreType.DMA((n,))
    pair = lambda n: [dma(n), dma(n)]
    scratch = [
        S((ROWS, FEATS), bf16), S((ROWS, FEATS), bf16),
        S((ROWS, FEATS), bf16), S((ROWS, FEATS), bf16), S((1, FULL), f32),
        S((2 * ROWS, FULL), bf16), S((2 * ROWS + TILE, FULL), bf16), S((TAKE, FULL), bf16),
        S((ROWS + TILE, 128), f32), S((ROWS, 128), f32),
        S((2 * ROWS, TAKE), f32), S((8, TAKE), f32), S((2 * ROWS, TAKE), bf16), S((TAKE, 2 * ROWS), bf16),
        S((8, FEATS), f32), S((TP, 8, FEATS), f32),
        S((16, 128), f32), S((16, 128), f32), S((16, 128), f32), S((8, 16, 128), f32),
        S((8, 128), f32), S((TP, 8, 128), f32),
        S((8, 128), f32), S((TP, 8, 128), f32),
        S((8, 128), f32), S((8, 128), f32), S((8, 128), f32), S((8, 8, 128), f32),
        S((DP, 8, 128), f32), S((8, 128), f32),
        S((TAKE + TILE, FULL), bf16), S((8, 3 * TILE, FULL), bf16),
        S((7, 3 * TILE, FULL), bf16), S((7, 3 * TILE, FULL), bf16),
        S((ROWS // 2, WIDE), f32), S((ROWS // 2, WIDE), f32),
        S((ROWS, WIDE), bf16), S((ROWS, WIDE), bf16), S((ROWS, WIDE), bf16),
        S((2, ROWS // 2, WIDE), bf16), S((ROWS, WIDE), bf16), S((ROWS, WIDE), bf16),
        S((ROWS, WIDE), f32), S((ROWS, FEATS), bf16), S((ROWS, FEATS), bf16),
        S((TP, 3 * TILE, FEATS), bf16), S((ROWS, FEATS), bf16), S((ROWS, TAKE), bf16),
        S((8, 128), f32), S((8, 128), f32), S((8, 128), f32), S((8, 8, 128), f32),
        S((ROWS, FEATS), bf16), S((ROWS, FEATS), bf16),
    ]
    sems = (
        pair(2 * NCH) + pair(TP) + pair(8) + pair(TP) + pair(TP) + pair(8) + pair(8)
        + pair(8 * NCH) + pair(64) + [dma(4)] + pair(32) + pair(32) + pair(7) + pair(TP) + pair(8)
        + pair(4) + [dma(2)]
    )
    gq, gdoc, ggain, loss = pl.pallas_call(
        step,
        name="infonce_step",
        out_shape=(
            jax.ShapeDtypeStruct((ROWS, FEATS), bf16),
            jax.ShapeDtypeStruct((ROWS, FEATS), bf16),
            jax.ShapeDtypeStruct((1, FEATS), f32),
            jax.ShapeDtypeStruct((1, 1), f32),
        ),
        in_specs=[hbm, hbm, vm, vm],
        out_specs=(hbm, hbm, vm, vm),
        scratch_shapes=scratch + sems,
        compiler_params=pltpu.CompilerParams(
            collective_id=0, has_side_effects=True, vmem_limit_bytes=56 * 2**20
        ),
        cost_estimate=pl.CostEstimate(
            flops=7_000_000_000, bytes_accessed=3_000_000, transcendentals=1_000_000
        ),
    )(query_states, doc_states, gain[None, :], positives)
    gq, gdoc, ggain, loss = pl.pallas_call(
        results,
        name="results",
        out_shape=(
            jax.ShapeDtypeStruct((ROWS, FEATS), bf16),
            jax.ShapeDtypeStruct((ROWS, FEATS), bf16),
            jax.ShapeDtypeStruct((1, FEATS), f32),
            jax.ShapeDtypeStruct((1, 1), f32),
        ),
        in_specs=[vm] * 4,
        out_specs=(vm,) * 4,
    )(gq, gdoc, ggain, loss)
    return gq, gdoc, ggain[0], loss[0, 0]


def solution(mesh):
    return jax.shard_map(
        shards,
        mesh=mesh,
        in_specs=(P("dp", "tensor"), P("dp", "tensor"), P("tensor"), P("dp")),
        out_specs=(P("dp", "tensor"), P("dp", "tensor"), P("tensor"), P()),
        check_vma=False,
    )
```

```python
import functools

import jax
import jax.numpy as jnp
from jax import lax
from jax.experimental import pallas as pl
from jax.experimental.pallas import tpu as pltpu
from jax.sharding import PartitionSpec as P

eps_len = 1e-06
inv_temp = 100.0
masked = -1e30

MESH = pl.DeviceIdType.MESH
HIGH = lax.Precision.HIGHEST
f32 = jnp.float32
bf16 = jnp.bfloat16

DP = 16
TP = 8
ROWS = 288
FEATS = 448
WIDE = 2 * FEATS
FULL = TP * FEATS
PAIRS = DP * ROWS
TAKE = DP * ROWS // TP
TILE = 16
CHUNK = 32
NCH = ROWS // CHUNK
HALF = CHUNK // 2


def step(
    hq, hd, gain, pos,
    oq, od, ogain, oloss,
    xq, xd, pq, pd, gfull, raw, emb, qi, invq, invd, logits, stat, wts, wtt,
    e0s, e0r, cs1, cr1, e1s, e1r, e2s, e2r, e3s, e3r, cs4, cr4, e4s, e4r, epr, posv,
    partq, sibr, sendq, recvq, acc1, acc2, pd2, pd1, pdm, halfs, r1, r2, gd, xsend, xrecv,
    asend, arecv, pick, cs5, cr5, e5s, e5r, outq, outd,
    x_s, x_r, e0_s, e0_r, e1_s, e1_r, e2_s, e2_r, e3_s, e3_r, e4_s, e4_r, ep_s, ep_r,
    y_s, y_r, a_s, a_r, loc, b_s, b_r, u_s, u_r, g_s, g_r, t_s, t_r, e5_s, e5_r, c_s, c_r, io,
):
    d = lax.axis_index("dp")
    t = lax.axis_index("tensor")
    hz = d // 2
    core = d % 2
    zc = hz % 4
    d4 = (hz // 4) * 2 + core
    low = t // 4
    y = t % 4
    xh = hz // 4
    sources = [pltpu.make_async_copy(hq, xq, io.at[0]), pltpu.make_async_copy(hd, xd, io.at[1])]
    for c in sources:
        c.start()
    third = t // 2
    sibling = (hz * 2 + (1 - core), t)
    partner = (d, (t + 4) % TP)
    up = (d, low * 4 + (y + 1) % 4)
    down = (d, low * 4 + (y + 3) % 4)
    zup = ((xh * 4 + (zc + 1) % 4) * 2 + core, t)
    zdown = ((xh * 4 + (zc + 3) % 4) * 2 + core, t)
    across = ((hz + 4) % 8 * 2 + core, t)

    sent = []

    def drain(count):
        for _ in range(min(count, len(sent))):
            sent.pop(0)()

    def copy(src, dst, ss, rs, dev):
        return pltpu.make_async_remote_copy(
            src_ref=src, dst_ref=dst, send_sem=ss, recv_sem=rs, device_id=dev, device_id_type=MESH
        )

    def lanes(block):
        return pl.ds(pl.multiple_of(block * WIDE, 128), WIDE)

    def rows_at(tile, n):
        return pl.ds(pl.multiple_of(tile * TILE, TILE), n)

    def place(hz_s, core_s, tens):
        q = (hz_s // 4) * 2 + core_s
        e = tens // 2
        return (hz_s % 4) * 9 + 2 * q + jnp.where(q > e, 1, 0)

    def begin(q, tens):
        return 2 * tens + jnp.clip(tens - 2 * q, 0, 2)

    def sized(extra, fn):
        @pl.when(extra)
        def _():
            fn(3 * TILE)

        @pl.when(jnp.logical_not(extra))
        def _():
            fn(2 * TILE)

    barrier = pltpu.get_barrier_semaphore()

    @pl.loop(1, TP)
    def _(k):
        pl.semaphore_signal(barrier, inc=1, device_id=(d, (t + k) % TP), device_id_type=MESH)

    @pl.loop(1, 8)
    def _(k):
        pl.semaphore_signal(
            barrier, inc=1, device_id=((hz + k) % 8 * 2 + core, t), device_id_type=MESH
        )

    pl.semaphore_signal(barrier, inc=1, device_id=sibling, device_id_type=MESH)
    def fold(ref, row, vec):
        for k in range(-(-vec.shape[1] // 128)):
            part = vec[:, 128 * k : 128 * (k + 1)]
            ref[row + k : row + k + 1, 0 : part.shape[1]] = part

    def unfold(tile, row, size):
        return jnp.concatenate(
            [
                tile[row + k : row + k + 1, 0 : min(128, size - 128 * k)]
                for k in range(-(-size // 128))
            ],
            axis=1,
        )

    def to_lanes(col):
        return jnp.transpose(jnp.broadcast_to(col, (ROWS, 128)))[:8]

    def to_rows(vec):
        return jnp.transpose(jnp.broadcast_to(vec, (128, ROWS)))

    sub8 = lambda n: lax.broadcasted_iota(jnp.int32, (8, n), 0)

    posv[...] = jnp.zeros_like(posv)
    for seg in range(3):
        at = slice(128 * seg, min(128 * (seg + 1), ROWS))
        width = at.stop - at.start
        posv[seg : seg + 1, 0:width] = (pos[at] // 128).astype(f32)[None, :]
        posv[3 + seg : 4 + seg, 0:width] = (pos[at] % 128).astype(f32)[None, :]
    pl.semaphore_wait(barrier, TP + 7)

    def xcopy(i):
        src, dst = (hq, pq) if i < NCH else (hd, pd)
        part = pl.ds((i % NCH) * CHUNK, CHUNK)
        return copy(src.at[part], dst.at[part], x_s.at[i], x_r.at[i], partner)

    def begun(c):
        c.start()
        sent.append(c.wait_send)

    def exchange(src, recv, ss, rs, size, me, dev):
        @pl.loop(1, size)
        def _(k):
            copy(src, recv.at[me], ss.at[k], rs.at[me], dev((me + k) % size)).start()

        @sent.append
        def _():
            @pl.loop(1, size)
            def _(k):
                copy(src, recv.at[me], ss.at[k], rs.at[me], dev((me + k) % size)).wait_send()

    def finish(src, recv, ss, rs, size, me, dev):
        recv[me] = src[...]

        @pl.loop(1, size)
        def _(k):
            s = (me + k) % size
            copy(src, recv.at[s], ss.at[k], rs.at[s], dev(s)).wait_recv()

    by_tensor = lambda s: (d, s)
    by_hz = lambda s: (s * 2 + core, t)

    def total(recv, size):
        acc = recv[0]
        for s in range(1, size):
            acc = acc + recv[s]
        return acc

    e0 = (e0s, e0r, e0_s, e0_r, TP, t, by_tensor)
    begun(xcopy(0))
    for c in sources:
        c.wait()
    nq = xq[...].astype(f32) * gain[...]
    nd = xd[...].astype(f32) * gain[...]
    lq = to_lanes(jnp.sum(nq * nq, axis=1, keepdims=True))
    ld = to_lanes(jnp.sum(nd * nd, axis=1, keepdims=True))
    e0s[...] = jnp.broadcast_to(gain[...], (8, FEATS))
    e0s[0:1, 0:ROWS] = lq[0:1]
    e0s[1:2, 0:ROWS] = ld[0:1]
    exchange(*e0)
    for i in range(1, 2 * NCH):
        begun(xcopy(i))

    mine = begin(d4, t)
    here = place(hz, core, t)
    extra = d4 == third

    def pack(a, k):
        own, part, base = (xq, pq, ROWS) if a == 0 else (xd, pd, 0)
        xcopy(a * NCH + k).wait_recv()
        rs = pl.ds(k * CHUNK, CHUNK)
        eo = own[rs].astype(f32)
        ep = part[rs].astype(f32)
        left = jnp.where(low == 0, eo, ep)
        right = jnp.where(low == 0, ep, eo)
        raw[pl.ds(base + k * CHUNK, CHUNK), lanes(y)] = jnp.concatenate(
            [left, right], axis=1
        ).astype(bf16)

    def normalise(a, k, block):
        inverse, base = (invq, ROWS) if a == 0 else (invd, 0)
        for part in range(2):
            rs = k * CHUNK + part * HALF
            scale = inverse[pl.ds(rs, HALF), 0:1]
            at = pl.ds(base + rs, HALF)
            cs = lanes(block)
            emb[at, cs] = (raw[at, cs].astype(f32) * gfull[:, cs] * scale).astype(bf16)

    def ycopy(a, k, kind):
        base = (ROWS if a == 0 else 0) + k * CHUNK
        i = (a * NCH + k) * 4 + kind
        if kind < 2:
            at, dev, block = pl.ds(base, CHUNK), (up, down)[kind], y
        elif kind == 2:
            at, dev, block = pl.ds(base, HALF), up, (y + 3) % 4
        else:
            at, dev, block = pl.ds(base + HALF, HALF), down, (y + 1) % 4
        ref = raw.at[at, lanes(block)]
        return copy(ref, ref, y_s.at[i], y_r.at[i], dev)

    def yrecv(a, k, kind):
        base = (ROWS if a == 0 else 0) + k * CHUNK
        i = (a * NCH + k) * 4 + kind
        at = pl.ds(base, CHUNK) if kind < 2 else pl.ds(base + (kind - 2) * HALF, HALF)
        block = ((y + 3) % 4, (y + 1) % 4, (y + 2) % 4, (y + 2) % 4)[kind]
        ref = raw.at[at, lanes(block)]
        copy(ref, ref, y_s.at[i], y_r.at[i], up).wait_recv()

    def source(s):
        return (xh + s // 4) % 2 * 4 + (zc + 4 - s % 4) % 4

    def gives(s, core_s):
        return (xh + s // 4) % 2 * 2 + core_s == third

    def device(s):
        return ((xh + s // 4) % 2 * 8 + (zc + s % 4) % 4 * 2 + core, t)

    def spot(i, s, core_s, n):
        block = (y + (0, 3, 1, 2)[i]) % 4
        return qi.at[rows_at(place(source(s), core_s, t), n), lanes(block)]

    def own_rows(i, n):
        block = (y + (0, 3, 1, 2)[i]) % 4
        return emb.at[pl.ds(pl.multiple_of(ROWS + mine * TILE, TILE), n), lanes(block)]

    def give_own(i, slot, dev):
        def c(n):
            return copy(
                own_rows(i, n), spot(i, 0, core, n), a_s.at[i * 16 + slot], a_r.at[i * 16 + slot], dev
            )

        sized(extra, lambda n: c(n).start())
        sent.append(lambda: sized(extra, lambda n: c(n).wait_send()))

    def pass_on(i, s, slot, dev):
        def c(n):
            ref = spot(i, s, core, n)
            return copy(ref, ref, a_s.at[i * 16 + slot], a_r.at[i * 16 + slot], dev)

        sized(gives(s, core), lambda n: c(n).start())
        sent.append(lambda: sized(gives(s, core), lambda n: c(n).wait_send()))

    def agot(i, s):
        def c(n):
            ref = spot(i, s, core, n)
            copy(ref, ref, a_s.at[i * 16 + s], a_r.at[i * 16 + s], sibling).wait_recv()

        sized(gives(s, core), c)

    def alocal(i, n):
        return pltpu.make_async_copy(own_rows(i, n), spot(i, 0, core, n), loc.at[i])

    def astart(i):
        for s in (1, 3, 2, 4) if i < 3 else (4, 1, 3, 2, 5, 7, 6):
            give_own(i, s, device(s))
        give_own(i, 8, sibling)
        sized(extra, lambda n: alocal(i, n).start())

    def amid(i):
        agot(i, 4)
        if i < 3:
            for s in (1, 3, 2):
                pass_on(i, 4, 4 + s, device(s))
        pass_on(i, 4, 12, sibling)
        for s in (1, 3, 2):
            agot(i, s)
            pass_on(i, s, 8 + s, sibling)

    def alast(i):
        for s in (5, 7, 6):
            agot(i, s)
            pass_on(i, s, 8 + s, sibling)

    def afinish(i):
        sized(extra, lambda n: alocal(i, n).wait())

        @pl.loop(0, 8)
        def _(s):
            def c(n):
                ref = spot(i, s, 1 - core, n)
                copy(ref, ref, a_s.at[i * 16], a_r.at[i * 16 + 8 + s], sibling).wait_recv()

            sized(gives(s, 1 - core), c)

    for k in range(NCH):
        pack(0, k)
        begun(ycopy(0, k, 0))
        begun(ycopy(0, k, 1))
    finish(*e0)
    inv = lax.rsqrt(total(e0r, TP)[:, 0:ROWS] + eps_len)
    invq[0:ROWS] = to_rows(inv[0:1])
    invd[...] = to_rows(inv[1:2])
    for b in range(4):
        gfull[:, b * WIDE : (b + 1) * WIDE] = jnp.concatenate(
            [e0r[b, 2:3], e0r[4 + b, 2:3]], axis=1
        )
    for k in range(NCH):
        normalise(0, k, y)
    astart(0)
    ep = (posv, epr, ep_s, ep_r, 8, hz, by_hz)
    exchange(*ep)
    for k in range(NCH):
        yrecv(0, k, 0)
        begun(ycopy(0, k, 2))
        yrecv(0, k, 1)
        begun(ycopy(0, k, 3))
    for k in range(NCH):
        pack(1, k)
        begun(ycopy(1, k, 0))
        begun(ycopy(1, k, 1))
    for k in range(NCH):
        normalise(0, k, (y + 3) % 4)
        normalise(0, k, (y + 1) % 4)
    astart(1)
    astart(2)
    amid(0)
    for k in range(NCH):
        yrecv(0, k, 2)
        yrecv(0, k, 3)
        normalise(0, k, (y + 2) % 4)
    astart(3)
    for k in range(NCH):
        normalise(1, k, y)
    alast(0)
    amid(1)
    amid(2)

    def docs_on(k):
        yrecv(1, k, 0)
        begun(ycopy(1, k, 2))
        yrecv(1, k, 1)
        begun(ycopy(1, k, 3))

    third_k = NCH // 3
    for k in range(third_k):
        docs_on(k)
    alast(1)
    for k in range(third_k, 2 * third_k):
        docs_on(k)
    alast(2)
    for k in range(2 * third_k, NCH):
        docs_on(k)
    for k in range(NCH):
        normalise(1, k, (y + 3) % 4)
        normalise(1, k, (y + 1) % 4)
    amid(3)
    alast(3)
    for i in range(4):
        afinish(i)

    lane_p = lax.broadcasted_iota(jnp.int32, (1, TAKE), 1)
    tile_p = lane_p // TILE
    w_p = tile_p % 9
    q_p = jnp.where(
        w_p < 2 * third, w_p // 2, jnp.where(w_p <= 2 * third + 2, third, (w_p - 1) // 2)
    )
    off_p = w_p - 2 * q_p - jnp.where(q_p > third, 1, 0)
    dev_p = (q_p // 2) * 8 + (tile_p // 9) * 2 + q_p % 2
    row_p = dev_p * ROWS + (begin(q_p, t) + off_p) * TILE + lane_p % TILE
    finish(*ep)
    epc = copy(epr.at[pl.ds(0, 8)], epr.at[pl.ds(8, 8)], c_s.at[0], c_r.at[0], sibling)
    begun(epc)

    stat[0:1] = jnp.full((1, TAKE), masked, f32)
    stat[1:8] = jnp.zeros((7, TAKE), f32)

    def product(rows, cs):
        return lax.dot_general(
            emb[rows, cs], qi[:, cs], (((1,), (1,)), ((), ())), preferred_element_type=f32
        )

    def statistics(s):
        old = stat[0:1]
        new = jnp.maximum(old, jnp.max(s, axis=0, keepdims=True))
        stat[0:1] = new
        stat[1:2] = stat[1:2] * jnp.exp(old - new) + jnp.sum(
            jnp.exp(s - new), axis=0, keepdims=True
        )

    own_j = d * ROWS + lax.broadcasted_iota(jnp.int32, (ROWS, TAKE), 0)
    logits[ROWS:] = product(pl.ds(ROWS, ROWS), slice(None))
    logits[ROWS:] = jnp.where(own_j == row_p, masked, logits[ROWS:] * inv_temp)
    statistics(logits[ROWS:])
    logits[0:ROWS] = product(pl.ds(0, ROWS), lanes(y))
    for b in (1, 3):
        logits[0:ROWS] = logits[0:ROWS] + product(pl.ds(0, ROWS), lanes((y + b) % 4))

    epc.wait_recv()
    local_p = (begin(q_p, t) + off_p) * TILE + lane_p % TILE
    lane_of = lax.broadcasted_iota(jnp.int32, (128, TAKE), 0)
    spread = jnp.where(lane_of == local_p % 128, 1.0, 0.0).astype(bf16)
    found = jnp.dot(
        epr[...].reshape(DP * 8, 128).astype(bf16), spread, preferred_element_type=f32
    )
    slot_p = jnp.where(dev_p % 2 == core, dev_p // 2, 8 + dev_p // 2) * 8 + local_p // 128
    high = jnp.sum(jnp.where(lane_of == slot_p, found, 0.0), axis=0, keepdims=True)
    rest = jnp.sum(jnp.where(lane_of == slot_p + 3, found, 0.0), axis=0, keepdims=True)
    pos_p = (high * 128.0 + rest).astype(jnp.int32)

    for k in range(NCH):
        yrecv(1, k, 2)
        yrecv(1, k, 3)
        normalise(1, k, (y + 2) % 4)
    logits[0:ROWS] = (logits[0:ROWS] + product(pl.ds(0, ROWS), lanes((y + 2) % 4))) * inv_temp
    stat[2:3] = jnp.sum(jnp.where(own_j == pos_p, logits[0:ROWS], 0.0), axis=0, keepdims=True)
    statistics(logits[0:ROWS])

    sub_t = sub8(TAKE)
    cs1[...] = jnp.zeros_like(cs1)
    for i in range(3):
        fold(cs1, 5 * i, stat[i : i + 1])
    c1 = copy(cs1, cr1, c_s.at[1], c_r.at[1], sibling)
    begun(c1)
    drain(50)
    c1.wait_recv()
    top, top_o = cs1[0:5], cr1[0:5]
    top_c = jnp.maximum(top, top_o)
    e1s[0:5] = top_c
    e1s[5:10] = cs1[5:10] * jnp.exp(top - top_c) + cr1[5:10] * jnp.exp(top_o - top_c)
    e1s[10:15] = cs1[10:15] + cr1[10:15]
    e1s[15:16] = jnp.zeros((1, 128), f32)
    e1 = (e1s, e1r, e1_s, e1_r, 8, hz, by_hz)
    exchange(*e1)
    drain(110)
    pick[...] = jnp.where(own_j == row_p, 1.0, 0.0).astype(bf16)
    finish(*e1)
    all_top = e1r[0, 0:5]
    for s in range(1, 8):
        all_top = jnp.maximum(all_top, e1r[s, 0:5])
    all_tot = jnp.zeros_like(all_top)
    all_pos = jnp.zeros_like(all_top)
    for s in range(8):
        all_tot = all_tot + e1r[s, 5:10] * jnp.exp(e1r[s, 0:5] - all_top)
        all_pos = all_pos + e1r[s, 10:15]
    lse = unfold(all_top, 0, TAKE) + jnp.log(unfold(all_tot, 0, TAKE))
    loss_part = jnp.sum(lse - unfold(all_pos, 0, TAKE), axis=1, keepdims=True)
    sub_t = sub8(TAKE)

    def own_lanes(vec):
        p1 = vec.astype(bf16).astype(f32)
        p2 = (vec - p1).astype(bf16).astype(f32)
        split = jnp.where(
            sub_t == 0, p1, jnp.where(sub_t == 1, p2, jnp.where(sub_t == 2, vec - p1 - p2, 0.0))
        )
        return jnp.sum(
            lax.dot_general(
                split.astype(bf16), pick[...], (((1,), (1,)), ((), ())),
                preferred_element_type=f32,
            ),
            axis=0, keepdims=True,
        )

    lse_own = own_lanes(lse)
    e2s[...] = jnp.broadcast_to(loss_part, (8, 128))
    fold(e2s, 0, lse_own)
    e2 = (e2s, e2r, e2_s, e2_r, TP, t, by_tensor)
    exchange(*e2)
    wd = (jnp.exp(logits[0:ROWS] - lse) - (own_j == pos_p).astype(f32)) * (1.0 / PAIRS)
    wts[0:ROWS] = wd.astype(bf16)

    def part_d(block):
        return lax.dot_general(
            wts[0:ROWS], qi[:, lanes(block)], (((1,), (0,)), ((), ())),
            preferred_element_type=f32,
        ) * inv_temp

    MID = ROWS // 2
    front, rear = pl.ds(0, MID), pl.ds(MID, MID)
    gc = [
        copy(pd2.at[front], halfs.at[0], g_s.at[0], g_r.at[0], up),
        copy(pd2.at[rear], halfs.at[1], g_s.at[1], g_r.at[1], down),
        copy(pd1.at[rear], r1.at[rear], g_s.at[2], g_r.at[2], up),
        copy(pdm.at[front], r2.at[front], g_s.at[3], g_r.at[3], down),
        copy(pd1.at[front], r1.at[front], g_s.at[4], g_r.at[4], up),
        copy(pdm.at[rear], r2.at[rear], g_s.at[5], g_r.at[5], down),
        copy(xsend, xrecv, g_s.at[6], g_r.at[6], partner),
    ]
    pd2[...] = part_d((y + 2) % 4).astype(bf16)
    begun(gc[0])
    begun(gc[1])
    gd[...] = part_d((y + 1) % 4)
    pd1[rear] = gd[rear].astype(bf16)
    begun(gc[2])
    acc1[...] = gd[front]
    gd[...] = part_d((y + 3) % 4)
    pdm[front] = gd[front].astype(bf16)
    begun(gc[3])
    acc2[...] = gd[rear]

    finish(*e2)
    sums = total(e2r, TP)
    oloss[...] = sums[3:4, 0:1] * (1.0 / PAIRS)
    lse_j = to_rows(unfold(sums, 0, ROWS))[:, 0:1]
    wq = (jnp.exp(logits[ROWS:] - lse) * (1.0 / PAIRS)).astype(bf16).astype(f32)
    wt = (jnp.exp(logits[ROWS:] - lse_j) * (1.0 / PAIRS)).astype(bf16).astype(f32)
    wts[ROWS:] = (wq + wt).astype(bf16)
    wtt[...] = jnp.transpose(wts[...])

    def target(s):
        return (xh + s // 4) % 2 * 4 + (zc + s % 4) % 4

    def cols(f):
        return lanes((y + 1 + f) % 4)

    def bcopy(f, k, n):
        at = rows_at(place(k, 1 - core, t), n)
        return copy(
            partq.at[at, cols(f)], sibr.at[k, pl.ds(0, n), cols(f)],
            b_s.at[f * 8 + k], b_r.at[f * 8 + k], sibling,
        )

    def three(k, core_s):
        return (k // 4) * 2 + core_s == third

    def part_q(f):
        partq[0:TAKE, cols(f)] = (
            jnp.dot(
                wtt[...], emb[0 : 2 * ROWS, cols(f)],
                preferred_element_type=f32,
            ) * inv_temp
        ).astype(bf16)

        @pl.loop(0, 8)
        def _(k):
            sized(three(k, 1 - core), lambda n: bcopy(f, k, n).start())

        @sent.append
        def _():
            @pl.loop(0, 8)
            def _(k):
                sized(three(k, 1 - core), lambda n: bcopy(f, k, n).wait_send())

    N3 = 3 * TILE

    def both(f, s):
        k = target(s)
        sized(three(k, core), lambda n: bcopy(f, k, n).wait_recv())
        cs = cols(f)
        return partq[rows_at(place(k, core, t), N3), cs].astype(f32) + sibr[k, :, cs].astype(f32)

    FLOW = ((2, zup), (6, zdown), (5, zup), (3, zdown), (1, zup), (7, zdown), (4, across))

    def ucopy(f, i, n):
        cs = cols(f)
        return copy(
            sendq.at[i, pl.ds(0, n), cs], recvq.at[i, pl.ds(0, n), cs],
            u_s.at[f * 8 + i], u_r.at[f * 8 + i], FLOW[i][1],
        )

    def usend(f, i, value):
        sendq[i, :, cols(f)] = value.astype(bf16)
        far = three(target(FLOW[i][0]), core)
        sized(far, lambda n: ucopy(f, i, n).start())
        sent.append(lambda: sized(far, lambda n: ucopy(f, i, n).wait_send()))

    def uwait(f, i, s):
        sized(three(target(s), core), lambda n: ucopy(f, i, n).wait_recv())
        return recvq[i, :, cols(f)].astype(f32)

    def q_far(f):
        usend(f, 0, both(f, 2))
        usend(f, 1, both(f, 6))
        usend(f, 2, both(f, 5))
        usend(f, 3, both(f, 3))

    def q_near(f):
        usend(f, 4, both(f, 1) + uwait(f, 0, 1))
        usend(f, 5, both(f, 7) + uwait(f, 1, 7))

    def q_across(f):
        usend(f, 6, both(f, 4) + uwait(f, 2, 4) + uwait(f, 5, 4))

    def tcopy(f, far, n):
        to = (y + 1 + f) % 4 + 4 * ((low + far) % 2)
        return copy(
            asend.at[to, pl.ds(0, n)], arecv.at[rows_at(mine, n)],
            t_s.at[f * 2 + far], t_r.at[f * 2 + far], (d, to),
        )

    def trecv(f, far):
        s = (y + 3 - f) % 4 + 4 * ((low + far) % 2)
        at = lambda n: arecv.at[rows_at(begin(d4, s), n)]
        sized(
            d4 == s // 2,
            lambda n: copy(at(n), at(n), t_s.at[0], t_r.at[f * 2 + far], (d, s)).wait_recv(),
        )

    def direct(f, s, n):
        cs = cols(f)
        return copy(
            sendq.at[s - 1, pl.ds(0, n), cs], recvq.at[s - 1, pl.ds(0, n), cs],
            u_s.at[f * 8 + s - 1], u_r.at[f * 8 + s - 1], device(s),
        )

    def q_direct(f):
        for s in (5, 7, 6, 4, 2, 1, 3):
            sendq[s - 1, :, cols(f)] = both(f, s).astype(bf16)
            far = three(target(s), core)
            sized(far, lambda n: direct(f, s, n).start())
            sent.append(
                lambda s=s, far=far: sized(far, lambda n: direct(f, s, n).wait_send())
            )

    def q_own(f):
        if f < 3:
            g = both(f, 0) + uwait(f, 3, 0) + uwait(f, 4, 0) + uwait(f, 6, 0)
        else:
            g = both(f, 0)
            for s in range(1, 8):
                sized(extra, lambda n: direct(f, s, n).wait_recv())
                g = g + recvq[s - 1, :, cols(f)].astype(f32)
        fb = (y + 1 + f) % 4
        asend[fb] = g[:, :FEATS].astype(bf16)
        asend[4 + fb] = g[:, FEATS:].astype(bf16)
        for far in range(2):
            if f < 3 or far == 1:
                sized(extra, lambda n: tcopy(f, far, n).start())
                sent.append(
                    lambda far=far: sized(extra, lambda n: tcopy(f, far, n).wait_send())
                )

    part_q(0)
    part_q(1)
    q_far(0)

    weighed = wts[...].astype(f32) * logits[...]
    cs5[...] = jnp.zeros_like(cs5)
    fold(cs5, 0, jnp.sum(weighed, axis=0, keepdims=True))
    c5 = copy(cs5, cr5, c_s.at[3], c_r.at[3], sibling)
    begun(c5)
    e3s[...] = jnp.zeros_like(e3s)
    fold(e3s, 3, to_lanes(jnp.sum(weighed[0:ROWS], axis=1, keepdims=True))[0:1])
    part_q(2)
    q_far(1)
    c5.wait_recv()
    e5s[...] = cs5[...] + cr5[...]
    e5 = (e5s, e5r, e5_s, e5_r, 8, hz, by_hz)
    exchange(*e5)
    gc[0].wait_recv()
    pd1[front] = (acc1[...] + halfs[0].astype(f32)).astype(bf16)
    begun(gc[4])
    gc[1].wait_recv()
    pdm[rear] = (acc2[...] + halfs[1].astype(f32)).astype(bf16)
    begun(gc[5])
    q_far(2)
    part_q(3)
    q_near(0)
    q_near(1)
    q_near(2)
    q_direct(3)
    gd[...] = part_d(y)
    finish(*e5)
    fold(e3s, 0, own_lanes(unfold(total(e5r, 8), 0, TAKE)))
    e3 = (e3s, e3r, e3_s, e3_r, TP, t, by_tensor)
    exchange(*e3)
    q_across(0)
    for i in range(2, 6):
        gc[i].wait_recv()
    gd[...] = gd[...] + r1[...].astype(f32) + r2[...].astype(f32)
    xsend[...] = jnp.where(low == 0, gd[:, FEATS:], gd[:, :FEATS]).astype(bf16)
    begun(gc[6])
    q_across(1)
    q_own(0)
    q_across(2)
    q_own(1)

    gc[6].wait_recv()
    gd[:, 0:FEATS] = jnp.where(low == 0, gd[:, :FEATS], gd[:, FEATS:]) + xrecv[...].astype(f32)
    q_own(2)
    q_own(3)

    def tlocal(n):
        arecv[rows_at(mine, n)] = asend[t, pl.ds(0, n)]

    sized(extra, tlocal)

    finish(*e3)
    dots = total(e3r, TP)
    col = to_rows(unfold(dots, 3, ROWS))[:, 0:1]
    iv = invd[:, 0:1]
    h = xd[...].astype(f32)
    gx = iv * gd[:, 0:FEATS] - h * gain[...] * (iv * iv * col)
    outd[...] = (gx * gain[...]).astype(bf16)
    outs = [pltpu.make_async_copy(outd, od, io.at[0]), pltpu.make_async_copy(outq, oq, io.at[1])]
    outs[0].start()
    gg = jnp.sum(gx * h, axis=0, keepdims=True)

    for f in range(4):
        for far in range(2):
            if f < 3 or far == 1:
                trecv(f, far)

    col = to_rows(unfold(dots, 0, ROWS))[:, 0:1]
    h = xq[...].astype(f32)
    iv = invq[0:ROWS, 0:1]
    gx = iv * arecv[...].astype(f32) - h * gain[...] * (iv * iv * col)
    gg = gg + jnp.sum(gx * h, axis=0, keepdims=True)
    cs4[...] = jnp.zeros_like(cs4)
    fold(cs4, 0, gg)
    c4 = copy(cs4, cr4, c_s.at[2], c_r.at[2], sibling)
    begun(c4)
    outq[...] = (gx * gain[...]).astype(bf16)
    outs[1].start()
    drain(30)
    c4.wait_recv()
    e4s[...] = cs4[...] + cr4[...]
    e4 = (e4s, e4r, e4_s, e4_r, 8, hz, by_hz)
    exchange(*e4)
    drain(len(sent))
    finish(*e4)
    ogain[...] = unfold(total(e4r, 8), 0, FEATS)
    for c in outs:
        c.wait()

    drain(len(sent))


def results(gq, gdoc, ggain, loss, oq, od, ogain, oloss):
    oq[...] = gq[...]
    od[...] = gdoc[...]
    ogain[...] = ggain[...]
    oloss[...] = loss[...]


def shards(query_states, doc_states, gain, positives):
    vm = pl.BlockSpec(memory_space=pltpu.VMEM)
    hbm = pl.BlockSpec(memory_space=pl.ANY)
    S = pltpu.VMEM
    dma = lambda n: pltpu.SemaphoreType.DMA((n,))
    pair = lambda n: [dma(n), dma(n)]
    scratch = [
        S((ROWS, FEATS), bf16), S((ROWS, FEATS), bf16),
        S((ROWS, FEATS), bf16), S((ROWS, FEATS), bf16), S((1, FULL), f32),
        S((2 * ROWS, FULL), bf16), S((2 * ROWS + TILE, FULL), bf16), S((TAKE, FULL), bf16),
        S((ROWS + TILE, 128), f32), S((ROWS, 128), f32),
        S((2 * ROWS, TAKE), f32), S((8, TAKE), f32), S((2 * ROWS, TAKE), bf16), S((TAKE, 2 * ROWS), bf16),
        S((8, FEATS), f32), S((TP, 8, FEATS), f32),
        S((16, 128), f32), S((16, 128), f32), S((16, 128), f32), S((8, 16, 128), f32),
        S((8, 128), f32), S((TP, 8, 128), f32),
        S((8, 128), f32), S((TP, 8, 128), f32),
        S((8, 128), f32), S((8, 128), f32), S((8, 128), f32), S((8, 8, 128), f32),
        S((DP, 8, 128), f32), S((8, 128), f32),
        S((TAKE + TILE, FULL), bf16), S((8, 3 * TILE, FULL), bf16),
        S((7, 3 * TILE, FULL), bf16), S((7, 3 * TILE, FULL), bf16),
        S((ROWS // 2, WIDE), f32), S((ROWS // 2, WIDE), f32),
        S((ROWS, WIDE), bf16), S((ROWS, WIDE), bf16), S((ROWS, WIDE), bf16),
        S((2, ROWS // 2, WIDE), bf16), S((ROWS, WIDE), bf16), S((ROWS, WIDE), bf16),
        S((ROWS, WIDE), f32), S((ROWS, FEATS), bf16), S((ROWS, FEATS), bf16),
        S((TP, 3 * TILE, FEATS), bf16), S((ROWS, FEATS), bf16), S((ROWS, TAKE), bf16),
        S((8, 128), f32), S((8, 128), f32), S((8, 128), f32), S((8, 8, 128), f32),
        S((ROWS, FEATS), bf16), S((ROWS, FEATS), bf16),
    ]
    sems = (
        pair(2 * NCH) + pair(TP) + pair(8) + pair(TP) + pair(TP) + pair(8) + pair(8)
        + pair(8 * NCH) + pair(64) + [dma(4)] + pair(32) + pair(32) + pair(7) + pair(TP) + pair(8)
        + pair(4) + [dma(2)]
    )
    gq, gdoc, ggain, loss = pl.pallas_call(
        step,
        name="infonce_step",
        out_shape=(
            jax.ShapeDtypeStruct((ROWS, FEATS), bf16),
            jax.ShapeDtypeStruct((ROWS, FEATS), bf16),
            jax.ShapeDtypeStruct((1, FEATS), f32),
            jax.ShapeDtypeStruct((1, 1), f32),
        ),
        in_specs=[hbm, hbm, vm, vm],
        out_specs=(hbm, hbm, vm, vm),
        scratch_shapes=scratch + sems,
        compiler_params=pltpu.CompilerParams(
            collective_id=0, has_side_effects=True, vmem_limit_bytes=56 * 2**20
        ),
        cost_estimate=pl.CostEstimate(
            flops=7_000_000_000, bytes_accessed=3_000_000, transcendentals=1_000_000
        ),
    )(query_states, doc_states, gain[None, :], positives)
    gq, gdoc, ggain, loss = pl.pallas_call(
        results,
        name="results",
        out_shape=(
            jax.ShapeDtypeStruct((ROWS, FEATS), bf16),
            jax.ShapeDtypeStruct((ROWS, FEATS), bf16),
            jax.ShapeDtypeStruct((1, FEATS), f32),
            jax.ShapeDtypeStruct((1, 1), f32),
        ),
        in_specs=[vm] * 4,
        out_specs=(vm,) * 4,
    )(gq, gdoc, ggain, loss)
    return gq, gdoc, ggain[0], loss[0, 0]


def solution(mesh):
    return jax.shard_map(
        shards,
        mesh=mesh,
        in_specs=(P("dp", "tensor"), P("dp", "tensor"), P("tensor"), P("dp")),
        out_specs=(P("dp", "tensor"), P("dp", "tensor"), P("tensor"), P()),
        check_vma=False,
    )
```
